32 devices in a mesh: seq: 4 (over z), fsdp: 8 (over y, x, core).
Axes of the slice: x: 2, y: 2, z: 4, core: 2. Of those that a mesh axis runs over, the one named last changes fastest.
Arguments:
- tokens: bfloat16 [8, 2048, 1536], P('fsdp', 'seq'), may hold values from -6 to 6
- pre_gain: bfloat16 [1536], P(('seq', 'fsdp')), may hold values from 0.5 to 1.5
- in_weight: bfloat16 [1536, 6448], P(('seq', 'fsdp')), may hold values from -0.15625 to 0.15625
- conv_weight: bfloat16 [4, 3328], P(None, ('seq', 'fsdp')), may hold values from -3 to 3
- conv_bias: bfloat16 [3328], P(('seq', 'fsdp')), may hold values from -1.75 to 1.75
- step_bias: float32 [48], replicated, may hold values from -7 to -2.3
- decay_log: float32 [48], replicated, may hold values from -1 to 1
- skip_gain: float32 [48], replicated, may hold values from 0.2 to 1
- norm_gain: bfloat16 [3072], P(('seq', 'fsdp')), may hold values from 0.5 to 1.5
- out_weight: bfloat16 [3072, 1536], P(('seq', 'fsdp')), may hold values from -0.109375 to 0.109375
- cotangent: bfloat16 [8, 2048, 1536], P('fsdp', 'seq'), may hold values from -6 to 6
Outputs:
- mixed: bfloat16 [8, 2048, 1536], P('fsdp', 'seq')
- grad_tokens: float32 [8, 2048, 1536], P('fsdp', 'seq')
- grad_pre_gain: float32 [1536], P(('seq', 'fsdp'))
- grad_in_weight: float32 [1536, 6448], P(('seq', 'fsdp'))
- grad_conv_weight: float32 [4, 3328], P(None, ('seq', 'fsdp'))
- grad_conv_bias: float32 [3328], P(('seq', 'fsdp'))
- grad_step_bias: float32 [48], replicated
- grad_decay_log: float32 [48], replicated
- grad_skip_gain: float32 [48], replicated
- grad_norm_gain: float32 [3072], P(('seq', 'fsdp'))
- grad_out_weight: float32 [3072, 1536], P(('seq', 'fsdp'))
The draws below stay inside these ranges and needn't reach their ends.
All inputs are finite; a program needn't handle non-finite values.
Results may differ from the reference program's by a relative error of at most 0.0067.
Values may be sent and summed in bfloat16 or wider, within the bound.
A program may use at most 320 MiB of HBM per device.

```python
import jax
import jax.numpy as jnp
from jax import lax

D = 1536
INNER = 3072
HEADS = 48
HEAD_DIM = 64
STATE = 128
CONV = 4
BLOCK_LEN = 256
CHANNELS = 3328
PROJ = 6448
SEQS = 8
LENGTH = 2048


def steps_of(stream_key, extent, pieces, smallest, high):
    level, own = 1.0, jax.random.fold_in(stream_key, 6)
    for axis_at, blocks in pieces:
        steps = jnp.exp(jax.random.uniform(jax.random.fold_in(own, axis_at), (blocks,), jnp.float32, smallest / len(pieces), high / len(pieces)))
        level = level * jnp.repeat(steps, extent[axis_at] // blocks).reshape([-1 if axis == axis_at else 1 for axis in range(len(extent))])
    return level


def centred(rng, shape, width, limit, split=(), held_as=jnp.bfloat16):
    factor_of = steps_of(rng, shape, split, -0.22, 0.18) if split else 1.0
    values = jax.random.normal(rng, shape, jnp.float32) * width * factor_of
    return jnp.minimum(jnp.maximum(values, -limit), limit).astype(held_as)


def setup_inputs(seed: int = 0) -> dict:
    arg_keys = jax.random.split(jax.random.key(seed), 12)
    return {
        "tokens": centred(arg_keys[0], (SEQS, LENGTH, D), 1.0, 6.0, ((0, 8), (1, 4))),
        "pre_gain": jnp.clip(1.0 + 0.1 * jax.random.normal(arg_keys[1], (D,), jnp.float32), 0.5, 1.5).astype(jnp.bfloat16),
        "in_weight": centred(arg_keys[2], (D, PROJ), D ** -0.5, 0.15625, ((0, 32),)),
        "conv_weight": centred(arg_keys[3], (CONV, CHANNELS), CONV ** -0.5, 3.0, ((1, 32),)),
        "conv_bias": centred(arg_keys[4], (CHANNELS,), 0.3, 1.75, ((0, 32),)),
        "step_bias": jnp.clip(jax.random.uniform(arg_keys[5], (HEADS,), jnp.float32, -7.0, -2.3), -7.0, -2.3),
        "decay_log": jnp.clip(jax.random.uniform(arg_keys[6], (HEADS,), jnp.float32, -1.0, 1.0), -1.0, 1.0),
        "skip_gain": jnp.clip(jax.random.uniform(arg_keys[7], (HEADS,), jnp.float32, 0.2, 1.0), 0.2, 1.0),
        "norm_gain": jnp.clip(1.0 + 0.1 * jax.random.normal(arg_keys[8], (INNER,), jnp.float32), 0.5, 1.5).astype(jnp.bfloat16),
        "out_weight": centred(arg_keys[9], (INNER, D), INNER ** -0.5, 0.109375, ((0, 32),)),
        "cotangent": centred(arg_keys[10], (SEQS, LENGTH, D), 1.0, 6.0, ((0, 8), (1, 4))),
    }


HIGHEST = lax.Precision.HIGHEST

@jax.custom_vjp
def low(v):
    return lax.optimization_barrier(v.astype(jnp.bfloat16)).astype(jnp.float32)

@jax.custom_vjp
def low_back(v):
    return v

def low_keep(v):
    return (low(v), None)

def low_pass(kept, grad):
    return (grad,)

def back_keep(v):
    return (v, None)

def back_low(kept, grad):
    return (low(grad),)
low.defvjp(low_keep, low_pass)
low_back.defvjp(back_keep, back_low)

def pre_norm(inputs, gain_vec):
    return inputs * lax.rsqrt(lax.optimization_barrier(jnp.mean(inputs * inputs, axis=-1, keepdims=True)) + 1e-05) * gain_vec

def gated_norm(mixer_out, gate_in, gain_vec):
    gated = mixer_out * jax.nn.silu(gate_in)
    return gated * lax.rsqrt(lax.optimization_barrier(jnp.mean(gated * gated, axis=-1, keepdims=True)) + 1e-05) * gain_vec

def ssd_local(projected, edge_rows, conv_weight, conv_bias, step_bias, decay_log, skip_gain):
    sequences = projected.shape[0]
    positions = projected.shape[1]
    blocks = positions // BLOCK_LEN
    gate_in = projected[:, :, :INNER]
    conv_in = projected[:, :, INNER:INNER + CHANNELS]
    step_raw = projected[:, :, INNER + CHANNELS:]
    padded = jnp.concatenate([edge_rows, conv_in], axis=1)
    conv_out = conv_bias + jnp.zeros_like(conv_in)
    for tap_index in range(CONV):
        conv_out = conv_out + padded[:, tap_index:tap_index + positions] * conv_weight[tap_index]
    active = jax.nn.silu(conv_out)
    values_in = active[:, :, :INNER].reshape(sequences, positions, HEADS, HEAD_DIM)
    input_map = active[:, :, INNER:INNER + STATE].reshape(sequences, blocks, BLOCK_LEN, STATE)
    output_map = active[:, :, INNER + STATE:]
    step_size = jax.nn.softplus(step_raw + step_bias)
    log_decay = -jnp.exp(decay_log) * step_size
    log_run = jnp.cumsum(log_decay.reshape(sequences, blocks, BLOCK_LEN, HEADS), axis=2)
    causal = jnp.tril(jnp.ones((BLOCK_LEN, BLOCK_LEN), bool))
    log_gap = log_run[:, :, :, None, :] - log_run[:, :, None, :, :]
    decay_pairs = jnp.exp(jnp.where(causal[None, None, :, :, None], log_gap, -1e+30))
    scaled = (values_in * step_size[..., None]).reshape(sequences, blocks, BLOCK_LEN, HEADS, HEAD_DIM)
    output_blocks = output_map.reshape(sequences, blocks, BLOCK_LEN, STATE)
    scores = jnp.einsum('bcqn,bcsn->bcqs', output_blocks, input_map, precision=HIGHEST)
    inner_out = jnp.einsum('bcqsh,bcshp->bcqhp', scores[..., None] * decay_pairs, scaled, precision=HIGHEST)
    to_end = jnp.exp(log_run[:, :, -1:, :] - log_run)
    block_states = jnp.einsum('bcshp,bcsn->bchpn', scaled * to_end[..., None], input_map, precision=HIGHEST)
    block_decay = jnp.exp(log_run[:, :, -1, :])
    running = jnp.zeros((sequences, HEADS, HEAD_DIM, STATE), jnp.float32)
    starts = []
    for block_index in range(blocks):
        starts.append(running)
        running = block_decay[:, block_index, :, None, None] * running + block_states[:, block_index]
    start_states = jnp.stack(starts, axis=1)
    carried = jnp.einsum('bcqn,bchpn->bcqhp', output_blocks, start_states, precision=HIGHEST) * jnp.exp(log_run)[..., None]
    mixer_out = (inner_out + carried).reshape(sequences, positions, HEADS, HEAD_DIM) + skip_gain[:, None] * values_in
    block_totals = log_run[:, :, -1, :]
    log_offset = jnp.cumsum(block_totals, axis=1) - block_totals
    log_device = (log_run + log_offset[:, :, None, :]).reshape(sequences, positions, HEADS)
    decay_total = jnp.exp(lax.optimization_barrier(jnp.sum(log_decay, axis=1)))
    return (mixer_out.reshape(sequences, positions, INNER), output_map, log_device, gate_in, running, decay_total)

def whole_block(inputs, pre_gain, in_weight, conv_weight, conv_bias, step_bias, decay_log, skip_gain, norm_gain, out_weight):
    normed = low(pre_norm(inputs, pre_gain))
    projected = low_back(jnp.einsum('btd,de->bte', normed, in_weight, precision=HIGHEST))
    edge_rows = jnp.zeros((inputs.shape[0], CONV - 1, CHANNELS), jnp.float32)
    local_out = ssd_local(projected, edge_rows, conv_weight, conv_bias, step_bias, decay_log, skip_gain)
    normed_out = low(gated_norm(local_out[0], local_out[3], norm_gain))
    return inputs + jnp.einsum('bti,id->btd', normed_out, out_weight, precision=HIGHEST)

def reference(tokens, pre_gain, in_weight, conv_weight, conv_bias, step_bias, decay_log, skip_gain, norm_gain, out_weight, cotangent):
    weights = tuple((weight.astype(jnp.float32) for weight in (pre_gain, in_weight, conv_weight, conv_bias, step_bias, decay_log, skip_gain, norm_gain, out_weight)))

    def per_sequence(totals, item):
        sequence, cot_rows = item
        result, pullback = jax.vjp(whole_block, sequence.astype(jnp.float32)[None], *weights)
        grads = pullback(cot_rows.astype(jnp.float32)[None])
        totals = tuple((total + grad for total, grad in zip(totals, grads[1:])))
        return (totals, (result[0].astype(jnp.bfloat16), grads[0][0]))
    zeros = tuple((jnp.zeros_like(weight) for weight in weights))
    totals, outputs = lax.scan(per_sequence, zeros, (tokens, cotangent))
    mixed, grad_tokens = outputs
    return (mixed, grad_tokens, totals[0], totals[1], totals[2], totals[3], totals[4], totals[5], totals[6], totals[7], totals[8])
```

```python
import functools
import jax
import jax.numpy as jnp
from jax import lax
from jax.experimental import pallas as pl
from jax.experimental.pallas import tpu as pltpu
from jax.sharding import PartitionSpec as P

INNER = 3072
HEADS = 48
HEAD_DIM = 64
STATE = 128
CONV = 4
BLOCK_LEN = 256
CHANNELS = 3328
PROJ = 6448
EDGE = 16
GROUP = 4
GROUPS = HEADS // GROUP
GCOLS = GROUP * HEAD_DIM
PAIRS = GROUP // 2
STRIP = 128
LOG2E = 1.4426950408889634
F32 = jnp.float32
BF16 = jnp.bfloat16

NT = (((1,), (1,)), ((), ()))
TN = (((0,), (0,)), ((), ()))
NN = (((1,), (0,)), ((), ()))


def dot(a, b, dims=NN):
    return lax.dot_general(a, b, dims, preferred_element_type=F32)


def first_half(shape):
    return lax.broadcasted_iota(jnp.int32, shape, len(shape) - 1) < HEAD_DIM


def per_pair(cols, kind, pair, rows):
    at = kind * GROUP + 2 * pair
    left, right = cols[rows, at : at + 1], cols[rows, at + 1 : at + 2]
    shape = (left.shape[0], 2 * HEAD_DIM)
    return jnp.where(
        first_half(shape), jnp.broadcast_to(left, shape), jnp.broadcast_to(right, shape)
    )


def convolved(p_ref, w_ref, b_ref, lo, count, lanes):
    out = b_ref[0:1, lanes] + jnp.zeros((count, lanes.size), F32)
    for tap in range(CONV):
        at = EDGE - CONV + 1 + tap + lo
        out = out + p_ref[at : at + count, lanes] * w_ref[tap : tap + 1, lanes]
    return out


def sigmoid(v):
    return 0.5 + 0.5 * jnp.tanh(0.5 * v)


def softplus(v):
    return jnp.maximum(v, 0.0) + jnp.log1p(jnp.exp(-jnp.abs(v)))


def lower_triangle():
    row = lax.broadcasted_iota(jnp.int32, (BLOCK_LEN, BLOCK_LEN), 0)
    col = lax.broadcasted_iota(jnp.int32, (BLOCK_LEN, BLOCK_LEN), 1)
    return jnp.where(row >= col, 1.0, 0.0)


def exact_dot(a, b, dims=NN):
    return lax.dot_general(
        a, b, dims, precision=lax.Precision.HIGHEST, preferred_element_type=F32
    )


def steps_kernel(
    p_ref, w_ref, b_ref, bias_ref, decay_ref, cols_ref, rows_ref, maps_ref, er_ref, decays_ref
):
    positions = maps_ref.shape[0]
    blocks = positions // BLOCK_LEN
    lower = lower_triangle()
    used = lax.broadcasted_iota(jnp.int32, (1, 128), 1) < HEADS
    rate = -jnp.exp(decay_ref[...])
    total = jnp.zeros((1, 128), F32)
    for block in range(blocks):
        lo = block * BLOCK_LEN
        rows = slice(lo, lo + BLOCK_LEN)
        conv = convolved(p_ref, w_ref, b_ref, lo, BLOCK_LEN, pl.ds(0, 2 * STATE))
        maps_ref[rows, :] = (conv * sigmoid(conv)).astype(BF16)
        step = softplus(p_ref[EDGE + lo : EDGE + lo + BLOCK_LEN, 2 * STATE : 2 * STATE + 128] + bias_ref[...])
        step = jnp.where(used, step, 0.0)
        run = exact_dot(lower, rate * step)
        end = run[BLOCK_LEN - 1 :]
        total = total + end
        run2 = run * LOG2E
        grown = jnp.exp(run)
        er_ref[rows, :] = grown
        decays_ref[block : block + 1, :] = jnp.exp(end)
        turned = run2.T
        kinds = (step, run2, grown, jnp.exp(end - run))
        for group in range(GROUPS):
            heads = slice(group * GROUP, (group + 1) * GROUP)
            rows_ref[group, :, rows] = turned[heads]
            cols_ref[group, rows, :] = jnp.concatenate([kind[:, heads] for kind in kinds], axis=1)
    decays_ref[blocks : blocks + 1, :] = jnp.exp(total)
    decays_ref[blocks + 1 :, :] = jnp.zeros((8 - blocks - 1, 128), F32)


def steps_of(p, w, b, bias, decay_log, positions):
    ext = p.shape[0]
    at = INNER // PIECE
    return pl.pallas_call(
        steps_kernel,
        grid=(1,),
        in_specs=[
            pl.BlockSpec((ext, PIECE), lambda i: (0, at)),
            pl.BlockSpec((8, PIECE), lambda i: (0, at)),
            pl.BlockSpec((1, PIECE), lambda i: (0, at)),
            pl.BlockSpec((1, 128), lambda i: (0, 0)),
            pl.BlockSpec((1, 128), lambda i: (0, 0)),
        ],
        out_specs=[pl.BlockSpec(memory_space=pltpu.VMEM)] * 5,
        out_shape=[
            jax.ShapeDtypeStruct((GROUPS, positions, 4 * GROUP), F32),
            jax.ShapeDtypeStruct((GROUPS, GROUP, positions), F32),
            jax.ShapeDtypeStruct((positions, 2 * STATE), BF16),
            jax.ShapeDtypeStruct((positions, 128), F32),
            jax.ShapeDtypeStruct((8, 128), F32),
        ],
        compiler_params=pltpu.CompilerParams(vmem_limit_bytes=48 * 2**20),
        cost_estimate=pl.CostEstimate(
            flops=4 * positions * BLOCK_LEN * 128, bytes_accessed=16 * positions * 512,
            transcendentals=positions * 1024,
        ),
        name="steps",
    )(p, w, b, bias, decay_log)


def masked_scores(maps_ref, scores_ref, blocks):
    row = lax.broadcasted_iota(jnp.int32, (BLOCK_LEN, BLOCK_LEN), 0)
    col = lax.broadcasted_iota(jnp.int32, (BLOCK_LEN, BLOCK_LEN), 1)
    for block in range(blocks):
        rows = slice(block * BLOCK_LEN, (block + 1) * BLOCK_LEN)
        scores = dot(maps_ref[rows, STATE:], maps_ref[rows, :STATE], NT)
        scores_ref[block] = jnp.where(row >= col, scores, 0.0)


def chain_copy(site, group, by, sent, got, send_sem, recv_sem):
    return pltpu.make_async_remote_copy(
        src_ref=sent.at[group % sent.shape[0]], dst_ref=got.at[group], send_sem=send_sem.at[group],
        recv_sem=recv_sem.at[group], device_id=(site.over(by), site.f), device_id_type=MESH,
    )


def by_head(decays, group, kind, rows=GCOLS):
    return jnp.concatenate(
        [
            jnp.full((HEAD_DIM, STATE), decays[kind, group * GROUP + head], F32)
            for head in range(rows // HEAD_DIM)
        ],
        axis=0,
    )


def scan_forward_kernel(
    pieces, lag, decays, p_ref, w_ref, b_ref, cols_ref, late_ref, rows_ref, maps_ref, skip_ref, own,
    y_ref, starts_ref, whole,
    scores_ref, x_ref, states_ref, sent, got, chain_send, chain_recv, *gather_refs,
):
    positions = y_ref.shape[0]
    blocks = positions // BLOCK_LEN
    step = pl.program_id(0)
    site = Site()
    behind = site.zs - 1

    @pl.when(step == 0)
    def _():
        site.greet()
        masked_scores(maps_ref, scores_ref, blocks)

    gather = Gather(site, own, whole, *gather_refs)
    at_stages(gather.stages, pieces, lag, step, gather.run)

    @pl.when(step < GROUPS)
    def _():
        slot = step % site.zs
        for pair in range(PAIRS):
            lanes = pl.ds(pair * 2 * HEAD_DIM, 2 * HEAD_DIM)
            for block in range(blocks):
                lo = block * BLOCK_LEN
                rows = slice(lo, lo + BLOCK_LEN)
                conv = convolved(p_ref, w_ref, b_ref, lo, BLOCK_LEN, lanes)
                x = conv * sigmoid(conv)
                x_ref[slot, rows, lanes] = x
                xs = x * per_pair(cols_ref, 0, pair, rows)
                ended = (xs * per_pair(cols_ref, 3, pair, rows)).astype(BF16)
                states_ref[slot, block, pair * 2 * HEAD_DIM : (pair + 1) * 2 * HEAD_DIM, :] = dot(
                    ended, maps_ref[rows, :STATE], TN
                )

    linked = step - site.z

    @pl.when(jnp.logical_and(linked >= 0, linked < GROUPS))
    def _():
        slot = linked % site.zs

        @pl.when(site.z == 0)
        def _():
            got[linked] = jnp.zeros((GCOLS, STATE), BF16)

        @pl.when(site.z > 0)
        def _():
            chain_copy(site, linked, 1, sent, got, chain_send, chain_recv).wait_recv()

        @pl.when(site.z < behind)
        def _():
            final = states_ref[slot, 0]
            for block in range(1, blocks):
                final = by_head(decays, linked, block) * final + states_ref[slot, block]
            sent[linked % sent.shape[0]] = (
                by_head(decays, linked, blocks) * got[linked].astype(F32) + final
            ).astype(BF16)
            chain_copy(site, linked, 1, sent, got, chain_send, chain_recv).start()

    group = step - behind

    @pl.when(jnp.logical_and(group >= 0, group < GROUPS))
    def _():
        slot = group % site.zs
        start = got[group].astype(F32)
        for block in range(blocks):
            if block:
                start = by_head(decays, group, block - 1) * start + states_ref[slot, block - 1]
            starts_ref[block] = start.astype(BF16)
        half = first_half((BLOCK_LEN, 2 * HEAD_DIM))
        for pair in range(PAIRS):
            lanes = pl.ds(pair * 2 * HEAD_DIM, 2 * HEAD_DIM)
            span = slice(pair * 2 * HEAD_DIM, (pair + 1) * 2 * HEAD_DIM)
            for block in range(blocks):
                lo = block * BLOCK_LEN
                rows = slice(lo, lo + BLOCK_LEN)
                x = x_ref[slot, rows, lanes]
                low = (x * per_pair(late_ref, 0, pair, rows)).astype(BF16)
                none = jnp.zeros_like(low)
                one, two = jnp.where(half, low, none), jnp.where(half, none, low)
                rest = skip_ref[0:1, lanes] * x + dot(
                    maps_ref[rows, STATE:], starts_ref[block, span, :], NT
                ) * per_pair(late_ref, 2, pair, rows)
                for strip in range(BLOCK_LEN // STRIP):
                    top = strip * STRIP
                    lim = top + STRIP
                    pieces_ = []
                    for side in range(2):
                        head = 2 * pair + side
                        at = GROUP + head
                        gap = (
                            late_ref[lo + top : lo + lim, at : at + 1]
                            - rows_ref[head : head + 1, lo : lo + lim]
                        )
                        decay = jnp.exp2(jnp.minimum(gap, 0.0))
                        pieces_.append((scores_ref[block, top:lim, :lim] * decay).astype(BF16))
                    y = dot(pieces_[0], one[:lim]) + dot(pieces_[1], two[:lim])
                    y_ref[lo + top : lo + lim, lanes] = y + rest[top:lim]

        @pl.when(site.z < behind)
        def _():
            chain_copy(site, group, 1, sent, got, chain_send, chain_recv).wait_send()


def hosted_steps(pieces, stages):
    zs = lax.axis_size("seq")
    steps = GROUPS + zs - 1
    lag = max(1, (steps - pieces) // (stages - 1))
    return max(steps, pieces + lag * (stages - 1)), lag


def chain_scratch():
    ring = max(lax.axis_size("seq"), LAG + 2)
    return [
        pltpu.VMEM((ring, GCOLS, STATE), BF16),
        pltpu.VMEM((GROUPS, GCOLS, STATE), BF16),
        pltpu.SemaphoreType.DMA((GROUPS,)),
        pltpu.SemaphoreType.DMA((GROUPS,)),
    ]


def scan_forward(decays, p, w, b, cols, rows, maps, skip, own, positions, collective_id):
    blocks = positions // BLOCK_LEN
    ext = p.shape[0]
    zs, n = lax.axis_size("seq"), lax.axis_size("fsdp")
    rows_there, columns = own.shape[1:]
    pieces = columns // PIECE
    steps, lag = hosted_steps(pieces, stages_of(n) - 1)

    def early(s):
        return jnp.minimum(s, GROUPS - 1)

    def late(s):
        return jnp.clip(s - (zs - 1), 0, GROUPS - 1)

    anywhere = pl.BlockSpec(memory_space=pl.ANY)
    return pl.pallas_call(
        functools.partial(scan_forward_kernel, pieces, lag),
        grid=(steps,),
        in_specs=[
            pl.BlockSpec(memory_space=pltpu.SMEM),
            pl.BlockSpec((ext, GCOLS), lambda s: (0, early(s))),
            pl.BlockSpec((8, GCOLS), lambda s: (0, early(s))),
            pl.BlockSpec((1, GCOLS), lambda s: (0, early(s))),
            pl.BlockSpec((None, positions, 4 * GROUP), lambda s: (early(s), 0, 0)),
            pl.BlockSpec((None, positions, 4 * GROUP), lambda s: (late(s), 0, 0)),
            pl.BlockSpec((None, GROUP, positions), lambda s: (late(s), 0, 0)),
            pl.BlockSpec((positions, 2 * STATE), lambda s: (0, 0)),
            pl.BlockSpec((1, GCOLS), lambda s: (0, late(s))),
            anywhere,
        ],
        out_specs=[
            pl.BlockSpec((positions, GCOLS), lambda s: (0, late(s))),
            pl.BlockSpec((blocks, GCOLS, STATE), lambda s: (0, late(s), 0)),
            anywhere,
        ],
        out_shape=[
            jax.ShapeDtypeStruct((positions, INNER), F32),
            jax.ShapeDtypeStruct((blocks, INNER, STATE), BF16),
            jax.ShapeDtypeStruct((zs, n, rows_there, columns), BF16),
        ],
        scratch_shapes=[
            pltpu.VMEM((blocks, BLOCK_LEN, BLOCK_LEN), F32),
            pltpu.VMEM((zs, positions, GCOLS), F32),
            pltpu.VMEM((zs, blocks, GCOLS, STATE), F32),
        ]
        + chain_scratch()
        + gather_scratch(pieces),
        compiler_params=pltpu.CompilerParams(
            collective_id=collective_id, has_side_effects=True, vmem_limit_bytes=48 * 2**20
        ),
        cost_estimate=pl.CostEstimate(
            flops=12 * positions * INNER * BLOCK_LEN, bytes_accessed=24 * positions * INNER,
            transcendentals=HEADS * positions * BLOCK_LEN,
        ),
        name="scan_forward",
    )(decays, p, w, b, cols, cols, rows, maps, skip, own)


def gate_kernel(
    y_ref, gate_ref, gno_ref, gain_ref, er_ref, maps_ref,
    out_ref, dy_ref, dye_ref, ggate_ref, ends_ref, gated_ref,
):
    rows = y_ref.shape[0]
    width = 2 * HEAD_DIM
    shape = (rows, width)
    square = jnp.zeros(shape, F32)
    cross = jnp.zeros(shape, F32)

    def decayed(pair):
        return jnp.where(
            first_half(shape),
            jnp.broadcast_to(er_ref[:, 2 * pair : 2 * pair + 1], shape),
            jnp.broadcast_to(er_ref[:, 2 * pair + 1 : 2 * pair + 2], shape),
        )

    for pair in range(HEADS // 2):
        lanes = slice(pair * width, (pair + 1) * width)
        gate = gate_ref[:, lanes]
        gated = y_ref[:, lanes] * gate * sigmoid(gate)
        gated_ref[:, lanes] = gated
        square = square + gated * gated
        cross = cross + gated * (gain_ref[:, lanes] * gno_ref[:, lanes])
    r1 = lax.rsqrt(jnp.sum(square, axis=-1, keepdims=True) * (1.0 / INNER) + 1e-05)
    back = r1 * r1 * r1 * (jnp.sum(cross, axis=-1, keepdims=True) * (1.0 / INNER))

    @pl.when(pl.program_id(0) % (BLOCK_LEN // rows) == 0)
    def _():
        ends_ref[...] = jnp.zeros_like(ends_ref)

    for pair in range(HEADS // 2):
        lanes = slice(pair * width, (pair + 1) * width)
        gate = gate_ref[:, lanes]
        sig = sigmoid(gate)
        gated = gated_ref[:, lanes]
        gain = gain_ref[:, lanes]
        out_ref[:, lanes] = (gated * r1 * gain).astype(BF16)
        ggated = gno_ref[:, lanes] * r1 * gain - gated * back
        low = (ggated * (gate * sig)).astype(BF16)
        dy_ref[:, lanes] = low
        ggate_ref[:, lanes] = (
            ggated * y_ref[:, lanes] * (sig * (1.0 + gate * (1.0 - sig)))
        ).astype(BF16)
        scaled = (low.astype(F32) * decayed(pair)).astype(BF16)
        dye_ref[:, lanes] = scaled
        ends_ref[lanes, :] += dot(scaled, maps_ref[:, STATE:], TN)


def gated(y, gate, gno, gain, er, maps):
    positions = y.shape[0]
    tile = 128
    per_block = BLOCK_LEN // tile
    wide = pl.BlockSpec((tile, INNER), lambda i: (i, 0))
    states = pl.BlockSpec((None, INNER, STATE), lambda i: (i // per_block, 0, 0))
    low = jax.ShapeDtypeStruct((positions, INNER), BF16)
    return pl.pallas_call(
        gate_kernel,
        grid=(positions // tile,),
        in_specs=[
            wide,
            wide,
            wide,
            pl.BlockSpec((1, INNER), lambda i: (0, 0)),
            pl.BlockSpec((tile, 128), lambda i: (i, 0)),
            pl.BlockSpec((tile, 2 * STATE), lambda i: (i, 0)),
        ],
        out_specs=[wide] * 4 + [states],
        out_shape=[
            low,
            low,
            low,
            low,
            jax.ShapeDtypeStruct((positions // BLOCK_LEN, INNER, STATE), F32),
        ],
        scratch_shapes=[pltpu.VMEM((tile, INNER), F32)],
        compiler_params=pltpu.CompilerParams(vmem_limit_bytes=48 * 2**20),
        cost_estimate=pl.CostEstimate(
            flops=4 * positions * INNER * STATE, bytes_accessed=24 * positions * INNER,
            transcendentals=2 * positions * INNER,
        ),
        name="gate",
    )(y, gate, gno, gain, er, maps)


OUT_PIECES = 6
OUT_SPLIT = 2


def scan_backward_kernel(
    decays, p_ref, w_ref, b_ref, cols_ref, rows_ref, maps_ref, skip_ref, y_ref, dy_ref,
    dye_ref, st_ref, grads_ref, turned_ref, cot_ref, ggate_ref, wgate_ref, wconv_ref,
    plast_ref, wlast_ref, blast_ref, bias_ref, decay_ref, grown_ref, tokens_ref, gain_ref,
    own_ref, gtokens_ref, total_ref,
    scores_ref, dscores_ref, dpad_ref, gacc_ref, dl_ref, x_ref, tail_ref, runs_ref, direct_ref, ends_ref,
    cross_ref, sent, got, chain_send, chain_recv, edge_sent, edge_got, edge_send, edge_recv,
    t_sent, t_got, t_send, t_recv, *scatter_refs,
):
    step_at = pl.program_id(0)
    site = Site()
    behind = site.zs - 1
    positions = y_ref.shape[0]
    gates = INNER // PIECE
    ahead = PIECE // GCOLS
    later = step_at - OUT_PIECES

    @pl.when(step_at == 0)
    def _():
        site.greet()
        gtokens_ref[...] = jnp.zeros_like(gtokens_ref)
        runs_ref[...] = jnp.zeros_like(runs_ref)
        direct_ref[...] = jnp.zeros_like(direct_ref)
        t_sent[0, CONV + 1 :, 0:INNER] = jnp.zeros((8 - CONV - 1, INNER), F32)

    def edge_copy(group):
        return pltpu.make_async_remote_copy(
            src_ref=edge_sent.at[group], dst_ref=edge_got.at[group], send_sem=edge_send.at[group],
            recv_sem=edge_recv.at[group], device_id=(site.over(behind), site.f), device_id_type=MESH,
        )

    def add_normed(weight_ref):
        def one(i, carry):
            span = pl.ds(pl.multiple_of(i * PIECE, 128), PIECE)
            gtokens_ref[:, span] += dot(x_ref[step_at % XRING], weight_ref[span, :], NT)
            return carry

        lax.fori_loop(0, gtokens_ref.shape[1] // PIECE, one, 0)

    @pl.when(step_at < OUT_PIECES)
    def _():
        cots = cot_ref.shape[1] // PIECE
        span = pl.ds(pl.multiple_of((step_at % cots) * PIECE, 128), PIECE)
        x_ref[step_at % XRING] = cot_ref[:, span]

    inside = jnp.logical_and(later >= 0, later < 2 * gates)

    @pl.when(jnp.logical_and(inside, later % 2 == 1))
    def _():
        x_ref[step_at % XRING] = ggate_ref[...]
        add_normed(wgate_ref)

    @pl.when(jnp.logical_and(inside, later % 2 == 0))
    def _():
        for side in range(ahead):
            group = (later // 2) * ahead + side
            lanes = slice(side * GCOLS, (side + 1) * GCOLS)

            @pl.when(site.z < behind)
            def _(group=group, lanes=lanes):
                edge_copy(group).wait_recv()
                x_ref[step_at % XRING, positions - 8 :, lanes] = (
                    tail_ref[group] + edge_got[group]
                ).astype(BF16)

            @pl.when(site.z > 0)
            def _(group=group):
                edge_copy(group).wait_send()

        add_normed(wconv_ref)

    last = OUT_PIECES + 2 * gates
    start = last - LAG - 1
    slot = last % XRING
    wide = 2 * STATE
    totals = Totals(site, t_sent, t_got, t_send, t_recv)

    def last_edge():
        return pltpu.make_async_remote_copy(
            src_ref=edge_sent.at[GROUPS], dst_ref=edge_got.at[GROUPS], send_sem=edge_send.at[GROUPS],
            recv_sem=edge_recv.at[GROUPS], device_id=(site.over(behind), site.f), device_id_type=MESH,
        )

    @pl.when(step_at == start)
    def _():
        tail, edge = maps_backward(plast_ref, wlast_ref, blast_ref, gacc_ref, dpad_ref, x_ref, slot, t_sent)
        tail_ref[GROUPS] = tail
        edge_sent[GROUPS] = edge

        @pl.when(site.z > 0)
        def _():
            last_edge().start()

        steps_backward(
            plast_ref, bias_ref, decay_ref, grown_ref, runs_ref, direct_ref, ends_ref, cross_ref, x_ref, slot,
            t_sent,
        )
        totals.start(0)

    for t in range(totals.count):

        @pl.when(step_at == start + 1 + t)
        def _(t=t):
            totals.next(t)

    @pl.when(step_at == start + 1 + totals.count)
    def _():
        total_ref[...] = t_sent[totals.count % 2]

    @pl.when(step_at == last)
    def _():
        @pl.when(site.z < behind)
        def _():
            last_edge().wait_recv()
            x_ref[slot, positions - 8 :, 0:wide] = (tail_ref[GROUPS] + edge_got[GROUPS]).astype(BF16)

        @pl.when(site.z > 0)
        def _():
            last_edge().wait_send()

        add_normed(wconv_ref)

    tile = 128
    after = step_at - last - 1

    @pl.when(jnp.logical_and(after >= 0, after < positions // tile))
    def _():
        rows = pl.ds(pl.multiple_of(after * tile, tile), tile)
        features = gtokens_ref.shape[1]
        inputs = tokens_ref[rows, :].astype(F32)
        r0 = lax.rsqrt(jnp.sum(inputs * inputs, axis=-1, keepdims=True) * (1.0 / features) + 1e-05)
        f = gain_ref[...] * gtokens_ref[rows, :]
        share = r0 * r0 * r0 * (jnp.sum(f * inputs, axis=-1, keepdims=True) * (1.0 / features))
        gtokens_ref[rows, :] = cot_ref[rows, :].astype(F32) + r0 * f - inputs * share

    def is_later(piece):
        return jnp.minimum(piece, OUT_PIECES) // OUT_PIECES

    def kind(piece):
        return (1 - is_later(piece)) * (1 + jnp.minimum(piece, OUT_PIECES - 1) // (OUT_PIECES // OUT_SPLIT))

    def column(piece):
        after = jnp.maximum(piece - OUT_PIECES, 0)
        return jnp.minimum(piece, OUT_PIECES) + is_later(piece) * (1 - after % 2) * gates + after // 2

    scatter = Streamed(site, turned_ref, kind, x_ref, own_ref, column, scatter_refs)
    at_stages(scatter.stages, last + 1, LAG, step_at, scatter.run)

    linked = step_at - (behind - site.z)
    blocks = positions // BLOCK_LEN

    @pl.when(jnp.logical_and(linked >= 0, linked < GROUPS))
    def _():
        @pl.when(site.z == behind)
        def _():
            got[linked] = jnp.zeros((GCOLS, STATE), BF16)

        @pl.when(site.z < behind)
        def _():
            chain_copy(site, linked, behind, sent, got, chain_send, chain_recv).wait_recv()

        @pl.when(site.z > 0)
        def _():
            span = pl.ds(pl.multiple_of(linked * GCOLS, GCOLS), GCOLS)
            grad = got[linked].astype(F32)
            for block in reversed(range(blocks)):
                grad = by_head(decays, linked, block) * grad + grads_ref[block, span, :]
            sent[linked % sent.shape[0]] = grad.astype(BF16)
            chain_copy(site, linked, behind, sent, got, chain_send, chain_recv).start()

    group = step_at - max(behind, LAG + 1)

    @pl.when(jnp.logical_and(group >= 0, group < GROUPS))
    def _():
        scan_backward_group(
            group, decays, p_ref, w_ref, b_ref, cols_ref, rows_ref, maps_ref, skip_ref, y_ref,
            dy_ref, dye_ref, st_ref, grads_ref, x_ref, tail_ref, edge_sent, t_sent, runs_ref, direct_ref,
            ends_ref, cross_ref, scores_ref, dscores_ref, dpad_ref, gacc_ref, dl_ref, got,
        )

        @pl.when(site.z > 0)
        def _():
            edge_copy(group).start()
            chain_copy(site, group, behind, sent, got, chain_send, chain_recv).wait_send()


def maps_backward(p_ref, w_ref, b_ref, grad_ref, dpad_ref, x_ref, slot, t_sent):
    positions, wide = grad_ref.shape
    blocks = positions // BLOCK_LEN
    lanes = pl.ds(0, wide)
    taps = [jnp.zeros((1, wide), F32) for _ in range(CONV + 1)]
    for block in range(blocks):
        lo = block * BLOCK_LEN
        conv = convolved(p_ref, w_ref, b_ref, lo, BLOCK_LEN, lanes)
        sig = sigmoid(conv)
        dconv = grad_ref[lo : lo + BLOCK_LEN, :] * (sig * (1.0 + conv * (1.0 - sig)))
        dpad_ref[8 + lo : 8 + lo + BLOCK_LEN, :] = dconv
        for tap in range(CONV):
            at = EDGE - CONV + 1 + tap + lo
            taps[tap] = taps[tap] + jnp.sum(
                dconv * p_ref[at : at + BLOCK_LEN, 0:wide], axis=0, keepdims=True
            )
        taps[CONV] = taps[CONV] + jnp.sum(dconv, axis=0, keepdims=True)
    for index in range(CONV + 1):
        t_sent[0, index : index + 1, INNER : INNER + wide] = taps[index]
    t_sent[0, CONV + 1 :, INNER : INNER + wide] = jnp.zeros((8 - CONV - 1, wide), F32)

    def back_rows(at, count):
        back = jnp.zeros((count, wide), F32)
        for tap in range(CONV):
            start = at + CONV - 1 - tap
            back = back + dpad_ref[start : start + count, :] * w_ref[tap : tap + 1, 0:wide]
        return back

    for block in range(blocks):
        lo = block * BLOCK_LEN
        x_ref[slot, lo : lo + BLOCK_LEN, 0:wide] = back_rows(8 + lo, BLOCK_LEN).astype(BF16)
    return back_rows(positions, 8), back_rows(0, 8)


def steps_backward(
    p_ref, bias_ref, decay_ref, decays_ref, runs_ref, direct_ref, ends_ref, cross_ref, x_ref, slot, t_sent
):
    positions = runs_ref.shape[0]
    blocks = positions // BLOCK_LEN
    wide = 2 * STATE
    used = lax.broadcasted_iota(jnp.int32, (1, 128), 1) < HEADS
    rate = -jnp.exp(decay_ref[...])
    by_heads = jnp.zeros((8, 128), F32)
    for at in range(0, INNER, PIECE):
        spread = jnp.where(
            (at + lax.broadcasted_iota(jnp.int32, (PIECE, 128), 0)) // HEAD_DIM
            == lax.broadcasted_iota(jnp.int32, (PIECE, 128), 1),
            1.0,
            0.0,
        )
        by_heads = by_heads + exact_dot(ends_ref[:, at : at + PIECE], spread)
    per_group = blocks * GROUP
    crossed = jnp.sum(cross_ref[...].reshape(GROUPS * per_group, STATE), axis=1, keepdims=True)
    row = lax.broadcasted_iota(jnp.int32, (GROUPS * per_group, 128), 0)
    lane = lax.broadcasted_iota(jnp.int32, (GROUPS * per_group, 128), 1)
    same = (row // per_group) * GROUP + row % GROUP == lane
    tri_row = lax.broadcasted_iota(jnp.int32, (BLOCK_LEN, BLOCK_LEN), 0)
    tri_col = lax.broadcasted_iota(jnp.int32, (BLOCK_LEN, BLOCK_LEN), 1)
    upper = jnp.where(tri_row <= tri_col, 1.0, 0.0)
    grad_bias = jnp.zeros((1, 128), F32)
    grad_decay = jnp.zeros((1, 128), F32)
    for block in range(blocks):
        lo = block * BLOCK_LEN
        rows = slice(lo, lo + BLOCK_LEN)
        here = jnp.logical_and(same, (row % per_group) // GROUP == block)
        end = by_heads[block : block + 1] + decays_ref[block : block + 1, :] * jnp.sum(
            jnp.where(here, crossed, 0.0), axis=0, keepdims=True
        )
        arg = p_ref[EDGE + lo : EDGE + lo + BLOCK_LEN, wide : wide + 128] + bias_ref[...]
        step = softplus(arg)
        grad_log = exact_dot(upper, runs_ref[rows, :]) + end
        grad_step = jnp.where(used, (direct_ref[rows, :] + rate * grad_log) * sigmoid(arg), 0.0)
        grad_bias = grad_bias + jnp.sum(grad_step, axis=0, keepdims=True)
        grad_decay = grad_decay + jnp.sum(
            jnp.where(used, grad_log * (rate * step), 0.0), axis=0, keepdims=True
        )
        x_ref[slot, rows, wide : wide + 128] = grad_step.astype(BF16)
        x_ref[slot, rows, wide + 128 :] = jnp.zeros((BLOCK_LEN, PIECE - wide - 128), BF16)
    t_sent[0, :, INNER + wide :] = jnp.concatenate(
        [grad_bias, grad_decay, by_heads[blocks : blocks + 1], jnp.zeros((5, 128), F32)], axis=0
    )


def scan_backward_group(
    step_at, decays, p_ref, w_ref, b_ref, cols_ref, rows_ref, maps_ref, skip_ref, y_ref, dy_ref,
    dye_ref, st_ref, grads_ref, x_ref, tail_ref, edge_ref, t_sent, runs_ref, direct_ref, ends_ref,
    cross_ref, scores_ref, dscores_ref, dpad_ref, gacc_ref, dl_ref, got,
):
    positions = y_ref.shape[0]
    blocks = positions // BLOCK_LEN
    width = 2 * HEAD_DIM

    @pl.when(step_at == 0)
    def _():
        masked_scores(maps_ref, scores_ref, blocks)
        ends_ref[...] = jnp.zeros_like(ends_ref)
        dscores_ref[...] = jnp.zeros_like(dscores_ref)
        gacc_ref[...] = jnp.zeros_like(gacc_ref)
        dpad_ref[0:8, :] = jnp.zeros((8, GCOLS), F32)
        dpad_ref[positions + 8 : positions + 16, :] = jnp.zeros((8, GCOLS), F32)

    ahead = PIECE // GCOLS
    slot = (OUT_PIECES + 2 * (step_at // ahead)) % XRING
    offset = (step_at % ahead) * GCOLS
    group_span = pl.ds(pl.multiple_of(step_at * GCOLS, GCOLS), GCOLS)
    grad = got[step_at].astype(F32)
    for block in reversed(range(blocks)):
        if block < blocks - 1:
            grad = by_head(decays, step_at, block + 1) * grad + grads_ref[block + 1, group_span, :]
        dl_ref[block] = grad.astype(BF16)
        product = grad * st_ref[block].astype(F32)
        for head in range(GROUP):
            at = block * GROUP + head
            cross_ref[step_at, at : at + 1, :] = jnp.sum(
                product[head * HEAD_DIM : (head + 1) * HEAD_DIM], axis=0, keepdims=True
            )

    half = first_half((BLOCK_LEN, width))
    for pair in range(PAIRS):
        lanes = pl.ds(pair * width, width)
        span = slice(pair * width, (pair + 1) * width)
        gw = [jnp.zeros((1, width), F32) for _ in range(CONV + 2)]
        for block in range(blocks):
            lo = block * BLOCK_LEN
            rows = slice(lo, lo + BLOCK_LEN)
            conv = convolved(p_ref, w_ref, b_ref, lo, BLOCK_LEN, lanes)
            sig = sigmoid(conv)
            x = conv * sig
            step = per_pair(cols_ref, 0, pair, rows)
            to_end = per_pair(cols_ref, 3, pair, rows)
            xs = x * step
            low = xs.astype(BF16)
            ended = (xs * to_end).astype(BF16)
            dyl = dy_ref[rows, lanes]
            dyf = dyl.astype(F32)
            none = jnp.zeros_like(dyl)
            sides = (jnp.where(half, dyl, none), jnp.where(half, none, dyl))
            turned = dyf.T.astype(BF16)
            dxt = [None, None]
            for strip in range(BLOCK_LEN // STRIP):
                top = strip * STRIP
                lim = top + STRIP
                scores = scores_ref[block, top:lim, :lim]
                gathered = jnp.zeros((STRIP, lim), F32)
                for side in range(2):
                    head = 2 * pair + side
                    at = GROUP + head
                    gap = (
                        cols_ref[lo + top : lo + lim, at : at + 1]
                        - rows_ref[head : head + 1, lo : lo + lim]
                    )
                    decay = jnp.exp2(jnp.minimum(gap, 0.0))
                    gathered = gathered + dot(sides[side][top:lim], low[:lim], NT) * decay
                    part = dot(
                        turned[side * HEAD_DIM : (side + 1) * HEAD_DIM, top:lim],
                        (scores * decay).astype(BF16),
                    )
                    if strip == 0:
                        dxt[side] = jnp.concatenate(
                            [part, jnp.zeros((HEAD_DIM, BLOCK_LEN - STRIP), F32)], axis=1
                        )
                    else:
                        dxt[side] = dxt[side] + part
                dscores_ref[block, top:lim, :lim] += gathered
            inner = jnp.concatenate(dxt, axis=0).T
            dls = dl_ref[block, span, :]
            outer = dot(maps_ref[rows, :STATE], dls, NT) * to_end
            gacc_ref[rows, :STATE] += dot(ended, dls)
            gacc_ref[rows, STATE:] += dot(dye_ref[rows, lanes], st_ref[block, span, :])
            dxs = inner + outer
            skip = skip_ref[0:1, lanes]
            vs = xs * outer
            runs = dyf * (y_ref[rows, lanes] - skip * x) - low.astype(F32) * inner - vs
            direct = x * dxs
            lane = lax.broadcasted_iota(jnp.int32, (BLOCK_LEN, 128), 1)
            for sums_ref, values in ((runs_ref, runs), (direct_ref, direct)):
                left = jnp.sum(jnp.where(half, values, 0.0), axis=1, keepdims=True)
                right = jnp.sum(jnp.where(half, 0.0, values), axis=1, keepdims=True)
                at = step_at * GROUP + 2 * pair
                sums_ref[rows, :] += jnp.where(
                    lane == at, left, jnp.where(lane == at + 1, right, 0.0)
                )
            group_lanes = pl.ds(pl.multiple_of(step_at * GCOLS + pair * width, width), width)
            ends_ref[block : block + 1, group_lanes] = jnp.sum(vs, axis=0, keepdims=True)
            gw[CONV + 1] = gw[CONV + 1] + jnp.sum(dyf * x, axis=0, keepdims=True)
            dconv = (dxs * step + skip * dyf) * (sig * (1.0 + conv * (1.0 - sig)))
            gw[CONV] = gw[CONV] + jnp.sum(dconv, axis=0, keepdims=True)
            dpad_ref[8 + lo : 8 + lo + BLOCK_LEN, lanes] = dconv
            for tap in range(CONV):
                at = EDGE - CONV + 1 + tap + lo
                gw[tap] = gw[tap] + jnp.sum(
                    dconv * p_ref[at : at + BLOCK_LEN, lanes], axis=0, keepdims=True
                )
        group_lanes = pl.ds(pl.multiple_of(step_at * GCOLS + pair * width, width), width)
        for index in range(CONV + 1):
            t_sent[0, index : index + 1, group_lanes] = gw[index]
        ends_ref[blocks : blocks + 1, group_lanes] = gw[CONV + 1]
        edge = jnp.zeros((8, width), F32)
        for tap in range(CONV):
            edge = edge + dpad_ref[CONV - 1 - tap : CONV - 1 - tap + 8, lanes] * w_ref[tap : tap + 1, lanes]
        edge_ref[step_at, :, lanes] = edge
        for block in range(blocks):
            lo = block * BLOCK_LEN
            back = jnp.zeros((BLOCK_LEN, width), F32)
            for tap in range(CONV):
                at = 8 + CONV - 1 - tap + lo
                back = back + dpad_ref[at : at + BLOCK_LEN, lanes] * w_ref[tap : tap + 1, lanes]
            x_ref[slot, lo : lo + BLOCK_LEN, pl.ds(pl.multiple_of(offset + pair * width, width), width)] = (
                back.astype(BF16)
            )
            if block == blocks - 1:
                tail_ref[step_at, :, lanes] = back[BLOCK_LEN - 8 :]

    @pl.when(step_at == GROUPS - 1)
    def _():
        row = lax.broadcasted_iota(jnp.int32, (BLOCK_LEN, BLOCK_LEN), 0)
        col = lax.broadcasted_iota(jnp.int32, (BLOCK_LEN, BLOCK_LEN), 1)
        for block in range(blocks):
            rows = slice(block * BLOCK_LEN, (block + 1) * BLOCK_LEN)
            low = jnp.where(row >= col, dscores_ref[block], 0.0).astype(BF16)
            gacc_ref[rows, :STATE] += dot(low, maps_ref[rows, STATE:], TN)
            gacc_ref[rows, STATE:] += dot(low, maps_ref[rows, :STATE])


def scan_backward(
    decays, p, w, b, cols, rows, maps, skip, y, dy, dye, starts, ends, turned, cot, grad_gate,
    inw_gate, inw_conv, bias, decay_log, tokens, gain, own_rows, collective_id,
):
    positions = y.shape[0]
    features = inw_gate.shape[0]
    blocks = positions // BLOCK_LEN
    ext = p.shape[0]
    zs, n = lax.axis_size("seq"), lax.axis_size("fsdp")
    gates = INNER // PIECE
    pieces = OUT_PIECES + 2 * gates + 1
    count = exchange_count(zs, n)
    steps = pieces + max(LAG * (stages_of(n) - 1), count - LAG)
    width = CHANNELS + 128
    dma = pltpu.SemaphoreType.DMA

    def late(s):
        return jnp.clip(s - max(zs - 1, LAG + 1), 0, GROUPS - 1)

    def turn(s, most):
        return jnp.clip((s - OUT_PIECES) // 2, 0, most)

    once = pl.Buffered(1)
    own = pl.BlockSpec((positions, GCOLS), lambda s: (0, late(s)))
    eight = pl.BlockSpec((8, GCOLS), lambda s: (0, late(s)))
    states = pl.BlockSpec((blocks, GCOLS, STATE), lambda s: (0, late(s), 0))

    def whole(x):
        return pl.BlockSpec(x.shape, lambda s: (0,) * len(x.shape), pipeline_mode=once)

    return pl.pallas_call(
        scan_backward_kernel,
        grid=(steps,),
        in_specs=[
            pl.BlockSpec(memory_space=pltpu.SMEM),
            pl.BlockSpec((ext, GCOLS), lambda s: (0, late(s))),
            eight,
            pl.BlockSpec((1, GCOLS), lambda s: (0, late(s))),
            pl.BlockSpec((None, positions, 4 * GROUP), lambda s: (late(s), 0, 0)),
            pl.BlockSpec((None, GROUP, positions), lambda s: (late(s), 0, 0)),
            whole(maps),
            pl.BlockSpec((1, GCOLS), lambda s: (0, late(s))),
            own,
            own,
            own,
            states,
            whole(ends),
            whole(turned),
            whole(cot),
            pl.BlockSpec((positions, PIECE), lambda s: (0, turn(s - 1, gates - 1))),
            pl.BlockSpec((features, PIECE), lambda s: (0, turn(s - 1, gates - 1))),
            pl.BlockSpec((features, PIECE), lambda s: (0, turn(s, gates))),
            pl.BlockSpec((ext, PIECE), lambda s: (0, gates), pipeline_mode=once),
            pl.BlockSpec((8, PIECE), lambda s: (0, gates), pipeline_mode=once),
            pl.BlockSpec((1, PIECE), lambda s: (0, gates), pipeline_mode=once),
            whole(bias),
            whole(decay_log),
            whole(decays),
            whole(tokens),
            whole(gain),
        ],
        out_specs=[
            pl.BlockSpec((own_rows, pieces * PIECE), lambda s: (0, 0), pipeline_mode=once),
            pl.BlockSpec((positions, features), lambda s: (0, 0), pipeline_mode=once),
            pl.BlockSpec((8, width), lambda s: (0, 0), pipeline_mode=once),
        ],
        out_shape=[
            jax.ShapeDtypeStruct((own_rows, pieces * PIECE), F32),
            jax.ShapeDtypeStruct((positions, features), F32),
            jax.ShapeDtypeStruct((8, width), F32),
        ],
        scratch_shapes=[
            pltpu.VMEM((blocks, BLOCK_LEN, BLOCK_LEN), F32),
            pltpu.VMEM((blocks, BLOCK_LEN, BLOCK_LEN), F32),
            pltpu.VMEM((positions + 16, GCOLS), F32),
            pltpu.VMEM((positions, 2 * STATE), F32),
            pltpu.VMEM((blocks, GCOLS, STATE), BF16),
            pltpu.VMEM((XRING, positions, PIECE), BF16),
            pltpu.VMEM((GROUPS + 1, 8, GCOLS), F32),
            pltpu.VMEM((positions, 128), F32),
            pltpu.VMEM((positions, 128), F32),
            pltpu.VMEM((8, INNER), F32),
            pltpu.VMEM((GROUPS, blocks * GROUP, STATE), F32),
        ]
        + chain_scratch()
        + [
            pltpu.VMEM((GROUPS + 1, 8, GCOLS), F32),
            pltpu.VMEM((GROUPS + 1, 8, GCOLS), F32),
            dma((GROUPS + 1,)),
            dma((GROUPS + 1,)),
            pltpu.VMEM((2, 8, width), F32),
            pltpu.VMEM((count, 8, width), F32),
            dma((count,)),
            dma((count,)),
        ]
        + Streamed.scratch(own_rows),
        compiler_params=pltpu.CompilerParams(
            collective_id=collective_id, has_side_effects=True, vmem_limit_bytes=63 * 2**20
        ),
        cost_estimate=pl.CostEstimate(
            flops=24 * positions * INNER * BLOCK_LEN, bytes_accessed=30 * positions * INNER,
            transcendentals=HEADS * positions * BLOCK_LEN,
        ),
        name="scan_backward",
    )(
        decays, p, w, b, cols, rows, maps, skip, y, dy, dye, starts, ends, turned, cot, grad_gate,
        inw_gate, inw_conv, p, w, b, bias, decay_log, decays, tokens, gain,
    )


PIECE = 512
LAG = 2
HALF = PIECE // 2
MESH = pl.DeviceIdType.MESH


class Site:
    def __init__(self):
        self.zs, self.n = lax.axis_size("seq"), lax.axis_size("fsdp")
        self.z, self.f = lax.axis_index("seq"), lax.axis_index("fsdp")
        self.chips = self.n // 2
        self.bits = self.chips.bit_length() - 1

    def bit(self, j):
        return (self.f // 2**j) % 2

    def flip(self, js):
        f = self.f
        for j in js:
            f = f + (1 - 2 * self.bit(j)) * 2**j
        return f

    def over(self, dz):
        return (self.z + dz) % self.zs

    def greet(self):
        barrier = pltpu.get_barrier_semaphore()
        for dz in range(1, self.zs):
            pl.semaphore_signal(barrier, inc=1, device_id=(self.over(dz), self.f), device_id_type=MESH)
        for j in range(self.bits + 1):
            pl.semaphore_signal(barrier, inc=1, device_id=(self.z, self.flip([j])), device_id_type=MESH)
        pl.semaphore_wait(barrier, self.zs + self.bits)


def subsets(js):
    found = [()]
    for j in js:
        found = found + [s + (j,) for s in found]
    return found


class Gather:
    def __init__(self, site, own, whole, local_sem, send_sem, recv_sem):
        self.site, self.own, self.whole = site, own, whole
        self.local_sem, self.send_sem, self.recv_sem = local_sem, send_sem, recv_sem
        self.along = len(own.shape) == 2
        self.skipped = 0 if self.along else 1
        self.stages = site.bits + 3 - self.skipped

    @staticmethod
    def slots(zs, n):
        return zs + 4 * (n // 2 - 1)

    def moves(self, piece):
        s = self.site
        start = piece * PIECE
        whole = pl.ds(pl.multiple_of(start, 128), PIECE)
        halves = (
            pl.ds(pl.multiple_of(start, 128), HALF),
            pl.ds(pl.multiple_of(start + HALF, 128), HALF),
        )
        slot = 0
        plan = [[] for _ in range(s.bits + 3)]
        for dz in range(1, s.zs):
            if not self.along:
                slot += 1
                continue
            plan[0].append(
                (slot, self.own.at[:, whole], self.whole.at[s.z, s.f, :, whole],
                 (s.over(dz), s.f), self.whole.at[s.over(s.zs - dz), s.f, :, whole])
            )
            slot += 1
        sibling = s.flip([0])

        def known(js, cols):
            if not js and not self.along:
                return self.own.at[:, :, cols]
            return self.whole.at[:, s.flip(js), :, cols]

        def shared(js, cols):
            return (slot, known(js, cols), self.whole.at[:, s.flip(js), :, cols],
                    (s.z, sibling), self.whole.at[:, s.flip(list(js) + [0]), :, cols])

        plan[1].append(shared([], whole))
        slot += 1
        up = list(range(1, s.bits + 1))
        for half, order in enumerate((up, up[::-1])):
            cols = halves[half]
            for at, j in enumerate(order):
                for js in subsets(order[:at]):
                    js = list(js)
                    plan[at + 1].append(
                        (slot, known(js, cols), self.whole.at[:, s.flip(js), :, cols],
                         (s.z, s.flip([j])), self.whole.at[:, s.flip(js + [j]), :, cols])
                    )
                    slot += 1
                    plan[at + 2].append(shared(js + [j], cols))
                    slot += 1
        return plan[self.skipped :]

    def leaving(self, piece, moves):
        return [
            pltpu.make_async_remote_copy(
                src_ref=src, dst_ref=dst, send_sem=self.send_sem.at[piece, slot],
                recv_sem=self.recv_sem.at[piece, slot], device_id=device, device_id_type=MESH,
            )
            for slot, src, dst, device, _ in moves
        ]

    def arriving(self, piece, moves):
        return [
            pltpu.make_async_remote_copy(
                src_ref=src, dst_ref=incoming, send_sem=self.send_sem.at[piece, slot],
                recv_sem=self.recv_sem.at[piece, slot], device_id=device, device_id_type=MESH,
            )
            for slot, src, _, device, incoming in moves
        ]

    def run(self, stage, piece):
        s = self.site
        plan = self.moves(piece)
        cols = pl.ds(pl.multiple_of(piece * PIECE, 128), PIECE)

        def local():
            if self.along:
                src, dst = self.own.at[:, cols], self.whole.at[s.z, s.f, :, cols]
            else:
                src, dst = self.own.at[:, :, cols], self.whole.at[:, s.f, :, cols]
            return pltpu.make_async_copy(src, dst, self.local_sem.at[piece])

        to_core = [[m for m in moves if self.is_core(stage_at, m)] for stage_at, moves in enumerate(plan)]
        others = [[m for m in moves if not self.is_core(stage_at, m)] for stage_at, moves in enumerate(plan)]
        if stage == 0:
            local().start()
        if stage == 1:
            local().wait()
        if 0 < stage:
            for copy in self.arriving(piece, others[stage - 1]):
                copy.wait_recv()
        if stage < self.stages - 1:
            for copy in self.leaving(piece, others[stage] + to_core[stage]):
                copy.start()
        else:
            for moves in to_core:
                for copy in self.arriving(piece, moves):
                    copy.wait_recv()
            for moves in plan:
                for copy in self.leaving(piece, moves):
                    copy.wait_send()

    def is_core(self, stage, move):
        slot = move[0]
        zs = self.site.zs
        if slot < zs - 1:
            return False
        return (slot - (zs - 1)) % 2 == 0


def at_stages(stages, pieces, lag, step, run):
    for stage in reversed(range(stages)):
        piece = step - lag * stage

        @pl.when(jnp.logical_and(piece >= 0, piece < pieces))
        def _(stage=stage, piece=piece):
            run(stage, piece)


def stages_of(n):
    return (n // 2).bit_length() + 2


def along_line(step, start, site, own, line, local_sem, send_sem, recv_sem):
    local = functools.partial(pltpu.make_async_copy, own, line.at[site.z], local_sem)

    def passing(hop, way):
        z = site.z - way * hop
        return pltpu.make_async_remote_copy(
            src_ref=own if hop == 0 else line.at[z], dst_ref=line.at[z],
            send_sem=send_sem.at[hop, (1 - way) // 2], recv_sem=recv_sem.at[hop, (1 - way) // 2],
            device_id=(site.z + way, site.f), device_id_type=MESH,
        )

    def arriving(hop, way):
        z = site.z - way * (hop + 1)
        return pltpu.make_async_remote_copy(
            src_ref=own, dst_ref=line.at[z],
            send_sem=send_sem.at[hop, (1 - way) // 2], recv_sem=recv_sem.at[hop, (1 - way) // 2],
            device_id=(site.z - way, site.f), device_id_type=MESH,
        )

    def inside(z):
        return jnp.logical_and(z >= 0, z < site.zs)

    for hop in range(site.zs):

        @pl.when(step == start + LAG * hop)
        def _(hop=hop):
            if hop == 0:
                local().start()
            else:
                for way in (1, -1):

                    @pl.when(inside(site.z - way * hop))
                    def _(way=way):
                        arriving(hop - 1, way).wait_recv()

            if hop < site.zs - 1:
                for way in (1, -1):

                    @pl.when(jnp.logical_and(inside(site.z - way * hop), inside(site.z + way)))
                    def _(way=way):
                        passing(hop, way).start()

            else:
                local().wait()
                for early in range(site.zs - 1):
                    for way in (1, -1):

                        @pl.when(jnp.logical_and(inside(site.z - way * early), inside(site.z + way)))
                        def _(way=way, early=early):
                            passing(early, way).wait_send()


def gather_kernel(pieces, start, own, late, last, whole, line, before, *refs):
    step = pl.program_id(0)
    site = Site()

    @pl.when(step == 0)
    def _():
        site.greet()

    edge_send, edge_recv = refs[3:5]

    def edge():
        return pltpu.make_async_remote_copy(
            src_ref=last, dst_ref=before, send_sem=edge_send, recv_sem=edge_recv,
            device_id=(site.over(1), site.f), device_id_type=MESH,
        )

    @pl.when(step == 0)
    def _():
        edge().start()

    gather = Gather(site, own, whole, *refs[:3])
    at_stages(gather.stages, pieces, LAG, step, gather.run)
    along_line(step, start, site, late, line, *refs[5:])

    @pl.when(step == pl.num_programs(0) - 1)
    def _():
        edge().wait()


def gather_scratch(pieces):
    slots = Gather.slots(lax.axis_size("seq"), lax.axis_size("fsdp"))
    return [
        pltpu.SemaphoreType.DMA((pieces,)),
        pltpu.SemaphoreType.DMA((pieces, slots)),
        pltpu.SemaphoreType.DMA((pieces, slots)),
    ]


def gathered(own, late, last, collective_id):
    rows, columns = own.shape
    zs, n = lax.axis_size("seq"), lax.axis_size("fsdp")
    pieces = columns // PIECE
    steps = max(pieces + LAG * (stages_of(n) - 1), LAG * zs)
    start = min(pieces // 2, steps - LAG * (zs - 1) - 1)
    anywhere = pl.BlockSpec(memory_space=pl.ANY)
    dma = pltpu.SemaphoreType.DMA
    return pl.pallas_call(
        functools.partial(gather_kernel, pieces, start),
        grid=(steps,),
        in_specs=[anywhere] * 3,
        out_specs=[anywhere] * 3,
        out_shape=[
            jax.ShapeDtypeStruct((zs, n, rows, columns), own.dtype),
            jax.ShapeDtypeStruct((zs,) + late.shape, late.dtype),
            jax.ShapeDtypeStruct(last.shape, last.dtype),
        ],
        scratch_shapes=gather_scratch(pieces) + [dma, dma, dma, dma((zs - 1, 2)), dma((zs - 1, 2))],
        compiler_params=pltpu.CompilerParams(collective_id=collective_id, has_side_effects=True),
        cost_estimate=pl.CostEstimate(
            flops=0, bytes_accessed=2 * zs * n * rows * columns, transcendentals=0
        ),
        name="gather_rows",
    )(own, late, last)


class Scatter:
    def take(self, refs):
        bits = self.site.bits
        self.kept = refs[:bits]
        self.sent = refs[bits : 2 * bits]
        self.got = refs[2 * bits : 3 * bits]
        self.z_kept, self.z_sent, self.z_got, self.send_sem, self.recv_sem = refs[3 * bits :]
        self.stages = bits + 3

    @staticmethod
    def common(pieces, rows):
        zs, n = lax.axis_size("seq"), lax.axis_size("fsdp")
        chips = n // 2
        bits = chips.bit_length() - 1
        slots = 1 + 2 * bits + zs - 1
        steps = [(pieces, 2, zs, chips >> (k + 1), rows, HALF) for k in range(bits)]
        return (
            [pltpu.VMEM(s, F32) for s in steps]
            + [pltpu.VMEM(s, BF16) for s in steps]
            + [pltpu.VMEM(s, BF16) for s in steps]
            + [
                pltpu.VMEM((pieces, rows, PIECE), F32),
                pltpu.VMEM((pieces, zs, rows, PIECE), BF16),
                pltpu.VMEM((pieces, zs - 1, rows, PIECE), BF16),
                pltpu.SemaphoreType.DMA((pieces, slots)),
                pltpu.SemaphoreType.DMA((pieces, slots)),
            ]
        )

    def remote(self, piece, slot, src, dst, device):
        at = self.at(piece)
        return pltpu.make_async_remote_copy(
            src_ref=src, dst_ref=dst, send_sem=self.send_sem.at[at, slot],
            recv_sem=self.recv_sem.at[at, slot], device_id=device, device_id_type=MESH,
        )

    def order(self, half):
        up = list(range(1, self.site.bits + 1))
        return up[::-1] if half == 0 else up

    def across(self, piece, k, half):
        s, at = self.site, self.at(piece)
        return self.remote(
            piece, 1 + 2 * k + half, self.sent[k].at[at, half], self.got[k].at[at, half],
            (s.z, s.flip([self.order(half)[k]])),
        )

    def along(self, piece, dz):
        s, at = self.site, self.at(piece)
        return self.remote(
            piece, 2 * s.bits + dz, self.z_sent.at[at, s.over(dz)], self.z_got.at[at, dz - 1],
            (s.over(dz), s.f),
        )

    def run(self, stage, piece):
        s, at = self.site, self.at(piece)
        bits = s.bits
        if stage == 0:
            self.begin(piece)
            self.to_core(piece).start()
            return
        if stage == 1:
            self.join(piece)
            self.to_core(piece).wait()
        elif stage <= bits + 1:
            for half in range(2):
                self.across(piece, stage - 2, half).wait()
        if stage <= bits:
            k = stage - 1
            for half in range(2):
                order = self.order(half)
                left = sorted(order[k:])
                j = order[k]
                place = left.index(j)
                mine = s.bit(j)

                def one(zi, carry, half=half, k=k, place=place, mine=mine):
                    for i in range(s.chips >> (k + 1)):
                        low = i % 2**place
                        base = (i - low) * 2 + low
                        self.sent[k][at, half, zi, i] = self.current(
                            k, piece, half, zi, base + (1 - mine) * 2**place
                        ).astype(BF16)
                        self.kept[k][at, half, zi, i] = self.current(
                            k, piece, half, zi, base + mine * 2**place
                        )
                    return carry

                lax.fori_loop(0, s.zs, one, 0)
                self.across(piece, k, half).start()
        elif stage == bits + 1:
            for half in range(2):
                lanes = slice(half * HALF, (half + 1) * HALF)

                def one(zi, carry, half=half, lanes=lanes):
                    self.z_sent[at, zi, :, lanes] = self.current(bits, piece, half, zi, 0).astype(BF16)
                    return carry

                lax.fori_loop(0, s.zs, one, 0)
                self.z_kept[at, :, lanes] = self.current(bits, piece, half, s.z, 0)
            for dz in range(1, s.zs):
                self.along(piece, dz).start()
        else:
            total = self.z_kept[at]
            for dz in range(1, s.zs):
                self.along(piece, dz).wait()
                total = total + self.z_got[at, dz - 1].astype(F32)
            self.out[:, pl.ds(pl.multiple_of(self.column(piece) * PIECE, 128), PIECE)] = total

    def current(self, k, piece, half, zi, index):
        at = self.at(piece)
        lanes = slice(half * HALF, (half + 1) * HALF)
        if k == 0:
            return self.first(piece, zi, index, lanes) + self.came[at, zi, index, :, lanes].astype(F32)
        return self.kept[k - 1][at, half, zi, index] + self.got[k - 1][at, half, zi, index].astype(F32)


RING = 4
XRING = 6


class Streamed(Scatter):
    def __init__(self, site, turned, kind, x, out, column, refs):
        self.site, self.turned, self.x, self.out = site, turned, x, out
        self.kind, self.column = kind, column
        self.ring, self.x_ring = refs[0].shape[0], x.shape[0]
        self.away, self.own, self.came = refs[:3]
        self.take(refs[3:])

    @staticmethod
    def scratch(rows, ring=RING):
        zs, n = lax.axis_size("seq"), lax.axis_size("fsdp")
        full = (zs, n // 2, rows, PIECE)
        return [
            pltpu.VMEM((ring,) + full, BF16),
            pltpu.VMEM(full, F32),
            pltpu.VMEM((ring,) + full, BF16),
        ] + Scatter.common(ring, rows)

    def at(self, piece):
        return piece % self.ring

    def to_core(self, piece):
        s, at = self.site, self.at(piece)
        return self.remote(piece, 0, self.away.at[at], self.came.at[at], (s.z, s.flip([0])))

    def product(self, core, piece, store):
        s = self.site
        rows = self.away.shape[3]
        together = 2 - s.zs % 2
        count = together * s.chips * rows

        def one(i, carry):
            lhs = self.turned[self.kind(piece), core, pl.ds(pl.multiple_of(i * count, 16), count), :]
            value = dot(lhs, self.x[piece % self.x_ring]).reshape(together, s.chips, rows, PIECE)
            store(pl.ds(i * together, together), value)
            return carry

        lax.fori_loop(0, s.zs // together, one, 0)

    def begin(self, piece):
        at = self.at(piece)

        def store(zi, value):
            self.away[at, zi] = value.astype(BF16)

        self.product(1 - self.site.bit(0), piece, store)

    def join(self, piece):
        def store(zi, value):
            self.own[zi] = value

        self.product(self.site.bit(0), piece, store)

    def first(self, piece, zi, index, lanes):
        return self.own[zi, index, :, lanes]


def exchange_count(zs, n):
    return (n.bit_length() - 1) + (zs.bit_length() - 1)


class Totals:
    def __init__(self, site, sent, got, send_sem, recv_sem):
        self.site, self.sent, self.got = site, sent, got
        self.send_sem, self.recv_sem = send_sem, recv_sem
        self.count = exchange_count(site.zs, site.n)

    def move(self, t):
        s = self.site
        if t <= s.bits:
            device = (s.z, s.flip([t]))
        else:
            j = t - s.bits - 1
            device = (s.z + (1 - 2 * ((s.z // 2**j) % 2)) * 2**j, s.f)
        return pltpu.make_async_remote_copy(
            src_ref=self.sent.at[t % 2], dst_ref=self.got.at[t], send_sem=self.send_sem.at[t],
            recv_sem=self.recv_sem.at[t], device_id=device, device_id_type=MESH,
        )

    def start(self, t):
        if t < self.count:
            self.move(t).start()

    def next(self, t):
        if t < self.count:
            self.move(t).wait()
            self.sent[(t + 1) % 2] = self.sent[t % 2] + self.got[t]
            self.start(t + 1)


CONV_COLS = 3584


def local(
    tokens, pre_gain, in_weight, conv_weight, conv_bias, step_bias, decay_log, skip_gain,
    norm_gain, out_weight, cotangent,
):
    both = ("seq", "fsdp")
    _, positions, features = tokens.shape
    blocks = positions // BLOCK_LEN
    devices = lax.axis_size("seq") * lax.axis_size("fsdp")

    rows = in_weight.shape[0]
    padded_rows = -(-rows // 16) * 16
    vectors = jnp.concatenate([pre_gain, conv_weight.reshape(-1), conv_bias, norm_gain])
    extra = -(-vectors.size // rows)
    sizes = (pre_gain.size, conv_weight.size, conv_bias.size, norm_gain.size)
    cuts = [sum(sizes[:i]) for i in range(5)]
    used = PROJ - INNER
    more_rows = ((0, padded_rows - rows), (0, 0))
    own = jnp.concatenate(
        [
            in_weight[:, INNER:],
            jnp.pad(vectors, (0, extra * rows - vectors.size)).reshape(rows, extra),
            jnp.zeros((rows, CONV_COLS - used - extra), BF16),
        ],
        axis=1,
    )
    inw_conv, gate_line, before = gathered(
        jnp.pad(own, more_rows),
        jnp.pad(in_weight[:, :INNER], more_rows),
        tokens[0, positions - EDGE :],
        1,
    )
    later, before = lax.optimization_barrier((out_weight, before))
    outw_full = lax.all_gather(later, both, axis=0, tiled=True)
    inw_conv = inw_conv[:, :, :rows].reshape(features, CONV_COLS)
    small_full = inw_conv[:, used : used + extra].reshape(devices, rows * extra)
    gain_full = small_full[:, : cuts[1]].reshape(1, features).astype(F32)
    convw_full = (
        small_full[:, cuts[1] : cuts[2]]
        .reshape(devices, CONV, -1)
        .transpose(1, 0, 2)
        .reshape(CONV, CHANNELS)
        .astype(F32)
    )
    convb_full = small_full[:, cuts[2] : cuts[3]].reshape(1, CHANNELS).astype(F32)
    normg_full = small_full[:, cuts[3] : cuts[4]].reshape(1, INNER).astype(F32)

    before = jnp.where(lax.axis_index("seq") == 0, jnp.zeros_like(before), before)
    ext = jnp.concatenate([before, tokens[0]], axis=0).astype(F32)
    r0_ext = lax.rsqrt(jnp.mean(ext * ext, axis=-1, keepdims=True) + 1e-05)
    normed_ext = (ext * r0_ext * gain_full).astype(BF16)
    inputs, r0, normed = ext[EDGE:], r0_ext[EDGE:], normed_ext[EDGE:]

    p = dot(normed_ext, inw_conv)
    unused = ((0, 0), (0, CONV_COLS - CHANNELS))
    w = jnp.pad(convw_full, ((0, 8 - CONV), (0, CONV_COLS - CHANNELS)))
    b = jnp.pad(convb_full, unused)
    wide_heads = ((0, 0), (0, 128 - HEADS))
    bias, decay_row = jnp.pad(step_bias[None], wide_heads), jnp.pad(decay_log[None], wide_heads)
    cols, run_rows, maps, run_exp, decays = steps_of(
        p, w, b, bias, decay_row, positions
    )
    skip = jnp.repeat(skip_gain, HEAD_DIM)[None]
    y, starts, inw_gate = scan_forward(
        decays, p, w, b, cols, run_rows, maps, skip, gate_line, positions, 2
    )
    inw_gate = inw_gate[:, :, :rows].reshape(features, INNER)
    gate = dot(normed, inw_gate)
    cot = cotangent[0]
    grad_normed_out = dot(cot, outw_full, NT)
    normed_out, dy, dye, grad_gate, ends = gated(
        y, gate, grad_normed_out, normg_full, run_exp, maps
    )
    mixed = (inputs + dot(normed_out, outw_full)).astype(BF16)[None]

    def turned(x, split):
        x = jnp.pad(x.T.reshape(-1, 2, split, rows, positions), ((0, 0),) * 3 + more_rows)
        return x.transpose(2, 1, 0, 3, 4).reshape(split, 2, -1, positions)

    turned_all = jnp.concatenate([turned(normed, 1), turned(normed_out, OUT_SPLIT)])
    own_main, grad_tokens, totals = scan_backward(
        decays, p, w, b, cols, run_rows, maps, skip, y, dy, dye, starts, ends, turned_all, cot, grad_gate,
        inw_gate, inw_conv, bias, decay_row, tokens[0], gain_full, padded_rows, 3,
    )
    own_main = own_main[:rows]
    out_cols = OUT_PIECES * PIECE
    own_out = own_main[:, :out_cols].reshape(rows, OUT_SPLIT, features).transpose(1, 0, 2)
    own_out = own_out.reshape(OUT_SPLIT * rows, features)
    own_in = own_main[:, out_cols : out_cols + PROJ]
    per_tap = conv_weight.shape[1]
    me = lax.axis_index("seq") * lax.axis_size("fsdp") + lax.axis_index("fsdp")
    own_taps = lax.dynamic_slice_in_dim(totals, me * per_tap, per_tap, axis=1)
    heads = totals[:3, CHANNELS : CHANNELS + HEADS]

    return (
        mixed,
        grad_tokens[None],
        jnp.sum(own_in * in_weight.astype(F32), axis=1) / pre_gain.astype(F32),
        own_in,
        own_taps[:CONV],
        own_taps[CONV],
        heads[0],
        heads[1],
        heads[2],
        jnp.sum(own_out * out_weight.astype(F32), axis=1) / norm_gain.astype(F32),
        own_out,
    )


def solution(mesh):
    split = P(("seq", "fsdp"), None)
    flat = P(("seq", "fsdp"))
    taps = P(None, ("seq", "fsdp"))
    data = P("fsdp", "seq", None)
    return jax.shard_map(
        local,
        mesh=mesh,
        in_specs=(data, flat, split, taps, flat, P(), P(), P(), flat, split, data),
        out_specs=(data, data, flat, split, taps, flat, P(), P(), P(), flat, split),
        check_vma=False,
    )
```

```python
import functools
import math
import jax
import jax.numpy as jnp
from jax import lax
from jax.experimental import pallas as pl
from jax.experimental.pallas import tpu as pltpu
from jax.sharding import PartitionSpec as P

INNER = 3072
HEADS = 48
HEAD_DIM = 64
STATE = 128
CONV = 4
BLOCK_LEN = 256
CHANNELS = 3328
PROJ = 6448
EDGE = 16
GROUP = 4
GROUPS = HEADS // GROUP
GCOLS = GROUP * HEAD_DIM
PAIRS = GROUP // 2
STRIP = 128
PART = 64
LOG2E = 1.4426950408889634
F32 = jnp.float32
BF16 = jnp.bfloat16

NT = (((1,), (1,)), ((), ()))
TN = (((0,), (0,)), ((), ()))
NN = (((1,), (0,)), ((), ()))


def dot(a, b, dims=NN):
    return lax.dot_general(a, b, dims, preferred_element_type=F32)


def first_half(shape):
    return lax.broadcasted_iota(jnp.int32, shape, len(shape) - 1) < HEAD_DIM


def per_pair(cols, kind, pair, rows):
    at = kind * GROUP + 2 * pair
    left, right = cols[rows, at : at + 1], cols[rows, at + 1 : at + 2]
    shape = (left.shape[0], 2 * HEAD_DIM)
    return jnp.where(
        first_half(shape), jnp.broadcast_to(left, shape), jnp.broadcast_to(right, shape)
    )


def convolved(p_ref, w_ref, b_ref, lo, count, lanes):
    out = b_ref[0:1, lanes] + jnp.zeros((count, lanes.size), F32)
    for tap in range(CONV):
        at = EDGE - CONV + 1 + tap + lo
        out = out + p_ref[at : at + count, lanes] * w_ref[tap : tap + 1, lanes]
    return out


def sigmoid(v):
    return 0.5 + 0.5 * jnp.tanh(0.5 * v)


def softplus(v):
    return jnp.maximum(v, 0.0) + jnp.log1p(jnp.exp(-jnp.abs(v)))


def lower_triangle():
    row = lax.broadcasted_iota(jnp.int32, (BLOCK_LEN, BLOCK_LEN), 0)
    col = lax.broadcasted_iota(jnp.int32, (BLOCK_LEN, BLOCK_LEN), 1)
    return jnp.where(row >= col, 1.0, 0.0)


def exact_dot(a, b, dims=NN):
    return lax.dot_general(
        a, b, dims, precision=lax.Precision.HIGHEST, preferred_element_type=F32
    )


def steps_kernel(
    p_ref, w_ref, b_ref, bias_ref, decay_ref, cols_ref, rows_ref, maps_ref, er_ref, decays_ref
):
    positions = maps_ref.shape[0]
    blocks = positions // BLOCK_LEN
    lower = lower_triangle()
    used = lax.broadcasted_iota(jnp.int32, (1, 128), 1) < HEADS
    rate = -jnp.exp(decay_ref[...])
    total = jnp.zeros((1, 128), F32)
    for block in range(blocks):
        lo = block * BLOCK_LEN
        rows = slice(lo, lo + BLOCK_LEN)
        conv = convolved(p_ref, w_ref, b_ref, lo, BLOCK_LEN, pl.ds(0, 2 * STATE))
        maps_ref[rows, :] = (conv * sigmoid(conv)).astype(BF16)
        step = softplus(p_ref[EDGE + lo : EDGE + lo + BLOCK_LEN, 2 * STATE : 2 * STATE + 128] + bias_ref[...])
        step = jnp.where(used, step, 0.0)
        run = exact_dot(lower, rate * step)
        end = run[BLOCK_LEN - 1 :]
        total = total + end
        run2 = run * LOG2E
        grown = jnp.exp(run)
        er_ref[rows, :] = grown
        decays_ref[block : block + 1, :] = jnp.exp(end)
        turned = run2.T
        kinds = (step, run2, grown, jnp.exp(end - run))
        for group in range(GROUPS):
            heads = slice(group * GROUP, (group + 1) * GROUP)
            rows_ref[group, :, rows] = turned[heads]
            cols_ref[group, rows, :] = jnp.concatenate([kind[:, heads] for kind in kinds], axis=1)
    decays_ref[blocks : blocks + 1, :] = jnp.exp(total)
    decays_ref[blocks + 1 :, :] = jnp.zeros((8 - blocks - 1, 128), F32)


def steps_of(p, w, b, bias, decay_log, positions):
    ext = p.shape[0]
    at = INNER // PIECE
    return pl.pallas_call(
        steps_kernel,
        grid=(1,),
        in_specs=[
            pl.BlockSpec((ext, PIECE), lambda i: (0, at)),
            pl.BlockSpec((8, PIECE), lambda i: (0, at)),
            pl.BlockSpec((1, PIECE), lambda i: (0, at)),
            pl.BlockSpec((1, 128), lambda i: (0, 0)),
            pl.BlockSpec((1, 128), lambda i: (0, 0)),
        ],
        out_specs=[pl.BlockSpec(memory_space=pltpu.VMEM)] * 5,
        out_shape=[
            jax.ShapeDtypeStruct((GROUPS, positions, 4 * GROUP), F32),
            jax.ShapeDtypeStruct((GROUPS, GROUP, positions), F32),
            jax.ShapeDtypeStruct((positions, 2 * STATE), BF16),
            jax.ShapeDtypeStruct((positions, 128), F32),
            jax.ShapeDtypeStruct((8, 128), F32),
        ],
        compiler_params=pltpu.CompilerParams(vmem_limit_bytes=48 * 2**20),
        cost_estimate=pl.CostEstimate(
            flops=4 * positions * BLOCK_LEN * 128, bytes_accessed=16 * positions * 512,
            transcendentals=positions * 1024,
        ),
        name="steps",
    )(p, w, b, bias, decay_log)


def masked_scores(maps_ref, scores_ref, blocks):
    row = lax.broadcasted_iota(jnp.int32, (BLOCK_LEN, BLOCK_LEN), 0)
    col = lax.broadcasted_iota(jnp.int32, (BLOCK_LEN, BLOCK_LEN), 1)
    for block in range(blocks):
        rows = slice(block * BLOCK_LEN, (block + 1) * BLOCK_LEN)
        scores = dot(maps_ref[rows, STATE:], maps_ref[rows, :STATE], NT)
        scores_ref[block] = jnp.where(row >= col, scores, 0.0)


def chain_copy(site, group, by, sent, got, send_sem, recv_sem):
    return pltpu.make_async_remote_copy(
        src_ref=sent.at[group % sent.shape[0]], dst_ref=got.at[group], send_sem=send_sem.at[group],
        recv_sem=recv_sem.at[group], device_id=(site.over(by), site.f), device_id_type=MESH,
    )


def by_head(decays, group, kind, rows=GCOLS):
    return jnp.concatenate(
        [
            jnp.full((HEAD_DIM, STATE), decays[kind, group * GROUP + head], F32)
            for head in range(rows // HEAD_DIM)
        ],
        axis=0,
    )


def scan_forward_kernel(
    pieces, decays, p_ref, w_ref, b_ref, cols_ref, late_ref, rows_ref, maps_ref, skip_ref, normed_ref, own,
    y_ref, starts_ref, gate_ref, turned_ref, whole,
    scores_ref, x_ref, states_ref, weight_ref, weight_sem, sent, got, chain_send, chain_recv, *gather_refs,
):
    positions = y_ref.shape[0]
    blocks = positions // BLOCK_LEN
    step = pl.program_id(0)
    site = Site()
    behind = site.zs - 1

    @pl.when(step == 0)
    def _():
        site.greet()
        masked_scores(maps_ref, scores_ref, blocks)

    @pl.when(step == 1)
    def _():
        put_turned(normed_ref, own.shape[1], lambda at: turned_ref.at[at % 2, span_of(at // 2, own.shape[1])])

    gather = Gather(site, own, whole, *gather_refs)
    arrived = step - LAG * (gather.stages - 1)

    def weight_copy(piece):
        cols = pl.ds(pl.multiple_of(piece * PIECE, 128), PIECE)
        return pltpu.make_async_copy(whole.at[:, :, :, cols], weight_ref, weight_sem)

    @pl.when(jnp.logical_and(arrived >= 1, arrived <= pieces))
    def _():
        weight_copy(arrived - 1).wait()
        gate_ref[...] = dot(normed_ref[...], weight_ref[...].reshape(-1, PIECE))

    at_stages(gather.stages, pieces, LAG, step, gather.run)

    @pl.when(jnp.logical_and(arrived >= 0, arrived < pieces))
    def _():
        weight_copy(arrived).start()

    @pl.when(step < GROUPS)
    def _():
        slot = step % site.zs
        for pair in range(PAIRS):
            lanes = pl.ds(pair * 2 * HEAD_DIM, 2 * HEAD_DIM)
            for block in range(blocks):
                lo = block * BLOCK_LEN
                rows = slice(lo, lo + BLOCK_LEN)
                conv = convolved(p_ref, w_ref, b_ref, lo, BLOCK_LEN, lanes)
                x = conv * sigmoid(conv)
                x_ref[slot, rows, lanes] = x
                xs = x * per_pair(cols_ref, 0, pair, rows)
                ended = (xs * per_pair(cols_ref, 3, pair, rows)).astype(BF16)
                states_ref[slot, block, pair * 2 * HEAD_DIM : (pair + 1) * 2 * HEAD_DIM, :] = dot(
                    ended, maps_ref[rows, :STATE], TN
                )

    linked = step - site.z

    @pl.when(jnp.logical_and(linked >= 0, linked < GROUPS))
    def _():
        slot = linked % site.zs

        @pl.when(site.z == 0)
        def _():
            got[linked] = jnp.zeros((GCOLS, STATE), BF16)

        @pl.when(site.z > 0)
        def _():
            chain_copy(site, linked, 1, sent, got, chain_send, chain_recv).wait_recv()

        @pl.when(site.z < behind)
        def _():
            final = states_ref[slot, 0]
            for block in range(1, blocks):
                final = by_head(decays, linked, block) * final + states_ref[slot, block]
            sent[linked % sent.shape[0]] = (
                by_head(decays, linked, blocks) * got[linked].astype(F32) + final
            ).astype(BF16)
            chain_copy(site, linked, 1, sent, got, chain_send, chain_recv).start()

    group = step - behind

    @pl.when(jnp.logical_and(group >= 0, group < GROUPS))
    def _():
        slot = group % site.zs
        start = got[group].astype(F32)
        for block in range(blocks):
            if block:
                start = by_head(decays, group, block - 1) * start + states_ref[slot, block - 1]
            starts_ref[block] = start.astype(BF16)
        half = first_half((BLOCK_LEN, 2 * HEAD_DIM))
        for pair in range(PAIRS):
            lanes = pl.ds(pair * 2 * HEAD_DIM, 2 * HEAD_DIM)
            span = slice(pair * 2 * HEAD_DIM, (pair + 1) * 2 * HEAD_DIM)
            for block in range(blocks):
                lo = block * BLOCK_LEN
                rows = slice(lo, lo + BLOCK_LEN)
                x = x_ref[slot, rows, lanes]
                low = (x * per_pair(late_ref, 0, pair, rows)).astype(BF16)
                none = jnp.zeros_like(low)
                one, two = jnp.where(half, low, none), jnp.where(half, none, low)
                rest = skip_ref[0:1, lanes] * x + dot(
                    maps_ref[rows, STATE:], starts_ref[block, span, :], NT
                ) * per_pair(late_ref, 2, pair, rows)
                for strip in range(BLOCK_LEN // STRIP):
                    top = strip * STRIP
                    lim = top + STRIP
                    pieces_ = []
                    for side in range(2):
                        head = 2 * pair + side
                        at = GROUP + head
                        gap = (
                            late_ref[lo + top : lo + lim, at : at + 1]
                            - rows_ref[head : head + 1, lo : lo + lim]
                        )
                        decay = jnp.exp2(jnp.minimum(gap, 0.0))
                        pieces_.append((scores_ref[block, top:lim, :lim] * decay).astype(BF16))
                    y = dot(pieces_[0], one[:lim]) + dot(pieces_[1], two[:lim])
                    y_ref[lo + top : lo + lim, lanes] = y + rest[top:lim]

        @pl.when(site.z < behind)
        def _():
            chain_copy(site, group, 1, sent, got, chain_send, chain_recv).wait_send()


def span_of(at, rows):
    return slice(at * rows, (at + 1) * rows)


def put_turned(x_ref, rows, place, lanes=slice(None)):
    together = rows * 128 // math.gcd(rows, 128)
    for at in range(x_ref.shape[1] // together):
        turned = x_ref[:, span_of(at, together)].astype(F32).T
        for index in range(together // rows):
            place(at * (together // rows) + index)[:, lanes] = turned[span_of(index, rows)].astype(BF16)


def chain_scratch():
    ring = max(lax.axis_size("seq"), LAG + 2)
    return [
        pltpu.VMEM((ring, GCOLS, STATE), BF16),
        pltpu.VMEM((GROUPS, GCOLS, STATE), BF16),
        pltpu.SemaphoreType.DMA((GROUPS,)),
        pltpu.SemaphoreType.DMA((GROUPS,)),
    ]


def scan_forward(decays, p, w, b, cols, rows, maps, skip, normed, own, positions, collective_id):
    blocks = positions // BLOCK_LEN
    ext = p.shape[0]
    zs, n = lax.axis_size("seq"), lax.axis_size("fsdp")
    rows_there, columns = own.shape[1:]
    pieces = columns // PIECE
    wait = LAG * (stages_of(n) - 2) + 1
    steps = max(GROUPS + zs - 1, pieces + wait)

    def early(s):
        return jnp.minimum(s, GROUPS - 1)

    def late(s):
        return jnp.clip(s - (zs - 1), 0, GROUPS - 1)

    anywhere = pl.BlockSpec(memory_space=pl.ANY)
    return pl.pallas_call(
        functools.partial(scan_forward_kernel, pieces),
        grid=(steps,),
        in_specs=[
            pl.BlockSpec(memory_space=pltpu.SMEM),
            pl.BlockSpec((ext, GCOLS), lambda s: (0, early(s))),
            pl.BlockSpec((8, GCOLS), lambda s: (0, early(s))),
            pl.BlockSpec((1, GCOLS), lambda s: (0, early(s))),
            pl.BlockSpec((None, positions, 4 * GROUP), lambda s: (early(s), 0, 0)),
            pl.BlockSpec((None, positions, 4 * GROUP), lambda s: (late(s), 0, 0)),
            pl.BlockSpec((None, GROUP, positions), lambda s: (late(s), 0, 0)),
            pl.BlockSpec((positions, 2 * STATE), lambda s: (0, 0)),
            pl.BlockSpec((1, GCOLS), lambda s: (0, late(s))),
            pl.BlockSpec(normed.shape, lambda s: (0, 0), pipeline_mode=pl.Buffered(1)),
            anywhere,
        ],
        out_specs=[
            pl.BlockSpec((positions, GCOLS), lambda s: (0, late(s))),
            pl.BlockSpec((blocks, GCOLS, STATE), lambda s: (0, late(s), 0)),
            pl.BlockSpec((positions, PIECE), lambda s: (0, jnp.clip(s - wait, 0, pieces - 1))),
            pl.BlockSpec(
                (2, zs * n // 2 * rows_there, positions), lambda s: (0, 0, 0), pipeline_mode=pl.Buffered(1)
            ),
            anywhere,
        ],
        out_shape=[
            jax.ShapeDtypeStruct((positions, INNER), F32),
            jax.ShapeDtypeStruct((blocks, INNER, STATE), BF16),
            jax.ShapeDtypeStruct((positions, columns), F32),
            jax.ShapeDtypeStruct((2, zs * n // 2 * rows_there, positions), BF16),
            jax.ShapeDtypeStruct((zs, n, rows_there, columns), BF16),
        ],
        scratch_shapes=[
            pltpu.VMEM((blocks, BLOCK_LEN, BLOCK_LEN), F32),
            pltpu.VMEM((zs, positions, GCOLS), F32),
            pltpu.VMEM((zs, blocks, GCOLS, STATE), F32),
            pltpu.VMEM((zs, n, rows_there, PIECE), BF16),
            pltpu.SemaphoreType.DMA,
        ]
        + chain_scratch()
        + gather_scratch(pieces),
        compiler_params=pltpu.CompilerParams(
            collective_id=collective_id, has_side_effects=True, vmem_limit_bytes=48 * 2**20
        ),
        cost_estimate=pl.CostEstimate(
            flops=12 * positions * INNER * BLOCK_LEN, bytes_accessed=24 * positions * INNER,
            transcendentals=HEADS * positions * BLOCK_LEN,
        ),
        name="scan_forward",
    )(decays, p, w, b, cols, cols, rows, maps, skip, normed, own)


def gate_kernel(
    y_ref, gate_ref, gno_ref, gain_ref, er_ref, maps_ref,
    out_ref, dy_ref, dye_ref, ggate_ref, ends_ref, *more_refs,
):
    gated_ref = more_refs[-1]
    rows = y_ref.shape[0]
    width = 2 * HEAD_DIM
    shape = (rows, width)
    square = jnp.zeros(shape, F32)
    cross = jnp.zeros(shape, F32)

    def decayed(pair):
        return jnp.where(
            first_half(shape),
            jnp.broadcast_to(er_ref[:, 2 * pair : 2 * pair + 1], shape),
            jnp.broadcast_to(er_ref[:, 2 * pair + 1 : 2 * pair + 2], shape),
        )

    for pair in range(HEADS // 2):
        lanes = slice(pair * width, (pair + 1) * width)
        gate = gate_ref[:, lanes]
        gated = y_ref[:, lanes] * gate * sigmoid(gate)
        gated_ref[:, lanes] = gated
        square = square + gated * gated
        cross = cross + gated * (gain_ref[:, lanes] * gno_ref[:, lanes])
    r1 = lax.rsqrt(jnp.sum(square, axis=-1, keepdims=True) * (1.0 / INNER) + 1e-05)
    back = r1 * r1 * r1 * (jnp.sum(cross, axis=-1, keepdims=True) * (1.0 / INNER))

    @pl.when(pl.program_id(0) % (BLOCK_LEN // rows) == 0)
    def _():
        ends_ref[...] = jnp.zeros_like(ends_ref)

    for pair in range(HEADS // 2):
        lanes = slice(pair * width, (pair + 1) * width)
        gate = gate_ref[:, lanes]
        sig = sigmoid(gate)
        gated = gated_ref[:, lanes]
        gain = gain_ref[:, lanes]
        out_ref[:, lanes] = (gated * r1 * gain).astype(BF16)
        ggated = gno_ref[:, lanes] * r1 * gain - gated * back
        low = (ggated * (gate * sig)).astype(BF16)
        dy_ref[:, lanes] = low
        ggate_ref[:, lanes] = (
            ggated * y_ref[:, lanes] * (sig * (1.0 + gate * (1.0 - sig)))
        ).astype(BF16)
        scaled = (low.astype(F32) * decayed(pair)).astype(BF16)
        dye_ref[:, lanes] = scaled
        ends_ref[lanes, :] += dot(scaled, maps_ref[:, STATE:], TN)

    if len(more_refs) == 2:
        turned_ref = more_refs[0]
        own_rows = INNER // (turned_ref.shape[0] * turned_ref.shape[1] * turned_ref.shape[2])

        def place(at):
            rest, split = at // OUT_SPLIT, at % OUT_SPLIT
            return turned_ref.at[split, rest % 2, rest // 2]

        put_turned(out_ref, own_rows, place)


def gated(y, gate, gno, gain, er, maps, own_rows):
    positions = y.shape[0]
    tile = 128
    per_block = BLOCK_LEN // tile
    wide = pl.BlockSpec((tile, INNER), lambda i: (i, 0))
    states = pl.BlockSpec((None, INNER, STATE), lambda i: (i // per_block, 0, 0))
    low = jax.ShapeDtypeStruct((positions, INNER), BF16)
    extra = []
    if own_rows:
        extra.append((OUT_SPLIT, 2, INNER // (2 * OUT_SPLIT * own_rows), own_rows, positions))
    return pl.pallas_call(
        gate_kernel,
        grid=(positions // tile,),
        in_specs=[
            wide,
            wide,
            wide,
            pl.BlockSpec((1, INNER), lambda i: (0, 0)),
            pl.BlockSpec((tile, 128), lambda i: (i, 0)),
            pl.BlockSpec((tile, 2 * STATE), lambda i: (i, 0)),
        ],
        out_specs=[wide] * 4
        + [states]
        + [pl.BlockSpec(turned[:-1] + (tile,), lambda i: (0, 0, 0, 0, i)) for turned in extra],
        out_shape=[
            low,
            low,
            low,
            low,
            jax.ShapeDtypeStruct((positions // BLOCK_LEN, INNER, STATE), F32),
        ]
        + [jax.ShapeDtypeStruct(turned, BF16) for turned in extra],
        scratch_shapes=[pltpu.VMEM((tile, INNER), F32)],
        compiler_params=pltpu.CompilerParams(vmem_limit_bytes=48 * 2**20),
        cost_estimate=pl.CostEstimate(
            flops=4 * positions * INNER * STATE, bytes_accessed=24 * positions * INNER,
            transcendentals=2 * positions * INNER,
        ),
        name="gate",
    )(y, gate, gno, gain, er, maps)


def scan_backward_kernel(
    decays, p_ref, w_ref, b_ref, cols_ref, rows_ref, maps_ref, skip_ref, y_ref, dy_ref,
    dye_ref, st_ref, grads_ref, turned_ref, turned_out_ref, cot_ref, ggate_ref, wgate_ref, wconv_ref,
    plast_ref, wlast_ref, blast_ref, bias_ref, decay_ref, grown_ref, tokens_ref, gain_ref,
    own_ref, gtokens_ref, total_ref,
    scores_ref, dscores_ref, dpad_ref, gacc_ref, dl_ref, x_ref, tail_ref, runs_ref, direct_ref, ends_ref,
    cross_ref, conv_ref, inner_ref, outer_ref, low_ref, ended_ref, sent, got, chain_send, chain_recv,
    edge_sent, edge_got, edge_send, edge_recv, t_sent, t_got, t_send, t_recv, *scatter_refs,
):
    step_at = pl.program_id(0)
    site = Site()
    behind = site.zs - 1
    positions = y_ref.shape[0]
    gates = INNER // PIECE
    ahead = PIECE // GCOLS
    later = step_at - OUT_PIECES

    @pl.when(step_at == 0)
    def _():
        site.greet()
        gtokens_ref[...] = jnp.zeros_like(gtokens_ref)
        runs_ref[...] = jnp.zeros_like(runs_ref)
        direct_ref[...] = jnp.zeros_like(direct_ref)
        t_sent[0, CONV + 1 :, 0:INNER] = jnp.zeros((8 - CONV - 1, INNER), F32)

    def edge_copy(group):
        return pltpu.make_async_remote_copy(
            src_ref=edge_sent.at[group], dst_ref=edge_got.at[group], send_sem=edge_send.at[group],
            recv_sem=edge_recv.at[group], device_id=(site.over(behind), site.f), device_id_type=MESH,
        )

    def add_normed(weight_ref, grads_of):
        def one(i, carry):
            span = pl.ds(pl.multiple_of(i * PIECE, 128), PIECE)
            gtokens_ref[:, span] += dot(grads_of(), weight_ref[span, :], NT)
            return carry

        lax.fori_loop(0, gtokens_ref.shape[1] // PIECE, one, 0)

    @pl.when(step_at < OUT_PIECES)
    def _():
        cots = cot_ref.shape[1] // PIECE
        span = pl.ds(pl.multiple_of((step_at % cots) * PIECE, 128), PIECE)
        x_ref[step_at % XRING] = cot_ref[:, span]

    inside = jnp.logical_and(later >= 0, later < 2 * gates)

    @pl.when(jnp.logical_and(inside, later % 2 == 1))
    def _():
        x_ref[step_at % XRING] = ggate_ref[...]

    @pl.when(jnp.logical_and(inside, later % 2 == 0))
    def _():
        for side in range(ahead):
            group = (later // 2) * ahead + side
            lanes = slice(side * GCOLS, (side + 1) * GCOLS)

            @pl.when(site.z < behind)
            def _(group=group, lanes=lanes):
                edge_copy(group).wait_recv()
                x_ref[step_at % XRING, positions - 8 :, lanes] = (
                    tail_ref[group] + edge_got[group]
                ).astype(BF16)

            @pl.when(site.z > 0)
            def _(group=group):
                edge_copy(group).wait_send()

        add_normed(wconv_ref, lambda: x_ref[step_at % XRING])

    last = OUT_PIECES + 2 * gates
    start = last - LAG - 1
    slot = last % XRING
    wide = 2 * STATE
    totals = Totals(site, t_sent, t_got, t_send, t_recv)

    def last_edge():
        return pltpu.make_async_remote_copy(
            src_ref=edge_sent.at[GROUPS], dst_ref=edge_got.at[GROUPS], send_sem=edge_send.at[GROUPS],
            recv_sem=edge_recv.at[GROUPS], device_id=(site.over(behind), site.f), device_id_type=MESH,
        )

    @pl.when(step_at == start)
    def _():
        tail, edge = maps_backward(plast_ref, wlast_ref, blast_ref, gacc_ref, dpad_ref, x_ref, slot, t_sent)
        tail_ref[GROUPS] = tail
        edge_sent[GROUPS] = edge

        @pl.when(site.z > 0)
        def _():
            last_edge().start()

        steps_backward(
            plast_ref, bias_ref, decay_ref, grown_ref, runs_ref, direct_ref, ends_ref, cross_ref, x_ref, slot,
            t_sent,
        )
        totals.start(0)

    for t in range(totals.count):

        @pl.when(step_at == start + 1 + t)
        def _(t=t):
            totals.next(t)

    @pl.when(step_at == start + 1 + totals.count)
    def _():
        total_ref[...] = t_sent[totals.count % 2]

    @pl.when(step_at == last)
    def _():
        @pl.when(site.z < behind)
        def _():
            last_edge().wait_recv()
            x_ref[slot, positions - 8 :, 0:wide] = (tail_ref[GROUPS] + edge_got[GROUPS]).astype(BF16)

        @pl.when(site.z > 0)
        def _():
            last_edge().wait_send()

        add_normed(wconv_ref, lambda: x_ref[step_at % XRING])

    after = step_at - last - 1

    @pl.when(jnp.logical_and(after >= 0, after < gates))
    def _():
        add_normed(wgate_ref, lambda: ggate_ref[...])

    tile = 128

    @pl.when(jnp.logical_and(after >= gates, after < gates + positions // (2 * tile)))
    def _():
        def one(i, carry):
            rows = pl.ds(pl.multiple_of((after - gates) * 2 * tile + i * tile, tile), tile)
            features = gtokens_ref.shape[1]
            inputs = tokens_ref[rows, :].astype(F32)
            r0 = lax.rsqrt(jnp.sum(inputs * inputs, axis=-1, keepdims=True) * (1.0 / features) + 1e-05)
            f = gain_ref[...] * gtokens_ref[rows, :]
            share = r0 * r0 * r0 * (jnp.sum(f * inputs, axis=-1, keepdims=True) * (1.0 / features))
            gtokens_ref[rows, :] = cot_ref[rows, :].astype(F32) + r0 * f - inputs * share
            return carry

        lax.fori_loop(0, 2, one, 0)

    def is_later(piece):
        return jnp.minimum(piece, OUT_PIECES) // OUT_PIECES

    def column(piece):
        after = jnp.maximum(piece - OUT_PIECES, 0)
        return jnp.minimum(piece, OUT_PIECES) + is_later(piece) * (1 - after % 2) * gates + after // 2

    scatter = Streamed(site, turned_ref, turned_out_ref, is_later, x_ref, own_ref, column, scatter_refs)
    at_stages(scatter.stages, last + 1, LAG, step_at, scatter.run)

    linked = step_at - (behind - site.z)
    blocks = positions // BLOCK_LEN

    @pl.when(jnp.logical_and(linked >= 0, linked < GROUPS))
    def _():
        @pl.when(site.z == behind)
        def _():
            got[linked] = jnp.zeros((GCOLS, STATE), BF16)

        @pl.when(site.z < behind)
        def _():
            chain_copy(site, linked, behind, sent, got, chain_send, chain_recv).wait_recv()

        @pl.when(site.z > 0)
        def _():
            span = pl.ds(pl.multiple_of(linked * GCOLS, GCOLS), GCOLS)
            grad = got[linked].astype(F32)
            for block in reversed(range(blocks)):
                grad = by_head(decays, linked, block) * grad + grads_ref[block, span, :]
            sent[linked % sent.shape[0]] = grad.astype(BF16)
            chain_copy(site, linked, behind, sent, got, chain_send, chain_recv).start()

    group = step_at - max(behind, LAG + 1)

    @pl.when(jnp.logical_and(group >= 0, group < GROUPS))
    def _():
        scan_backward_group(
            group, decays, p_ref, w_ref, b_ref, cols_ref, rows_ref, maps_ref, skip_ref, y_ref,
            dy_ref, dye_ref, st_ref, grads_ref, x_ref, tail_ref, edge_sent, t_sent, runs_ref, direct_ref,
            ends_ref, cross_ref, scores_ref, dscores_ref, dpad_ref, gacc_ref, dl_ref, got, conv_ref, inner_ref,
            outer_ref, low_ref, ended_ref,
        )

        @pl.when(site.z > 0)
        def _():
            edge_copy(group).start()
            chain_copy(site, group, behind, sent, got, chain_send, chain_recv).wait_send()


def maps_backward(p_ref, w_ref, b_ref, grad_ref, dpad_ref, x_ref, slot, t_sent):
    positions, wide = grad_ref.shape
    blocks = positions // BLOCK_LEN
    lanes = pl.ds(0, wide)
    taps = [jnp.zeros((1, wide), F32) for _ in range(CONV + 1)]
    for block in range(blocks):
        lo = block * BLOCK_LEN
        conv = convolved(p_ref, w_ref, b_ref, lo, BLOCK_LEN, lanes)
        sig = sigmoid(conv)
        dconv = grad_ref[lo : lo + BLOCK_LEN, :] * (sig * (1.0 + conv * (1.0 - sig)))
        dpad_ref[8 + lo : 8 + lo + BLOCK_LEN, :] = dconv
        for tap in range(CONV):
            at = EDGE - CONV + 1 + tap + lo
            taps[tap] = taps[tap] + jnp.sum(
                dconv * p_ref[at : at + BLOCK_LEN, 0:wide], axis=0, keepdims=True
            )
        taps[CONV] = taps[CONV] + jnp.sum(dconv, axis=0, keepdims=True)
    for index in range(CONV + 1):
        t_sent[0, index : index + 1, INNER : INNER + wide] = taps[index]
    t_sent[0, CONV + 1 :, INNER : INNER + wide] = jnp.zeros((8 - CONV - 1, wide), F32)

    def back_rows(at, count):
        back = jnp.zeros((count, wide), F32)
        for tap in range(CONV):
            start = at + CONV - 1 - tap
            back = back + dpad_ref[start : start + count, :] * w_ref[tap : tap + 1, 0:wide]
        return back

    for block in range(blocks):
        lo = block * BLOCK_LEN
        x_ref[slot, lo : lo + BLOCK_LEN, 0:wide] = back_rows(8 + lo, BLOCK_LEN).astype(BF16)
    return back_rows(positions, 8), back_rows(0, 8)


def steps_backward(
    p_ref, bias_ref, decay_ref, decays_ref, runs_ref, direct_ref, ends_ref, cross_ref, x_ref, slot, t_sent
):
    positions = runs_ref.shape[0]
    blocks = positions // BLOCK_LEN
    wide = 2 * STATE
    used = lax.broadcasted_iota(jnp.int32, (1, 128), 1) < HEADS
    rate = -jnp.exp(decay_ref[...])
    by_heads = jnp.zeros((8, 128), F32)
    for at in range(0, INNER, PIECE):
        spread = jnp.where(
            (at + lax.broadcasted_iota(jnp.int32, (PIECE, 128), 0)) // HEAD_DIM
            == lax.broadcasted_iota(jnp.int32, (PIECE, 128), 1),
            1.0,
            0.0,
        )
        by_heads = by_heads + exact_dot(ends_ref[:, at : at + PIECE], spread)
    per_group = blocks * GROUP
    crossed = jnp.sum(cross_ref[...].reshape(GROUPS * per_group, STATE), axis=1, keepdims=True)
    row = lax.broadcasted_iota(jnp.int32, (GROUPS * per_group, 128), 0)
    lane = lax.broadcasted_iota(jnp.int32, (GROUPS * per_group, 128), 1)
    same = (row // per_group) * GROUP + row % GROUP == lane
    tri_row = lax.broadcasted_iota(jnp.int32, (BLOCK_LEN, BLOCK_LEN), 0)
    tri_col = lax.broadcasted_iota(jnp.int32, (BLOCK_LEN, BLOCK_LEN), 1)
    upper = jnp.where(tri_row <= tri_col, 1.0, 0.0)
    grad_bias = jnp.zeros((1, 128), F32)
    grad_decay = jnp.zeros((1, 128), F32)
    for block in range(blocks):
        lo = block * BLOCK_LEN
        rows = slice(lo, lo + BLOCK_LEN)
        here = jnp.logical_and(same, (row % per_group) // GROUP == block)
        end = by_heads[block : block + 1] + decays_ref[block : block + 1, :] * jnp.sum(
            jnp.where(here, crossed, 0.0), axis=0, keepdims=True
        )
        arg = p_ref[EDGE + lo : EDGE + lo + BLOCK_LEN, wide : wide + 128] + bias_ref[...]
        step = softplus(arg)
        grad_log = exact_dot(upper, runs_ref[rows, :]) + end
        grad_step = jnp.where(used, (direct_ref[rows, :] + rate * grad_log) * sigmoid(arg), 0.0)
        grad_bias = grad_bias + jnp.sum(grad_step, axis=0, keepdims=True)
        grad_decay = grad_decay + jnp.sum(
            jnp.where(used, grad_log * (rate * step), 0.0), axis=0, keepdims=True
        )
        x_ref[slot, rows, wide : wide + 128] = grad_step.astype(BF16)
        x_ref[slot, rows, wide + 128 :] = jnp.zeros((BLOCK_LEN, PIECE - wide - 128), BF16)
    t_sent[0, :, INNER + wide :] = jnp.concatenate(
        [grad_bias, grad_decay, by_heads[blocks : blocks + 1], jnp.zeros((5, 128), F32)], axis=0
    )


def scan_backward_group(
    step_at, decays, p_ref, w_ref, b_ref, cols_ref, rows_ref, maps_ref, skip_ref, y_ref, dy_ref,
    dye_ref, st_ref, grads_ref, x_ref, tail_ref, edge_ref, t_sent, runs_ref, direct_ref, ends_ref,
    cross_ref, scores_ref, dscores_ref, dpad_ref, gacc_ref, dl_ref, got, conv_ref, inner_ref, outer_ref,
    low_ref, ended_ref,
):
    positions = y_ref.shape[0]
    blocks = positions // BLOCK_LEN
    width = 2 * HEAD_DIM

    @pl.when(step_at == 0)
    def _():
        masked_scores(maps_ref, scores_ref, blocks)
        ends_ref[...] = jnp.zeros_like(ends_ref)
        dscores_ref[...] = jnp.zeros_like(dscores_ref)
        gacc_ref[...] = jnp.zeros_like(gacc_ref)
        dpad_ref[0:8, :] = jnp.zeros((8, GCOLS), F32)
        dpad_ref[positions + 8 : positions + 16, :] = jnp.zeros((8, GCOLS), F32)

    ahead = PIECE // GCOLS
    slot = (OUT_PIECES + 2 * (step_at // ahead)) % XRING
    offset = (step_at % ahead) * GCOLS
    group_span = pl.ds(pl.multiple_of(step_at * GCOLS, GCOLS), GCOLS)
    grad = got[step_at].astype(F32)
    for block in reversed(range(blocks)):
        if block < blocks - 1:
            grad = by_head(decays, step_at, block + 1) * grad + grads_ref[block + 1, group_span, :]
        dl_ref[block] = grad.astype(BF16)
        product = grad * st_ref[block].astype(F32)
        for head in range(GROUP):
            at = block * GROUP + head
            cross_ref[step_at, at : at + 1, :] = jnp.sum(
                product[head * HEAD_DIM : (head + 1) * HEAD_DIM], axis=0, keepdims=True
            )

    half = first_half((BLOCK_LEN, width))
    lane_row = lax.broadcasted_iota(jnp.int32, (width, 128), 0)
    lane_col = lax.broadcasted_iota(jnp.int32, (width, 128), 1)
    gw = [[jnp.zeros((8, width), F32) for _ in range(CONV + 2)] for _ in range(PAIRS)]
    for block in range(blocks):
        lo = block * BLOCK_LEN
        rows = slice(lo, lo + BLOCK_LEN)
        outer_ref[...] = dot(maps_ref[rows, :STATE], dl_ref[block], NT)
        for pair in range(PAIRS):
            lanes = pl.ds(pair * width, width)
            for top in range(0, BLOCK_LEN, PART):
                part = slice(lo + top, lo + top + PART)
                here = slice(top, top + PART)
                conv = convolved(p_ref, w_ref, b_ref, lo + top, PART, lanes)
                conv_ref[here, :] = conv
                xs = conv * sigmoid(conv) * per_pair(cols_ref, 0, pair, part)
                low_ref[here, :] = xs.astype(BF16)
                ended_ref[here, lanes] = (xs * per_pair(cols_ref, 3, pair, part)).astype(BF16)
            dyl = dy_ref[rows, lanes]
            none = jnp.zeros_like(dyl)
            sides = (jnp.where(half, dyl, none), jnp.where(half, none, dyl))
            turned = dyl.astype(F32).T.astype(BF16)
            dxt = [None, None]
            for strip in range(BLOCK_LEN // STRIP):
                top = strip * STRIP
                lim = top + STRIP
                scores = scores_ref[block, top:lim, :lim]
                gathered = jnp.zeros((STRIP, lim), F32)
                for side in range(2):
                    head = 2 * pair + side
                    at = GROUP + head
                    gap = (
                        cols_ref[lo + top : lo + lim, at : at + 1]
                        - rows_ref[head : head + 1, lo : lo + lim]
                    )
                    decay = jnp.exp2(jnp.minimum(gap, 0.0))
                    gathered = gathered + dot(sides[side][top:lim], low_ref[:lim, :], NT) * decay
                    part = dot(
                        turned[side * HEAD_DIM : (side + 1) * HEAD_DIM, top:lim],
                        (scores * decay).astype(BF16),
                    )
                    if strip == 0:
                        dxt[side] = jnp.concatenate(
                            [part, jnp.zeros((HEAD_DIM, BLOCK_LEN - STRIP), F32)], axis=1
                        )
                    else:
                        dxt[side] = dxt[side] + part
                dscores_ref[block, top:lim, :lim] += gathered
            inner_ref[...] = jnp.concatenate(dxt, axis=0).T
            skip = skip_ref[0:1, lanes]
            at = step_at * GROUP + 2 * pair
            heads_of = jnp.where(lane_col == at + lane_row // HEAD_DIM, 1.0, 0.0).astype(BF16)
            ends = jnp.zeros((8, width), F32)

            def folded(values):
                return jnp.sum(values.reshape(PART // 8, 8, width), axis=0)

            for top in range(0, BLOCK_LEN, PART):
                part = slice(lo + top, lo + top + PART)
                here = slice(top, top + PART)
                conv = conv_ref[here, :]
                sig = sigmoid(conv)
                x = conv * sig
                step = per_pair(cols_ref, 0, pair, part)
                inner = inner_ref[here, :]
                outer = outer_ref[here, lanes] * per_pair(cols_ref, 3, pair, part)
                dyf = dy_ref[part, lanes].astype(F32)
                dxs = inner + outer
                vs = x * step * outer
                ends = ends + folded(vs)
                runs = dyf * (y_ref[part, lanes] - skip * x) - low_ref[here, :].astype(F32) * inner - vs
                for sums_ref, values in ((runs_ref, runs), (direct_ref, x * dxs)):
                    high = values.astype(BF16)
                    rest = (values - high.astype(F32)).astype(BF16)
                    sums_ref[part, :] += dot(high, heads_of) + dot(rest, heads_of)
                gw[pair][CONV + 1] = gw[pair][CONV + 1] + folded(dyf * x)
                dconv = (dxs * step + skip * dyf) * (sig * (1.0 + conv * (1.0 - sig)))
                gw[pair][CONV] = gw[pair][CONV] + folded(dconv)
                dpad_ref[8 + lo + top : 8 + lo + top + PART, lanes] = dconv
                for tap in range(CONV):
                    first = EDGE - CONV + 1 + tap + lo + top
                    gw[pair][tap] = gw[pair][tap] + folded(dconv * p_ref[first : first + PART, lanes])
            group_lanes = pl.ds(pl.multiple_of(step_at * GCOLS + pair * width, width), width)
            ends_ref[block : block + 1, group_lanes] = jnp.sum(ends, axis=0, keepdims=True)
        gacc_ref[rows, :STATE] += dot(ended_ref[...], dl_ref[block])
        gacc_ref[rows, STATE:] += dot(dye_ref[rows, :], st_ref[block])

    for pair in range(PAIRS):
        lanes = pl.ds(pair * width, width)
        group_lanes = pl.ds(pl.multiple_of(step_at * GCOLS + pair * width, width), width)
        for index in range(CONV + 1):
            t_sent[0, index : index + 1, group_lanes] = jnp.sum(gw[pair][index], axis=0, keepdims=True)
        ends_ref[blocks : blocks + 1, group_lanes] = jnp.sum(gw[pair][CONV + 1], axis=0, keepdims=True)
        edge = jnp.zeros((8, width), F32)
        for tap in range(CONV):
            edge = edge + dpad_ref[CONV - 1 - tap : CONV - 1 - tap + 8, lanes] * w_ref[tap : tap + 1, lanes]
        edge_ref[step_at, :, lanes] = edge
        for top in range(0, positions, PART):
            back = jnp.zeros((PART, width), F32)
            for tap in range(CONV):
                at = 8 + CONV - 1 - tap + top
                back = back + dpad_ref[at : at + PART, lanes] * w_ref[tap : tap + 1, lanes]
            x_ref[slot, top : top + PART, pl.ds(pl.multiple_of(offset + pair * width, width), width)] = (
                back.astype(BF16)
            )
        tail_ref[step_at, :, lanes] = back[PART - 8 :]

    @pl.when(step_at == GROUPS - 1)
    def _():
        row = lax.broadcasted_iota(jnp.int32, (BLOCK_LEN, BLOCK_LEN), 0)
        col = lax.broadcasted_iota(jnp.int32, (BLOCK_LEN, BLOCK_LEN), 1)
        for block in range(blocks):
            rows = slice(block * BLOCK_LEN, (block + 1) * BLOCK_LEN)
            low = jnp.where(row >= col, dscores_ref[block], 0.0).astype(BF16)
            gacc_ref[rows, :STATE] += dot(low, maps_ref[rows, STATE:], TN)
            gacc_ref[rows, STATE:] += dot(low, maps_ref[rows, :STATE])


def scan_backward(
    decays, p, w, b, cols, rows, maps, skip, y, dy, dye, starts, ends, turned, turned_out, cot, grad_gate,
    inw_gate, inw_conv, bias, decay_log, tokens, gain, own_rows, collective_id,
):
    positions = y.shape[0]
    features = inw_gate.shape[0]
    blocks = positions // BLOCK_LEN
    ext = p.shape[0]
    zs, n = lax.axis_size("seq"), lax.axis_size("fsdp")
    gates = INNER // PIECE
    pieces = OUT_PIECES + 2 * gates + 1
    count = exchange_count(zs, n)
    steps = pieces + max(LAG * (stages_of(n) - 1), count - LAG, gates + positions // 256)
    width = CHANNELS + 128
    dma = pltpu.SemaphoreType.DMA

    def late(s):
        return jnp.clip(s - max(zs - 1, LAG + 1), 0, GROUPS - 1)

    def turn(s, most):
        return jnp.clip((s - OUT_PIECES) // 2, 0, most)

    def gate_turn(s):
        again = jnp.maximum(s - pieces + 1, 0)
        return turn(s - 1, gates - 1) * (1 - jnp.minimum(again, 1)) + jnp.clip(again - 1, 0, gates - 1)

    once = pl.Buffered(1)
    own = pl.BlockSpec((positions, GCOLS), lambda s: (0, late(s)))
    eight = pl.BlockSpec((8, GCOLS), lambda s: (0, late(s)))
    states = pl.BlockSpec((blocks, GCOLS, STATE), lambda s: (0, late(s), 0))

    def whole(x):
        return pl.BlockSpec(x.shape, lambda s: (0,) * len(x.shape), pipeline_mode=once)

    return pl.pallas_call(
        scan_backward_kernel,
        grid=(steps,),
        in_specs=[
            pl.BlockSpec(memory_space=pltpu.SMEM),
            pl.BlockSpec((ext, GCOLS), lambda s: (0, late(s))),
            eight,
            pl.BlockSpec((1, GCOLS), lambda s: (0, late(s))),
            pl.BlockSpec((None, positions, 4 * GROUP), lambda s: (late(s), 0, 0)),
            pl.BlockSpec((None, GROUP, positions), lambda s: (late(s), 0, 0)),
            whole(maps),
            pl.BlockSpec((1, GCOLS), lambda s: (0, late(s))),
            own,
            own,
            own,
            states,
            whole(ends),
            whole(turned),
            whole(turned_out),
            whole(cot),
            pl.BlockSpec((positions, PIECE), lambda s: (0, gate_turn(s))),
            pl.BlockSpec((features, PIECE), lambda s: (0, jnp.clip(s - pieces, 0, gates - 1))),
            pl.BlockSpec((features, PIECE), lambda s: (0, turn(s, gates))),
            pl.BlockSpec((ext, PIECE), lambda s: (0, gates), pipeline_mode=once),
            pl.BlockSpec((8, PIECE), lambda s: (0, gates), pipeline_mode=once),
            pl.BlockSpec((1, PIECE), lambda s: (0, gates), pipeline_mode=once),
            whole(bias),
            whole(decay_log),
            whole(decays),
            whole(tokens),
            whole(gain),
        ],
        out_specs=[
            pl.BlockSpec((own_rows, pieces * PIECE), lambda s: (0, 0), pipeline_mode=once),
            pl.BlockSpec((positions, features), lambda s: (0, 0), pipeline_mode=once),
            pl.BlockSpec((8, width), lambda s: (0, 0), pipeline_mode=once),
        ],
        out_shape=[
            jax.ShapeDtypeStruct((own_rows, pieces * PIECE), F32),
            jax.ShapeDtypeStruct((positions, features), F32),
            jax.ShapeDtypeStruct((8, width), F32),
        ],
        scratch_shapes=[
            pltpu.VMEM((blocks, BLOCK_LEN, BLOCK_LEN), F32),
            pltpu.VMEM((blocks, BLOCK_LEN, BLOCK_LEN), F32),
            pltpu.VMEM((positions + 16, GCOLS), F32),
            pltpu.VMEM((positions, 2 * STATE), F32),
            pltpu.VMEM((blocks, GCOLS, STATE), BF16),
            pltpu.VMEM((XRING, positions, PIECE), BF16),
            pltpu.VMEM((GROUPS + 1, 8, GCOLS), F32),
            pltpu.VMEM((positions, 128), F32),
            pltpu.VMEM((positions, 128), F32),
            pltpu.VMEM((8, INNER), F32),
            pltpu.VMEM((GROUPS, blocks * GROUP, STATE), F32),
            pltpu.VMEM((BLOCK_LEN, 2 * HEAD_DIM), F32),
            pltpu.VMEM((BLOCK_LEN, 2 * HEAD_DIM), F32),
            pltpu.VMEM((BLOCK_LEN, GCOLS), F32),
            pltpu.VMEM((BLOCK_LEN, 2 * HEAD_DIM), BF16),
            pltpu.VMEM((BLOCK_LEN, GCOLS), BF16),
        ]
        + chain_scratch()
        + [
            pltpu.VMEM((GROUPS + 1, 8, GCOLS), F32),
            pltpu.VMEM((GROUPS + 1, 8, GCOLS), F32),
            dma((GROUPS + 1,)),
            dma((GROUPS + 1,)),
            pltpu.VMEM((2, 8, width), F32),
            pltpu.VMEM((count, 8, width), F32),
            dma((count,)),
            dma((count,)),
        ]
        + Streamed.scratch(own_rows),
        compiler_params=pltpu.CompilerParams(
            collective_id=collective_id, has_side_effects=True, vmem_limit_bytes=63 * 2**20
        ),
        cost_estimate=pl.CostEstimate(
            flops=24 * positions * INNER * BLOCK_LEN, bytes_accessed=30 * positions * INNER,
            transcendentals=HEADS * positions * BLOCK_LEN,
        ),
        name="scan_backward",
    )(
        decays, p, w, b, cols, rows, maps, skip, y, dy, dye, starts, ends, turned, turned_out, cot, grad_gate,
        inw_gate, inw_conv, p, w, b, bias, decay_log, decays, tokens, gain,
    )


PIECE = 512
LAG = 2
HALF = PIECE // 2
MESH = pl.DeviceIdType.MESH


class Site:
    def __init__(self):
        self.zs, self.n = lax.axis_size("seq"), lax.axis_size("fsdp")
        self.z, self.f = lax.axis_index("seq"), lax.axis_index("fsdp")
        self.chips = self.n // 2
        self.bits = self.chips.bit_length() - 1

    def bit(self, j):
        return (self.f // 2**j) % 2

    def flip(self, js):
        f = self.f
        for j in js:
            f = f + (1 - 2 * self.bit(j)) * 2**j
        return f

    def over(self, dz):
        return (self.z + dz) % self.zs

    def greet(self):
        barrier = pltpu.get_barrier_semaphore()
        for dz in range(1, self.zs):
            pl.semaphore_signal(barrier, inc=1, device_id=(self.over(dz), self.f), device_id_type=MESH)
        for j in range(self.bits + 1):
            pl.semaphore_signal(barrier, inc=1, device_id=(self.z, self.flip([j])), device_id_type=MESH)
        pl.semaphore_wait(barrier, self.zs + self.bits)


def subsets(js):
    found = [()]
    for j in js:
        found = found + [s + (j,) for s in found]
    return found


class Gather:
    def __init__(self, site, own, whole, local_sem, send_sem, recv_sem):
        self.site, self.own, self.whole = site, own, whole
        self.local_sem, self.send_sem, self.recv_sem = local_sem, send_sem, recv_sem
        self.along = len(own.shape) == 2
        self.skipped = 0 if self.along else 1
        self.stages = site.bits + 3 - self.skipped

    @staticmethod
    def slots(zs, n):
        return zs + 4 * (n // 2 - 1)

    def moves(self, piece):
        s = self.site
        start = piece * PIECE
        whole = pl.ds(pl.multiple_of(start, 128), PIECE)
        halves = (
            pl.ds(pl.multiple_of(start, 128), HALF),
            pl.ds(pl.multiple_of(start + HALF, 128), HALF),
        )
        slot = 0
        plan = [[] for _ in range(s.bits + 3)]
        for dz in range(1, s.zs):
            if not self.along:
                slot += 1
                continue
            plan[0].append(
                (slot, self.own.at[:, whole], self.whole.at[s.z, s.f, :, whole],
                 (s.over(dz), s.f), self.whole.at[s.over(s.zs - dz), s.f, :, whole])
            )
            slot += 1
        sibling = s.flip([0])

        def known(js, cols):
            if not js and not self.along:
                return self.own.at[:, :, cols]
            return self.whole.at[:, s.flip(js), :, cols]

        def shared(js, cols):
            return (slot, known(js, cols), self.whole.at[:, s.flip(js), :, cols],
                    (s.z, sibling), self.whole.at[:, s.flip(list(js) + [0]), :, cols])

        plan[1].append(shared([], whole))
        slot += 1
        up = list(range(1, s.bits + 1))
        for half, order in enumerate((up, up[::-1])):
            cols = halves[half]
            for at, j in enumerate(order):
                for js in subsets(order[:at]):
                    js = list(js)
                    plan[at + 1].append(
                        (slot, known(js, cols), self.whole.at[:, s.flip(js), :, cols],
                         (s.z, s.flip([j])), self.whole.at[:, s.flip(js + [j]), :, cols])
                    )
                    slot += 1
                    plan[at + 2].append(shared(js + [j], cols))
                    slot += 1
        return plan[self.skipped :]

    def leaving(self, piece, moves):
        return [
            pltpu.make_async_remote_copy(
                src_ref=src, dst_ref=dst, send_sem=self.send_sem.at[piece, slot],
                recv_sem=self.recv_sem.at[piece, slot], device_id=device, device_id_type=MESH,
            )
            for slot, src, dst, device, _ in moves
        ]

    def arriving(self, piece, moves):
        return [
            pltpu.make_async_remote_copy(
                src_ref=src, dst_ref=incoming, send_sem=self.send_sem.at[piece, slot],
                recv_sem=self.recv_sem.at[piece, slot], device_id=device, device_id_type=MESH,
            )
            for slot, src, _, device, incoming in moves
        ]

    def run(self, stage, piece):
        s = self.site
        plan = self.moves(piece)
        cols = pl.ds(pl.multiple_of(piece * PIECE, 128), PIECE)

        def local():
            if self.along:
                src, dst = self.own.at[:, cols], self.whole.at[s.z, s.f, :, cols]
            else:
                src, dst = self.own.at[:, :, cols], self.whole.at[:, s.f, :, cols]
            return pltpu.make_async_copy(src, dst, self.local_sem.at[piece])

        to_core = [[m for m in moves if self.is_core(stage_at, m)] for stage_at, moves in enumerate(plan)]
        others = [[m for m in moves if not self.is_core(stage_at, m)] for stage_at, moves in enumerate(plan)]
        if stage == 0:
            local().start()
        if stage == 1:
            local().wait()
        if 0 < stage:
            for copy in self.arriving(piece, others[stage - 1]):
                copy.wait_recv()
        if stage < self.stages - 1:
            for copy in self.leaving(piece, others[stage] + to_core[stage]):
                copy.start()
        else:
            for moves in to_core:
                for copy in self.arriving(piece, moves):
                    copy.wait_recv()
            for moves in plan:
                for copy in self.leaving(piece, moves):
                    copy.wait_send()

    def is_core(self, stage, move):
        slot = move[0]
        zs = self.site.zs
        if slot < zs - 1:
            return False
        return (slot - (zs - 1)) % 2 == 0


def at_stages(stages, pieces, lag, step, run):
    for stage in reversed(range(stages)):
        piece = step - lag * stage

        @pl.when(jnp.logical_and(piece >= 0, piece < pieces))
        def _(stage=stage, piece=piece):
            run(stage, piece)


def stages_of(n):
    return (n // 2).bit_length() + 2


def along_line(step, start, site, own, line, local_sem, send_sem, recv_sem):
    local = functools.partial(pltpu.make_async_copy, own, line.at[site.z], local_sem)

    def passing(hop, way):
        z = site.z - way * hop
        return pltpu.make_async_remote_copy(
            src_ref=own if hop == 0 else line.at[z], dst_ref=line.at[z],
            send_sem=send_sem.at[hop, (1 - way) // 2], recv_sem=recv_sem.at[hop, (1 - way) // 2],
            device_id=(site.z + way, site.f), device_id_type=MESH,
        )

    def arriving(hop, way):
        z = site.z - way * (hop + 1)
        return pltpu.make_async_remote_copy(
            src_ref=own, dst_ref=line.at[z],
            send_sem=send_sem.at[hop, (1 - way) // 2], recv_sem=recv_sem.at[hop, (1 - way) // 2],
            device_id=(site.z - way, site.f), device_id_type=MESH,
        )

    def inside(z):
        return jnp.logical_and(z >= 0, z < site.zs)

    for hop in range(site.zs):

        @pl.when(step == start + LAG * hop)
        def _(hop=hop):
            if hop == 0:
                local().start()
            else:
                for way in (1, -1):

                    @pl.when(inside(site.z - way * hop))
                    def _(way=way):
                        arriving(hop - 1, way).wait_recv()

            if hop < site.zs - 1:
                for way in (1, -1):

                    @pl.when(jnp.logical_and(inside(site.z - way * hop), inside(site.z + way)))
                    def _(way=way):
                        passing(hop, way).start()

            else:
                local().wait()
                for early in range(site.zs - 1):
                    for way in (1, -1):

                        @pl.when(jnp.logical_and(inside(site.z - way * early), inside(site.z + way)))
                        def _(way=way, early=early):
                            passing(early, way).wait_send()


def gather_kernel(pieces, start, own, late, last, whole, line, before, *refs):
    step = pl.program_id(0)
    site = Site()

    @pl.when(step == 0)
    def _():
        site.greet()

    edge_send, edge_recv = refs[3:5]

    def edge():
        return pltpu.make_async_remote_copy(
            src_ref=last, dst_ref=before, send_sem=edge_send, recv_sem=edge_recv,
            device_id=(site.over(1), site.f), device_id_type=MESH,
        )

    @pl.when(step == 0)
    def _():
        edge().start()

    gather = Gather(site, own, whole, *refs[:3])
    at_stages(gather.stages, pieces, LAG, step, gather.run)
    along_line(step, start, site, late, line, *refs[5:])

    @pl.when(step == pl.num_programs(0) - 1)
    def _():
        edge().wait()


def gather_scratch(pieces):
    slots = Gather.slots(lax.axis_size("seq"), lax.axis_size("fsdp"))
    return [
        pltpu.SemaphoreType.DMA((pieces,)),
        pltpu.SemaphoreType.DMA((pieces, slots)),
        pltpu.SemaphoreType.DMA((pieces, slots)),
    ]


def gathered(own, late, last, collective_id):
    rows, columns = own.shape
    zs, n = lax.axis_size("seq"), lax.axis_size("fsdp")
    pieces = columns // PIECE
    steps = max(pieces + LAG * (stages_of(n) - 1), LAG * zs)
    start = min(pieces // 2, steps - LAG * (zs - 1) - 1)
    anywhere = pl.BlockSpec(memory_space=pl.ANY)
    dma = pltpu.SemaphoreType.DMA
    return pl.pallas_call(
        functools.partial(gather_kernel, pieces, start),
        grid=(steps,),
        in_specs=[anywhere] * 3,
        out_specs=[anywhere] * 3,
        out_shape=[
            jax.ShapeDtypeStruct((zs, n, rows, columns), own.dtype),
            jax.ShapeDtypeStruct((zs,) + late.shape, late.dtype),
            jax.ShapeDtypeStruct(last.shape, last.dtype),
        ],
        scratch_shapes=gather_scratch(pieces) + [dma, dma, dma, dma((zs - 1, 2)), dma((zs - 1, 2))],
        compiler_params=pltpu.CompilerParams(collective_id=collective_id, has_side_effects=True),
        cost_estimate=pl.CostEstimate(
            flops=0, bytes_accessed=2 * zs * n * rows * columns, transcendentals=0
        ),
        name="gather_rows",
    )(own, late, last)


class Scatter:
    def take(self, refs):
        bits = self.site.bits
        self.kept = refs[:bits]
        self.sent = refs[bits : 2 * bits]
        self.got = refs[2 * bits : 3 * bits]
        self.z_kept, self.z_sent, self.z_got, self.send_sem, self.recv_sem = refs[3 * bits :]
        self.stages = bits + 3

    @staticmethod
    def common(pieces, rows):
        zs, n = lax.axis_size("seq"), lax.axis_size("fsdp")
        chips = n // 2
        bits = chips.bit_length() - 1
        slots = 1 + 2 * bits + zs - 1
        steps = [(pieces, 2, zs, chips >> (k + 1), rows, HALF) for k in range(bits)]
        return (
            [pltpu.VMEM(s, F32) for s in steps]
            + [pltpu.VMEM(s, BF16) for s in steps]
            + [pltpu.VMEM(s, BF16) for s in steps]
            + [
                pltpu.VMEM((pieces, rows, PIECE), F32),
                pltpu.VMEM((pieces, zs, rows, PIECE), BF16),
                pltpu.VMEM((pieces, zs - 1, rows, PIECE), BF16),
                pltpu.SemaphoreType.DMA((pieces, slots)),
                pltpu.SemaphoreType.DMA((pieces, slots)),
            ]
        )

    def remote(self, piece, slot, src, dst, device):
        at = self.at(piece)
        return pltpu.make_async_remote_copy(
            src_ref=src, dst_ref=dst, send_sem=self.send_sem.at[at, slot],
            recv_sem=self.recv_sem.at[at, slot], device_id=device, device_id_type=MESH,
        )

    def order(self, half):
        up = list(range(1, self.site.bits + 1))
        return up[::-1] if half == 0 else up

    def across(self, piece, k, half):
        s, at = self.site, self.at(piece)
        return self.remote(
            piece, 1 + 2 * k + half, self.sent[k].at[at, half], self.got[k].at[at, half],
            (s.z, s.flip([self.order(half)[k]])),
        )

    def along(self, piece, dz):
        s, at = self.site, self.at(piece)
        return self.remote(
            piece, 2 * s.bits + dz, self.z_sent.at[at, s.over(dz)], self.z_got.at[at, dz - 1],
            (s.over(dz), s.f),
        )

    def run(self, stage, piece):
        s, at = self.site, self.at(piece)
        bits = s.bits
        if stage == 0:
            self.begin(piece)
            self.to_core(piece).start()
            return
        if stage == 1:
            self.join(piece)
            self.to_core(piece).wait()
        elif stage <= bits + 1:
            for half in range(2):
                self.across(piece, stage - 2, half).wait()
        if stage <= bits:
            k = stage - 1
            for half in range(2):
                order = self.order(half)
                left = sorted(order[k:])
                j = order[k]
                place = left.index(j)
                mine = s.bit(j)

                def one(zi, carry, half=half, k=k, place=place, mine=mine):
                    for i in range(s.chips >> (k + 1)):
                        low = i % 2**place
                        base = (i - low) * 2 + low
                        self.sent[k][at, half, zi, i] = self.current(
                            k, piece, half, zi, base + (1 - mine) * 2**place
                        ).astype(BF16)
                        self.kept[k][at, half, zi, i] = self.current(
                            k, piece, half, zi, base + mine * 2**place
                        )
                    return carry

                lax.fori_loop(0, s.zs, one, 0)
                self.across(piece, k, half).start()
        elif stage == bits + 1:
            for half in range(2):
                lanes = slice(half * HALF, (half + 1) * HALF)

                def one(zi, carry, half=half, lanes=lanes):
                    self.z_sent[at, zi, :, lanes] = self.current(bits, piece, half, zi, 0).astype(BF16)
                    return carry

                lax.fori_loop(0, s.zs, one, 0)
                self.z_kept[at, :, lanes] = self.current(bits, piece, half, s.z, 0)
            for dz in range(1, s.zs):
                self.along(piece, dz).start()
        else:
            total = self.z_kept[at]
            for dz in range(1, s.zs):
                self.along(piece, dz).wait()
                total = total + self.z_got[at, dz - 1].astype(F32)
            self.out[:, pl.ds(pl.multiple_of(self.column(piece) * PIECE, 128), PIECE)] = total

    def current(self, k, piece, half, zi, index):
        at = self.at(piece)
        lanes = slice(half * HALF, (half + 1) * HALF)
        if k == 0:
            return self.first(piece, zi, index, lanes) + self.came[at, zi, index, :, lanes].astype(F32)
        return self.kept[k - 1][at, half, zi, index] + self.got[k - 1][at, half, zi, index].astype(F32)


RING = 4
XRING = 6
OUT_PIECES = 6
OUT_SPLIT = 2


class Streamed(Scatter):
    def __init__(self, site, turned, turned_out, is_later, x, out, column, refs):
        self.site, self.x, self.out = site, x, out
        self.turned, self.turned_out, self.is_later, self.column = turned, turned_out, is_later, column
        self.ring, self.x_ring = refs[0].shape[0], x.shape[0]
        self.away, self.own, self.came = refs[:3]
        self.take(refs[3:])

    @staticmethod
    def scratch(rows, ring=RING):
        zs, n = lax.axis_size("seq"), lax.axis_size("fsdp")
        full = (zs, n // 2, rows, PIECE)
        return [
            pltpu.VMEM((ring,) + full, BF16),
            pltpu.VMEM(full, BF16),
            pltpu.VMEM((ring,) + full, BF16),
        ] + Scatter.common(ring, rows)

    def at(self, piece):
        return piece % self.ring

    def to_core(self, piece):
        s, at = self.site, self.at(piece)
        return self.remote(piece, 0, self.away.at[at], self.came.at[at], (s.z, s.flip([0])))

    def product(self, core, piece, store):
        s = self.site
        rows = self.away.shape[3]
        together = 2 - s.zs % 2
        count = together * s.chips * rows
        share = OUT_PIECES // OUT_SPLIT

        for later in range(2):

            @pl.when(self.is_later(piece) == later)
            def _(later=later):
                def one(i, carry):
                    span = pl.ds(pl.multiple_of(i * count, 16), count)
                    if later:
                        lhs = self.turned[core, span, :]
                    else:
                        lhs = self.turned_out[jnp.minimum(piece, OUT_PIECES - 1) // share, core, span, :]
                    value = dot(lhs, self.x[piece % self.x_ring]).reshape(together, s.chips, rows, PIECE)
                    store(pl.ds(i * together, together), value)
                    return carry

                lax.fori_loop(0, s.zs // together, one, 0)

    def begin(self, piece):
        at = self.at(piece)

        def store(zi, value):
            self.away[at, zi] = value.astype(BF16)

        self.product(1 - self.site.bit(0), piece, store)

    def join(self, piece):
        def store(zi, value):
            self.own[zi] = value.astype(BF16)

        self.product(self.site.bit(0), piece, store)

    def first(self, piece, zi, index, lanes):
        return self.own[zi, index, :, lanes].astype(F32)


def exchange_count(zs, n):
    return (n.bit_length() - 1) + (zs.bit_length() - 1)


class Totals:
    def __init__(self, site, sent, got, send_sem, recv_sem):
        self.site, self.sent, self.got = site, sent, got
        self.send_sem, self.recv_sem = send_sem, recv_sem
        self.count = exchange_count(site.zs, site.n)

    def move(self, t):
        s = self.site
        if t <= s.bits:
            device = (s.z, s.flip([t]))
        else:
            j = t - s.bits - 1
            device = (s.z + (1 - 2 * ((s.z // 2**j) % 2)) * 2**j, s.f)
        return pltpu.make_async_remote_copy(
            src_ref=self.sent.at[t % 2], dst_ref=self.got.at[t], send_sem=self.send_sem.at[t],
            recv_sem=self.recv_sem.at[t], device_id=device, device_id_type=MESH,
        )

    def start(self, t):
        if t < self.count:
            self.move(t).start()

    def next(self, t):
        if t < self.count:
            self.move(t).wait()
            self.sent[(t + 1) % 2] = self.sent[t % 2] + self.got[t]
            self.start(t + 1)


CONV_COLS = 3584


def local(
    tokens, pre_gain, in_weight, conv_weight, conv_bias, step_bias, decay_log, skip_gain,
    norm_gain, out_weight, cotangent,
):
    both = ("seq", "fsdp")
    _, positions, features = tokens.shape
    blocks = positions // BLOCK_LEN
    devices = lax.axis_size("seq") * lax.axis_size("fsdp")

    rows = in_weight.shape[0]
    padded_rows = -(-rows // 16) * 16
    vectors = jnp.concatenate([pre_gain, conv_weight.reshape(-1), conv_bias, norm_gain])
    extra = -(-vectors.size // rows)
    sizes = (pre_gain.size, conv_weight.size, conv_bias.size, norm_gain.size)
    cuts = [sum(sizes[:i]) for i in range(5)]
    used = PROJ - INNER
    more_rows = ((0, padded_rows - rows), (0, 0))
    own = jnp.concatenate(
        [
            in_weight[:, INNER:],
            jnp.pad(vectors, (0, extra * rows - vectors.size)).reshape(rows, extra),
            jnp.zeros((rows, CONV_COLS - used - extra), BF16),
        ],
        axis=1,
    )
    inw_conv, gate_line, before = gathered(
        jnp.pad(own, more_rows),
        jnp.pad(in_weight[:, :INNER], more_rows),
        tokens[0, positions - EDGE :],
        1,
    )
    later, before = lax.optimization_barrier((out_weight, before))
    outw_full = lax.all_gather(later, both, axis=0, tiled=True)
    inw_conv = inw_conv[:, :, :rows].reshape(features, CONV_COLS)
    small_full = inw_conv[:, used : used + extra].reshape(devices, rows * extra)
    gain_full = small_full[:, : cuts[1]].reshape(1, features).astype(F32)
    convw_full = (
        small_full[:, cuts[1] : cuts[2]]
        .reshape(devices, CONV, -1)
        .transpose(1, 0, 2)
        .reshape(CONV, CHANNELS)
        .astype(F32)
    )
    convb_full = small_full[:, cuts[2] : cuts[3]].reshape(1, CHANNELS).astype(F32)
    normg_full = small_full[:, cuts[3] : cuts[4]].reshape(1, INNER).astype(F32)

    before = jnp.where(lax.axis_index("seq") == 0, jnp.zeros_like(before), before)
    ext = jnp.concatenate([before, tokens[0]], axis=0).astype(F32)
    r0_ext = lax.rsqrt(jnp.mean(ext * ext, axis=-1, keepdims=True) + 1e-05)
    normed_ext = (ext * r0_ext * gain_full).astype(BF16)
    inputs, r0, normed = ext[EDGE:], r0_ext[EDGE:], normed_ext[EDGE:]

    p = dot(normed_ext, inw_conv)
    unused = ((0, 0), (0, CONV_COLS - CHANNELS))
    w = jnp.pad(convw_full, ((0, 8 - CONV), (0, CONV_COLS - CHANNELS)))
    b = jnp.pad(convb_full, unused)
    wide_heads = ((0, 0), (0, 128 - HEADS))
    bias, decay_row = jnp.pad(step_bias[None], wide_heads), jnp.pad(decay_log[None], wide_heads)
    cols, run_rows, maps, run_exp, decays = steps_of(
        p, w, b, bias, decay_row, positions
    )
    skip = jnp.repeat(skip_gain, HEAD_DIM)[None]
    by_rows = jnp.pad(normed.reshape(positions, devices, rows), ((0, 0), (0, 0), more_rows[0]))
    y, starts, gate, turned_in, inw_gate = scan_forward(
        decays, p, w, b, cols, run_rows, maps, skip, by_rows.reshape(positions, -1), gate_line, positions, 2
    )
    inw_gate = inw_gate[:, :, :rows].reshape(features, INNER)
    cot = cotangent[0]
    grad_normed_out = dot(cot, outw_full, NT)
    normed_out, dy, dye, grad_gate, ends, *turned_out = gated(
        y, gate, grad_normed_out, normg_full, run_exp, maps, rows if rows == padded_rows else None
    )
    mixed = (inputs + dot(normed_out, outw_full)).astype(BF16)[None]

    if turned_out:
        turned_out = turned_out[0]
    else:
        turned_out = normed_out.T.reshape(-1, 2, OUT_SPLIT, rows, positions)
        turned_out = jnp.pad(turned_out, ((0, 0),) * 3 + more_rows).transpose(2, 1, 0, 3, 4)
    turned_out = turned_out.reshape(OUT_SPLIT, 2, -1, positions)
    own_main, grad_tokens, totals = scan_backward(
        decays, p, w, b, cols, run_rows, maps, skip, y, dy, dye, starts, ends, turned_in, turned_out, cot, grad_gate,
        inw_gate, inw_conv, bias, decay_row, tokens[0], gain_full, padded_rows, 3,
    )
    own_main = own_main[:rows]
    out_cols = OUT_PIECES * PIECE
    own_out = own_main[:, :out_cols].reshape(rows, OUT_SPLIT, features).transpose(1, 0, 2)
    own_out = own_out.reshape(OUT_SPLIT * rows, features)
    own_in = own_main[:, out_cols : out_cols + PROJ]
    per_tap = conv_weight.shape[1]
    me = lax.axis_index("seq") * lax.axis_size("fsdp") + lax.axis_index("fsdp")
    own_taps = lax.dynamic_slice_in_dim(totals, me * per_tap, per_tap, axis=1)
    heads = totals[:3, CHANNELS : CHANNELS + HEADS]

    return (
        mixed,
        grad_tokens[None],
        jnp.sum(own_in * in_weight.astype(F32), axis=1) / pre_gain.astype(F32),
        own_in,
        own_taps[:CONV],
        own_taps[CONV],
        heads[0],
        heads[1],
        heads[2],
        jnp.sum(own_out * out_weight.astype(F32), axis=1) / norm_gain.astype(F32),
        own_out,
    )


def solution(mesh):
    split = P(("seq", "fsdp"), None)
    flat = P(("seq", "fsdp"))
    taps = P(None, ("seq", "fsdp"))
    data = P("fsdp", "seq", None)
    return jax.shard_map(
        local,
        mesh=mesh,
        in_specs=(data, flat, split, taps, flat, P(), P(), P(), flat, split, data),
        out_specs=(data, data, flat, split, taps, flat, P(), P(), P(), flat, split),
        check_vma=False,
    )
```

```python
import functools
import math
import jax
import jax.numpy as jnp
from jax import lax
from jax.experimental import pallas as pl
from jax.experimental.pallas import tpu as pltpu
from jax.sharding import PartitionSpec as P

INNER = 3072
HEADS = 48
HEAD_DIM = 64
STATE = 128
CONV = 4
BLOCK_LEN = 256
CHANNELS = 3328
PROJ = 6448
EDGE = 16
GROUP = 4
GROUPS = HEADS // GROUP
GCOLS = GROUP * HEAD_DIM
PAIRS = GROUP // 2
STRIP = 128
PART = 64
MIXED_COLS = 128
LOG2E = 1.4426950408889634
F32 = jnp.float32
BF16 = jnp.bfloat16

NT = (((1,), (1,)), ((), ()))
TN = (((0,), (0,)), ((), ()))
NN = (((1,), (0,)), ((), ()))


def dot(a, b, dims=NN):
    return lax.dot_general(a, b, dims, preferred_element_type=F32)


def first_half(shape):
    return lax.broadcasted_iota(jnp.int32, shape, len(shape) - 1) < HEAD_DIM


def per_pair(cols, kind, pair, rows):
    at = kind * GROUP + 2 * pair
    left, right = cols[rows, at : at + 1], cols[rows, at + 1 : at + 2]
    shape = (left.shape[0], 2 * HEAD_DIM)
    return jnp.where(
        first_half(shape), jnp.broadcast_to(left, shape), jnp.broadcast_to(right, shape)
    )


def convolved(p_ref, w_ref, b_ref, lo, count, lanes):
    out = b_ref[0:1, lanes] + jnp.zeros((count, lanes.size), F32)
    for tap in range(CONV):
        at = EDGE - CONV + 1 + tap + lo
        out = out + p_ref[at : at + count, lanes] * w_ref[tap : tap + 1, lanes]
    return out


def sigmoid(v):
    return 0.5 + 0.5 * jnp.tanh(0.5 * v)


def softplus(v):
    return jnp.maximum(v, 0.0) + jnp.log1p(jnp.exp(-jnp.abs(v)))


def lower_triangle():
    row = lax.broadcasted_iota(jnp.int32, (BLOCK_LEN, BLOCK_LEN), 0)
    col = lax.broadcasted_iota(jnp.int32, (BLOCK_LEN, BLOCK_LEN), 1)
    return jnp.where(row >= col, 1.0, 0.0)


def exact_dot(a, b, dims=NN):
    return lax.dot_general(
        a, b, dims, precision=lax.Precision.HIGHEST, preferred_element_type=F32
    )


def steps_kernel(
    p_ref, w_ref, b_ref, bias_ref, decay_ref, cols_ref, rows_ref, maps_ref, er_ref, decays_ref
):
    positions = maps_ref.shape[0]
    blocks = positions // BLOCK_LEN
    lower = lower_triangle()
    used = lax.broadcasted_iota(jnp.int32, (1, 128), 1) < HEADS
    rate = -jnp.exp(decay_ref[...])
    total = jnp.zeros((1, 128), F32)
    for block in range(blocks):
        lo = block * BLOCK_LEN
        rows = slice(lo, lo + BLOCK_LEN)
        conv = convolved(p_ref, w_ref, b_ref, lo, BLOCK_LEN, pl.ds(0, 2 * STATE))
        maps_ref[rows, :] = (conv * sigmoid(conv)).astype(BF16)
        step = softplus(p_ref[EDGE + lo : EDGE + lo + BLOCK_LEN, 2 * STATE : 2 * STATE + 128] + bias_ref[...])
        step = jnp.where(used, step, 0.0)
        run = exact_dot(lower, rate * step)
        end = run[BLOCK_LEN - 1 :]
        total = total + end
        run2 = run * LOG2E
        grown = jnp.exp(run)
        er_ref[rows, :] = grown
        decays_ref[block : block + 1, :] = jnp.exp(end)
        turned = run2.T
        kinds = (step, run2, grown, jnp.exp(end - run))
        for group in range(GROUPS):
            heads = slice(group * GROUP, (group + 1) * GROUP)
            rows_ref[group, :, rows] = turned[heads]
            cols_ref[group, rows, :] = jnp.concatenate([kind[:, heads] for kind in kinds], axis=1)
    decays_ref[blocks : blocks + 1, :] = jnp.exp(total)
    decays_ref[blocks + 1 :, :] = jnp.zeros((8 - blocks - 1, 128), F32)


def steps_of(p, w, b, bias, decay_log, positions):
    ext = p.shape[0]
    at = INNER // PIECE
    return pl.pallas_call(
        steps_kernel,
        grid=(1,),
        in_specs=[
            pl.BlockSpec((ext, PIECE), lambda i: (0, at)),
            pl.BlockSpec((8, PIECE), lambda i: (0, at)),
            pl.BlockSpec((1, PIECE), lambda i: (0, at)),
            pl.BlockSpec((1, 128), lambda i: (0, 0)),
            pl.BlockSpec((1, 128), lambda i: (0, 0)),
        ],
        out_specs=[pl.BlockSpec(memory_space=pltpu.VMEM)] * 5,
        out_shape=[
            jax.ShapeDtypeStruct((GROUPS, positions, 4 * GROUP), F32),
            jax.ShapeDtypeStruct((GROUPS, GROUP, positions), F32),
            jax.ShapeDtypeStruct((positions, 2 * STATE), BF16),
            jax.ShapeDtypeStruct((positions, 128), F32),
            jax.ShapeDtypeStruct((8, 128), F32),
        ],
        compiler_params=pltpu.CompilerParams(vmem_limit_bytes=48 * 2**20),
        cost_estimate=pl.CostEstimate(
            flops=4 * positions * BLOCK_LEN * 128, bytes_accessed=16 * positions * 512,
            transcendentals=positions * 1024,
        ),
        name="steps",
    )(p, w, b, bias, decay_log)


def masked_scores(maps_ref, scores_ref, blocks):
    row = lax.broadcasted_iota(jnp.int32, (BLOCK_LEN, BLOCK_LEN), 0)
    col = lax.broadcasted_iota(jnp.int32, (BLOCK_LEN, BLOCK_LEN), 1)
    for block in range(blocks):
        rows = slice(block * BLOCK_LEN, (block + 1) * BLOCK_LEN)
        scores = dot(maps_ref[rows, STATE:], maps_ref[rows, :STATE], NT)
        scores_ref[block] = jnp.where(row >= col, scores, 0.0)


def chain_copy(site, group, by, sent, got, send_sem, recv_sem):
    return pltpu.make_async_remote_copy(
        src_ref=sent.at[group % sent.shape[0]], dst_ref=got.at[group], send_sem=send_sem.at[group],
        recv_sem=recv_sem.at[group], device_id=(site.over(by), site.f), device_id_type=MESH,
    )


def by_head(decays, group, kind, rows=GCOLS):
    return jnp.concatenate(
        [
            jnp.full((HEAD_DIM, STATE), decays[kind, group * GROUP + head], F32)
            for head in range(rows // HEAD_DIM)
        ],
        axis=0,
    )


def scan_forward_kernel(
    pieces, decays, p_ref, w_ref, b_ref, cols_ref, late_ref, rows_ref, maps_ref, skip_ref, normed_ref, own,
    y_ref, starts_ref, gate_ref, turned_ref, whole,
    scores_ref, x_ref, states_ref, weight_ref, weight_sem, sent, got, chain_send, chain_recv, *gather_refs,
):
    positions = y_ref.shape[0]
    blocks = positions // BLOCK_LEN
    step = pl.program_id(0)
    site = Site()
    behind = site.zs - 1

    @pl.when(step == 0)
    def _():
        site.greet()
        masked_scores(maps_ref, scores_ref, blocks)

    @pl.when(step == 1)
    def _():
        put_turned(normed_ref, own.shape[1], lambda at: turned_ref.at[at % 2, span_of(at // 2, own.shape[1])])

    gather = Gather(site, own, whole, *gather_refs)
    arrived = step - LAG * (gather.stages - 1)

    def weight_copy(piece):
        cols = pl.ds(pl.multiple_of(piece * PIECE, 128), PIECE)
        return pltpu.make_async_copy(whole.at[:, :, :, cols], weight_ref, weight_sem)

    @pl.when(jnp.logical_and(arrived >= 1, arrived <= pieces))
    def _():
        weight_copy(arrived - 1).wait()
        gate_ref[...] = dot(normed_ref[...], weight_ref[...].reshape(-1, PIECE)).astype(BF16)

    at_stages(gather.stages, pieces, LAG, step, gather.run)

    @pl.when(jnp.logical_and(arrived >= 0, arrived < pieces))
    def _():
        weight_copy(arrived).start()

    @pl.when(step < GROUPS)
    def _():
        slot = step % site.zs
        for pair in range(PAIRS):
            lanes = pl.ds(pair * 2 * HEAD_DIM, 2 * HEAD_DIM)
            for block in range(blocks):
                lo = block * BLOCK_LEN
                rows = slice(lo, lo + BLOCK_LEN)
                conv = convolved(p_ref, w_ref, b_ref, lo, BLOCK_LEN, lanes)
                x = conv * sigmoid(conv)
                x_ref[slot, rows, lanes] = x
                xs = x * per_pair(cols_ref, 0, pair, rows)
                ended = (xs * per_pair(cols_ref, 3, pair, rows)).astype(BF16)
                states_ref[slot, block, pair * 2 * HEAD_DIM : (pair + 1) * 2 * HEAD_DIM, :] = dot(
                    ended, maps_ref[rows, :STATE], TN
                )

    linked = step - site.z

    @pl.when(jnp.logical_and(linked >= 0, linked < GROUPS))
    def _():
        slot = linked % site.zs

        @pl.when(site.z == 0)
        def _():
            got[linked] = jnp.zeros((GCOLS, STATE), BF16)

        @pl.when(site.z > 0)
        def _():
            chain_copy(site, linked, 1, sent, got, chain_send, chain_recv).wait_recv()

        @pl.when(site.z < behind)
        def _():
            final = states_ref[slot, 0]
            for block in range(1, blocks):
                final = by_head(decays, linked, block) * final + states_ref[slot, block]
            sent[linked % sent.shape[0]] = (
                by_head(decays, linked, blocks) * got[linked].astype(F32) + final
            ).astype(BF16)
            chain_copy(site, linked, 1, sent, got, chain_send, chain_recv).start()

    group = step - behind

    @pl.when(jnp.logical_and(group >= 0, group < GROUPS))
    def _():
        slot = group % site.zs
        start = got[group].astype(F32)
        for block in range(blocks):
            if block:
                start = by_head(decays, group, block - 1) * start + states_ref[slot, block - 1]
            starts_ref[block] = start.astype(BF16)
        half = first_half((BLOCK_LEN, 2 * HEAD_DIM))
        for pair in range(PAIRS):
            lanes = pl.ds(pair * 2 * HEAD_DIM, 2 * HEAD_DIM)
            span = slice(pair * 2 * HEAD_DIM, (pair + 1) * 2 * HEAD_DIM)
            for block in range(blocks):
                lo = block * BLOCK_LEN
                rows = slice(lo, lo + BLOCK_LEN)
                x = x_ref[slot, rows, lanes]
                low = (x * per_pair(late_ref, 0, pair, rows)).astype(BF16)
                none = jnp.zeros_like(low)
                one, two = jnp.where(half, low, none), jnp.where(half, none, low)
                rest = skip_ref[0:1, lanes] * x + dot(
                    maps_ref[rows, STATE:], starts_ref[block, span, :], NT
                ) * per_pair(late_ref, 2, pair, rows)
                for strip in range(BLOCK_LEN // STRIP):
                    top = strip * STRIP
                    lim = top + STRIP
                    pieces_ = []
                    for side in range(2):
                        head = 2 * pair + side
                        at = GROUP + head
                        gap = (
                            late_ref[lo + top : lo + lim, at : at + 1]
                            - rows_ref[head : head + 1, lo : lo + lim]
                        )
                        decay = jnp.exp2(jnp.minimum(gap, 0.0))
                        pieces_.append((scores_ref[block, top:lim, :lim] * decay).astype(BF16))
                    y = dot(pieces_[0], one[:lim]) + dot(pieces_[1], two[:lim])
                    y_ref[lo + top : lo + lim, lanes] = y + rest[top:lim]

        @pl.when(site.z < behind)
        def _():
            chain_copy(site, group, 1, sent, got, chain_send, chain_recv).wait_send()


def span_of(at, rows):
    return slice(at * rows, (at + 1) * rows)


def put_turned(x_ref, rows, place, lanes=slice(None)):
    together = rows * 128 // math.gcd(rows, 128)
    for at in range(x_ref.shape[1] // together):
        turned = x_ref[:, span_of(at, together)].astype(F32).T
        for index in range(together // rows):
            place(at * (together // rows) + index)[:, lanes] = turned[span_of(index, rows)].astype(BF16)


def chain_scratch():
    ring = max(lax.axis_size("seq"), LAG + 2)
    return [
        pltpu.VMEM((ring, GCOLS, STATE), BF16),
        pltpu.VMEM((GROUPS, GCOLS, STATE), BF16),
        pltpu.SemaphoreType.DMA((GROUPS,)),
        pltpu.SemaphoreType.DMA((GROUPS,)),
    ]


def scan_forward(decays, p, w, b, cols, rows, maps, skip, normed, own, positions, collective_id):
    blocks = positions // BLOCK_LEN
    ext = p.shape[0]
    zs, n = lax.axis_size("seq"), lax.axis_size("fsdp")
    rows_there, columns = own.shape[1:]
    pieces = columns // PIECE
    wait = LAG * (stages_of(n) - 2) + 1
    steps = max(GROUPS + zs - 1, pieces + wait)

    def early(s):
        return jnp.minimum(s, GROUPS - 1)

    def late(s):
        return jnp.clip(s - (zs - 1), 0, GROUPS - 1)

    anywhere = pl.BlockSpec(memory_space=pl.ANY)
    return pl.pallas_call(
        functools.partial(scan_forward_kernel, pieces),
        grid=(steps,),
        in_specs=[
            pl.BlockSpec(memory_space=pltpu.SMEM),
            pl.BlockSpec((ext, GCOLS), lambda s: (0, early(s))),
            pl.BlockSpec((8, GCOLS), lambda s: (0, early(s))),
            pl.BlockSpec((1, GCOLS), lambda s: (0, early(s))),
            pl.BlockSpec((None, positions, 4 * GROUP), lambda s: (early(s), 0, 0)),
            pl.BlockSpec((None, positions, 4 * GROUP), lambda s: (late(s), 0, 0)),
            pl.BlockSpec((None, GROUP, positions), lambda s: (late(s), 0, 0)),
            pl.BlockSpec((positions, 2 * STATE), lambda s: (0, 0)),
            pl.BlockSpec((1, GCOLS), lambda s: (0, late(s))),
            pl.BlockSpec(normed.shape, lambda s: (0, 0), pipeline_mode=pl.Buffered(1)),
            anywhere,
        ],
        out_specs=[
            pl.BlockSpec((positions, GCOLS), lambda s: (0, late(s))),
            pl.BlockSpec((blocks, GCOLS, STATE), lambda s: (0, late(s), 0)),
            pl.BlockSpec((positions, PIECE), lambda s: (0, jnp.clip(s - wait, 0, pieces - 1))),
            pl.BlockSpec(
                (2, zs * n // 2 * rows_there, positions), lambda s: (0, 0, 0), pipeline_mode=pl.Buffered(1)
            ),
            anywhere,
        ],
        out_shape=[
            jax.ShapeDtypeStruct((positions, INNER), F32),
            jax.ShapeDtypeStruct((blocks, INNER, STATE), BF16),
            jax.ShapeDtypeStruct((positions, columns), BF16),
            jax.ShapeDtypeStruct((2, zs * n // 2 * rows_there, positions), BF16),
            jax.ShapeDtypeStruct((zs, n, rows_there, columns), BF16),
        ],
        scratch_shapes=[
            pltpu.VMEM((blocks, BLOCK_LEN, BLOCK_LEN), F32),
            pltpu.VMEM((zs, positions, GCOLS), F32),
            pltpu.VMEM((zs, blocks, GCOLS, STATE), F32),
            pltpu.VMEM((zs, n, rows_there, PIECE), BF16),
            pltpu.SemaphoreType.DMA,
        ]
        + chain_scratch()
        + gather_scratch(pieces),
        compiler_params=pltpu.CompilerParams(
            collective_id=collective_id, has_side_effects=True, vmem_limit_bytes=48 * 2**20
        ),
        cost_estimate=pl.CostEstimate(
            flops=12 * positions * INNER * BLOCK_LEN, bytes_accessed=24 * positions * INNER,
            transcendentals=HEADS * positions * BLOCK_LEN,
        ),
        name="scan_forward",
    )(decays, p, w, b, cols, cols, rows, maps, skip, normed, own)


def gate_kernel(
    y_ref, gate_ref, gno_ref, gain_ref, er_ref, maps_ref,
    out_ref, dy_ref, dye_ref, ggate_ref, ends_ref, *more_refs,
):
    gated_ref = more_refs[-1]
    rows = y_ref.shape[0]
    width = 2 * HEAD_DIM
    shape = (rows, width)
    square = jnp.zeros(shape, F32)
    cross = jnp.zeros(shape, F32)

    def decayed(pair):
        return jnp.where(
            first_half(shape),
            jnp.broadcast_to(er_ref[:, 2 * pair : 2 * pair + 1], shape),
            jnp.broadcast_to(er_ref[:, 2 * pair + 1 : 2 * pair + 2], shape),
        )

    for pair in range(HEADS // 2):
        lanes = slice(pair * width, (pair + 1) * width)
        gate = gate_ref[:, lanes].astype(F32)
        gated = y_ref[:, lanes] * gate * sigmoid(gate)
        gated_ref[:, lanes] = gated
        square = square + gated * gated
        cross = cross + gated * (gain_ref[:, lanes] * gno_ref[:, lanes].astype(F32))
    r1 = lax.rsqrt(jnp.sum(square, axis=-1, keepdims=True) * (1.0 / INNER) + 1e-05)
    back = r1 * r1 * r1 * (jnp.sum(cross, axis=-1, keepdims=True) * (1.0 / INNER))

    @pl.when(pl.program_id(0) % (BLOCK_LEN // rows) == 0)
    def _():
        ends_ref[...] = jnp.zeros_like(ends_ref)

    for pair in range(HEADS // 2):
        lanes = slice(pair * width, (pair + 1) * width)
        gate = gate_ref[:, lanes].astype(F32)
        sig = sigmoid(gate)
        gated = gated_ref[:, lanes]
        gain = gain_ref[:, lanes]
        out_ref[:, lanes] = (gated * r1 * gain).astype(BF16)
        ggated = gno_ref[:, lanes].astype(F32) * r1 * gain - gated * back
        low = (ggated * (gate * sig)).astype(BF16)
        dy_ref[:, lanes] = low
        ggate_ref[:, lanes] = (
            ggated * y_ref[:, lanes] * (sig * (1.0 + gate * (1.0 - sig)))
        ).astype(BF16)
        scaled = (low.astype(F32) * decayed(pair)).astype(BF16)
        dye_ref[:, lanes] = scaled
        ends_ref[lanes, :] += dot(scaled, maps_ref[:, STATE:], TN)

    if len(more_refs) == 2:
        turned_ref = more_refs[0]
        own_rows = INNER // (turned_ref.shape[0] * turned_ref.shape[1] * turned_ref.shape[2])

        def place(at):
            rest, split = at // OUT_SPLIT, at % OUT_SPLIT
            return turned_ref.at[split, rest % 2, rest // 2]

        put_turned(out_ref, own_rows, place)


def gated(y, gate, gno, gain, er, maps, own_rows):
    positions = y.shape[0]
    tile = 128
    per_block = BLOCK_LEN // tile
    wide = pl.BlockSpec((tile, INNER), lambda i: (i, 0))
    states = pl.BlockSpec((None, INNER, STATE), lambda i: (i // per_block, 0, 0))
    low = jax.ShapeDtypeStruct((positions, INNER), BF16)
    extra = []
    if own_rows:
        extra.append((OUT_SPLIT, 2, INNER // (2 * OUT_SPLIT * own_rows), own_rows, positions))
    return pl.pallas_call(
        gate_kernel,
        grid=(positions // tile,),
        in_specs=[
            wide,
            wide,
            wide,
            pl.BlockSpec((1, INNER), lambda i: (0, 0)),
            pl.BlockSpec((tile, 128), lambda i: (i, 0)),
            pl.BlockSpec((tile, 2 * STATE), lambda i: (i, 0)),
        ],
        out_specs=[wide] * 4
        + [states]
        + [pl.BlockSpec(turned[:-1] + (tile,), lambda i: (0, 0, 0, 0, i)) for turned in extra],
        out_shape=[
            low,
            low,
            low,
            low,
            jax.ShapeDtypeStruct((positions // BLOCK_LEN, INNER, STATE), F32),
        ]
        + [jax.ShapeDtypeStruct(turned, BF16) for turned in extra],
        scratch_shapes=[pltpu.VMEM((tile, INNER), F32)],
        compiler_params=pltpu.CompilerParams(vmem_limit_bytes=48 * 2**20),
        cost_estimate=pl.CostEstimate(
            flops=4 * positions * INNER * STATE, bytes_accessed=24 * positions * INNER,
            transcendentals=2 * positions * INNER,
        ),
        name="gate",
    )(y, gate, gno, gain, er, maps)


def scan_backward_kernel(
    branch, decays, p_ref, w_ref, b_ref, cols_ref, rows_ref, maps_ref, skip_ref, y_ref, dy_ref,
    dye_ref, st_ref, grads_ref, turned_ref, turned_out_ref, cot_ref, ggate_ref, wgate_ref, wconv_ref,
    plast_ref, wlast_ref, blast_ref, bias_ref, decay_ref, grown_ref, tokens_ref, gain_ref, *more_refs,
):
    if branch:
        nout_ref, wout_ref, *more_refs = more_refs
        mixed_ref = more_refs.pop(3)
        first = GROUPS + LAG + 1
        at = pl.program_id(0) - first

        @pl.when(jnp.logical_and(at >= 0, at < tokens_ref.shape[1] // MIXED_COLS))
        def _():
            lanes = pl.ds(pl.multiple_of(at * MIXED_COLS, 128), MIXED_COLS)
            mixed_ref[...] = (
                tokens_ref[:, lanes].astype(F32) + dot(nout_ref[...], wout_ref[...])
            ).astype(BF16)

    scan_backward_steps(
        decays, p_ref, w_ref, b_ref, cols_ref, rows_ref, maps_ref, skip_ref, y_ref, dy_ref,
        dye_ref, st_ref, grads_ref, turned_ref, turned_out_ref, cot_ref, ggate_ref, wgate_ref, wconv_ref,
        plast_ref, wlast_ref, blast_ref, bias_ref, decay_ref, grown_ref, tokens_ref, gain_ref, *more_refs,
    )


def scan_backward_steps(
    decays, p_ref, w_ref, b_ref, cols_ref, rows_ref, maps_ref, skip_ref, y_ref, dy_ref,
    dye_ref, st_ref, grads_ref, turned_ref, turned_out_ref, cot_ref, ggate_ref, wgate_ref, wconv_ref,
    plast_ref, wlast_ref, blast_ref, bias_ref, decay_ref, grown_ref, tokens_ref, gain_ref,
    own_ref, gtokens_ref, total_ref,
    scores_ref, dscores_ref, dpad_ref, gacc_ref, dl_ref, x_ref, tail_ref, runs_ref, direct_ref, ends_ref,
    cross_ref, conv_ref, inner_ref, outer_ref, low_ref, ended_ref, sent, got, chain_send, chain_recv,
    edge_sent, edge_got, edge_send, edge_recv, t_sent, t_got, t_send, t_recv, *scatter_refs,
):
    step_at = pl.program_id(0)
    site = Site()
    behind = site.zs - 1
    positions = y_ref.shape[0]
    gates = INNER // PIECE
    ahead = PIECE // GCOLS
    later = step_at - OUT_PIECES

    @pl.when(step_at == 0)
    def _():
        site.greet()
        gtokens_ref[...] = jnp.zeros_like(gtokens_ref)
        runs_ref[...] = jnp.zeros_like(runs_ref)
        direct_ref[...] = jnp.zeros_like(direct_ref)
        t_sent[0, CONV + 1 :, 0:INNER] = jnp.zeros((8 - CONV - 1, INNER), F32)

    def edge_copy(group):
        return pltpu.make_async_remote_copy(
            src_ref=edge_sent.at[group], dst_ref=edge_got.at[group], send_sem=edge_send.at[group],
            recv_sem=edge_recv.at[group], device_id=(site.over(behind), site.f), device_id_type=MESH,
        )

    def add_normed(weight_ref, grads_of):
        def one(i, carry):
            span = pl.ds(pl.multiple_of(i * PIECE, 128), PIECE)
            gtokens_ref[:, span] += dot(grads_of(), weight_ref[span, :], NT)
            return carry

        lax.fori_loop(0, gtokens_ref.shape[1] // PIECE, one, 0)

    @pl.when(step_at < OUT_PIECES)
    def _():
        cots = cot_ref.shape[1] // PIECE
        span = pl.ds(pl.multiple_of((step_at % cots) * PIECE, 128), PIECE)
        x_ref[step_at % XRING] = cot_ref[:, span]

    inside = jnp.logical_and(later >= 0, later < 2 * gates)

    @pl.when(jnp.logical_and(inside, later % 2 == 1))
    def _():
        x_ref[step_at % XRING] = ggate_ref[...]

    @pl.when(jnp.logical_and(inside, later % 2 == 0))
    def _():
        for side in range(ahead):
            group = (later // 2) * ahead + side
            lanes = slice(side * GCOLS, (side + 1) * GCOLS)

            @pl.when(site.z < behind)
            def _(group=group, lanes=lanes):
                edge_copy(group).wait_recv()
                x_ref[step_at % XRING, positions - 8 :, lanes] = (
                    tail_ref[group] + edge_got[group]
                ).astype(BF16)

            @pl.when(site.z > 0)
            def _(group=group):
                edge_copy(group).wait_send()

        add_normed(wconv_ref, lambda: x_ref[step_at % XRING])

    last = OUT_PIECES + 2 * gates
    start = last - LAG - 1
    slot = last % XRING
    wide = 2 * STATE
    totals = Totals(site, t_sent, t_got, t_send, t_recv)

    def last_edge():
        return pltpu.make_async_remote_copy(
            src_ref=edge_sent.at[GROUPS], dst_ref=edge_got.at[GROUPS], send_sem=edge_send.at[GROUPS],
            recv_sem=edge_recv.at[GROUPS], device_id=(site.over(behind), site.f), device_id_type=MESH,
        )

    @pl.when(step_at == start)
    def _():
        tail, edge = maps_backward(plast_ref, wlast_ref, blast_ref, gacc_ref, dpad_ref, x_ref, slot, t_sent)
        tail_ref[GROUPS] = tail
        edge_sent[GROUPS] = edge

        @pl.when(site.z > 0)
        def _():
            last_edge().start()

        steps_backward(
            plast_ref, bias_ref, decay_ref, grown_ref, runs_ref, direct_ref, ends_ref, cross_ref, x_ref, slot,
            t_sent,
        )
        totals.start(0)

    for t in range(totals.count):

        @pl.when(step_at == start + 1 + t)
        def _(t=t):
            totals.next(t)

    @pl.when(step_at == start + 1 + totals.count)
    def _():
        total_ref[...] = t_sent[totals.count % 2]

    @pl.when(step_at == last)
    def _():
        @pl.when(site.z < behind)
        def _():
            last_edge().wait_recv()
            x_ref[slot, positions - 8 :, 0:wide] = (tail_ref[GROUPS] + edge_got[GROUPS]).astype(BF16)

        @pl.when(site.z > 0)
        def _():
            last_edge().wait_send()

        add_normed(wconv_ref, lambda: x_ref[step_at % XRING])

    after = step_at - last - 1

    @pl.when(jnp.logical_and(after >= 0, after < gates))
    def _():
        add_normed(wgate_ref, lambda: ggate_ref[...])

    tile = 128

    @pl.when(jnp.logical_and(after >= gates, after < gates + positions // (2 * tile)))
    def _():
        def one(i, carry):
            rows = pl.ds(pl.multiple_of((after - gates) * 2 * tile + i * tile, tile), tile)
            features = gtokens_ref.shape[1]
            inputs = tokens_ref[rows, :].astype(F32)
            r0 = lax.rsqrt(jnp.sum(inputs * inputs, axis=-1, keepdims=True) * (1.0 / features) + 1e-05)
            f = gain_ref[...] * gtokens_ref[rows, :]
            share = r0 * r0 * r0 * (jnp.sum(f * inputs, axis=-1, keepdims=True) * (1.0 / features))
            gtokens_ref[rows, :] = cot_ref[rows, :].astype(F32) + r0 * f - inputs * share
            return carry

        lax.fori_loop(0, 2, one, 0)

    def is_later(piece):
        return jnp.minimum(piece, OUT_PIECES) // OUT_PIECES

    def column(piece):
        after = jnp.maximum(piece - OUT_PIECES, 0)
        return jnp.minimum(piece, OUT_PIECES) + is_later(piece) * (1 - after % 2) * gates + after // 2

    scatter = Streamed(site, turned_ref, turned_out_ref, is_later, x_ref, own_ref, column, scatter_refs)
    at_stages(scatter.stages, last + 1, LAG, step_at, scatter.run)

    linked = step_at - (behind - site.z)
    blocks = positions // BLOCK_LEN

    @pl.when(jnp.logical_and(linked >= 0, linked < GROUPS))
    def _():
        @pl.when(site.z == behind)
        def _():
            got[linked] = jnp.zeros((GCOLS, STATE), BF16)

        @pl.when(site.z < behind)
        def _():
            chain_copy(site, linked, behind, sent, got, chain_send, chain_recv).wait_recv()

        @pl.when(site.z > 0)
        def _():
            span = pl.ds(pl.multiple_of(linked * GCOLS, GCOLS), GCOLS)
            grad = got[linked].astype(F32)
            for block in reversed(range(blocks)):
                grad = by_head(decays, linked, block) * grad + grads_ref[block, span, :]
            sent[linked % sent.shape[0]] = grad.astype(BF16)
            chain_copy(site, linked, behind, sent, got, chain_send, chain_recv).start()

    group = step_at - max(behind, LAG + 1)

    @pl.when(jnp.logical_and(group >= 0, group < GROUPS))
    def _():
        scan_backward_group(
            group, decays, p_ref, w_ref, b_ref, cols_ref, rows_ref, maps_ref, skip_ref, y_ref,
            dy_ref, dye_ref, st_ref, grads_ref, x_ref, tail_ref, edge_sent, t_sent, runs_ref, direct_ref,
            ends_ref, cross_ref, scores_ref, dscores_ref, dpad_ref, gacc_ref, dl_ref, got, conv_ref, inner_ref,
            outer_ref, low_ref, ended_ref,
        )

        @pl.when(site.z > 0)
        def _():
            edge_copy(group).start()
            chain_copy(site, group, behind, sent, got, chain_send, chain_recv).wait_send()


def maps_backward(p_ref, w_ref, b_ref, grad_ref, dpad_ref, x_ref, slot, t_sent):
    positions, wide = grad_ref.shape
    blocks = positions // BLOCK_LEN
    lanes = pl.ds(0, wide)
    taps = [jnp.zeros((1, wide), F32) for _ in range(CONV + 1)]
    for block in range(blocks):
        lo = block * BLOCK_LEN
        conv = convolved(p_ref, w_ref, b_ref, lo, BLOCK_LEN, lanes)
        sig = sigmoid(conv)
        dconv = grad_ref[lo : lo + BLOCK_LEN, :] * (sig * (1.0 + conv * (1.0 - sig)))
        dpad_ref[8 + lo : 8 + lo + BLOCK_LEN, :] = dconv
        for tap in range(CONV):
            at = EDGE - CONV + 1 + tap + lo
            taps[tap] = taps[tap] + jnp.sum(
                dconv * p_ref[at : at + BLOCK_LEN, 0:wide], axis=0, keepdims=True
            )
        taps[CONV] = taps[CONV] + jnp.sum(dconv, axis=0, keepdims=True)
    for index in range(CONV + 1):
        t_sent[0, index : index + 1, INNER : INNER + wide] = taps[index]
    t_sent[0, CONV + 1 :, INNER : INNER + wide] = jnp.zeros((8 - CONV - 1, wide), F32)

    def back_rows(at, count):
        back = jnp.zeros((count, wide), F32)
        for tap in range(CONV):
            start = at + CONV - 1 - tap
            back = back + dpad_ref[start : start + count, :] * w_ref[tap : tap + 1, 0:wide]
        return back

    for block in range(blocks):
        lo = block * BLOCK_LEN
        x_ref[slot, lo : lo + BLOCK_LEN, 0:wide] = back_rows(8 + lo, BLOCK_LEN).astype(BF16)
    return back_rows(positions, 8), back_rows(0, 8)


def steps_backward(
    p_ref, bias_ref, decay_ref, decays_ref, runs_ref, direct_ref, ends_ref, cross_ref, x_ref, slot, t_sent
):
    positions = runs_ref.shape[0]
    blocks = positions // BLOCK_LEN
    wide = 2 * STATE
    used = lax.broadcasted_iota(jnp.int32, (1, 128), 1) < HEADS
    rate = -jnp.exp(decay_ref[...])
    by_heads = jnp.zeros((8, 128), F32)
    for at in range(0, INNER, PIECE):
        spread = jnp.where(
            (at + lax.broadcasted_iota(jnp.int32, (PIECE, 128), 0)) // HEAD_DIM
            == lax.broadcasted_iota(jnp.int32, (PIECE, 128), 1),
            1.0,
            0.0,
        )
        by_heads = by_heads + exact_dot(ends_ref[:, at : at + PIECE], spread)
    per_group = blocks * GROUP
    crossed = jnp.sum(cross_ref[...].reshape(GROUPS * per_group, STATE), axis=1, keepdims=True)
    row = lax.broadcasted_iota(jnp.int32, (GROUPS * per_group, 128), 0)
    lane = lax.broadcasted_iota(jnp.int32, (GROUPS * per_group, 128), 1)
    same = (row // per_group) * GROUP + row % GROUP == lane
    tri_row = lax.broadcasted_iota(jnp.int32, (BLOCK_LEN, BLOCK_LEN), 0)
    tri_col = lax.broadcasted_iota(jnp.int32, (BLOCK_LEN, BLOCK_LEN), 1)
    upper = jnp.where(tri_row <= tri_col, 1.0, 0.0)
    grad_bias = jnp.zeros((1, 128), F32)
    grad_decay = jnp.zeros((1, 128), F32)
    for block in range(blocks):
        lo = block * BLOCK_LEN
        rows = slice(lo, lo + BLOCK_LEN)
        here = jnp.logical_and(same, (row % per_group) // GROUP == block)
        end = by_heads[block : block + 1] + decays_ref[block : block + 1, :] * jnp.sum(
            jnp.where(here, crossed, 0.0), axis=0, keepdims=True
        )
        arg = p_ref[EDGE + lo : EDGE + lo + BLOCK_LEN, wide : wide + 128] + bias_ref[...]
        step = softplus(arg)
        grad_log = exact_dot(upper, runs_ref[rows, :]) + end
        grad_step = jnp.where(used, (direct_ref[rows, :] + rate * grad_log) * sigmoid(arg), 0.0)
        grad_bias = grad_bias + jnp.sum(grad_step, axis=0, keepdims=True)
        grad_decay = grad_decay + jnp.sum(
            jnp.where(used, grad_log * (rate * step), 0.0), axis=0, keepdims=True
        )
        x_ref[slot, rows, wide : wide + 128] = grad_step.astype(BF16)
        x_ref[slot, rows, wide + 128 :] = jnp.zeros((BLOCK_LEN, PIECE - wide - 128), BF16)
    t_sent[0, :, INNER + wide :] = jnp.concatenate(
        [grad_bias, grad_decay, by_heads[blocks : blocks + 1], jnp.zeros((5, 128), F32)], axis=0
    )


def scan_backward_group(
    step_at, decays, p_ref, w_ref, b_ref, cols_ref, rows_ref, maps_ref, skip_ref, y_ref, dy_ref,
    dye_ref, st_ref, grads_ref, x_ref, tail_ref, edge_ref, t_sent, runs_ref, direct_ref, ends_ref,
    cross_ref, scores_ref, dscores_ref, dpad_ref, gacc_ref, dl_ref, got, conv_ref, inner_ref, outer_ref,
    low_ref, ended_ref,
):
    positions = y_ref.shape[0]
    blocks = positions // BLOCK_LEN
    width = 2 * HEAD_DIM

    @pl.when(step_at == 0)
    def _():
        masked_scores(maps_ref, scores_ref, blocks)
        ends_ref[...] = jnp.zeros_like(ends_ref)
        dscores_ref[...] = jnp.zeros_like(dscores_ref)
        gacc_ref[...] = jnp.zeros_like(gacc_ref)
        dpad_ref[0:8, :] = jnp.zeros((8, GCOLS), F32)
        dpad_ref[positions + 8 : positions + 16, :] = jnp.zeros((8, GCOLS), F32)

    ahead = PIECE // GCOLS
    slot = (OUT_PIECES + 2 * (step_at // ahead)) % XRING
    offset = (step_at % ahead) * GCOLS
    group_span = pl.ds(pl.multiple_of(step_at * GCOLS, GCOLS), GCOLS)
    grad = got[step_at].astype(F32)
    for block in reversed(range(blocks)):
        if block < blocks - 1:
            grad = by_head(decays, step_at, block + 1) * grad + grads_ref[block + 1, group_span, :]
        dl_ref[block] = grad.astype(BF16)
        product = grad * st_ref[block].astype(F32)
        for head in range(GROUP):
            at = block * GROUP + head
            cross_ref[step_at, at : at + 1, :] = jnp.sum(
                product[head * HEAD_DIM : (head + 1) * HEAD_DIM], axis=0, keepdims=True
            )

    half = first_half((BLOCK_LEN, width))
    lane_row = lax.broadcasted_iota(jnp.int32, (width, 128), 0)
    lane_col = lax.broadcasted_iota(jnp.int32, (width, 128), 1)
    gw = [[jnp.zeros((8, width), F32) for _ in range(CONV + 2)] for _ in range(PAIRS)]
    for block in range(blocks):
        lo = block * BLOCK_LEN
        rows = slice(lo, lo + BLOCK_LEN)
        outer_ref[...] = dot(maps_ref[rows, :STATE], dl_ref[block], NT)
        for pair in range(PAIRS):
            lanes = pl.ds(pair * width, width)
            for top in range(0, BLOCK_LEN, PART):
                part = slice(lo + top, lo + top + PART)
                here = slice(top, top + PART)
                conv = convolved(p_ref, w_ref, b_ref, lo + top, PART, lanes)
                conv_ref[here, :] = conv
                xs = conv * sigmoid(conv) * per_pair(cols_ref, 0, pair, part)
                low_ref[here, :] = xs.astype(BF16)
                ended_ref[here, lanes] = (xs * per_pair(cols_ref, 3, pair, part)).astype(BF16)
            dyl = dy_ref[rows, lanes]
            none = jnp.zeros_like(dyl)
            sides = (jnp.where(half, dyl, none), jnp.where(half, none, dyl))
            turned = dyl.astype(F32).T.astype(BF16)
            dxt = [None, None]
            for strip in range(BLOCK_LEN // STRIP):
                top = strip * STRIP
                lim = top + STRIP
                scores = scores_ref[block, top:lim, :lim]
                gathered = jnp.zeros((STRIP, lim), F32)
                for side in range(2):
                    head = 2 * pair + side
                    at = GROUP + head
                    gap = (
                        cols_ref[lo + top : lo + lim, at : at + 1]
                        - rows_ref[head : head + 1, lo : lo + lim]
                    )
                    decay = jnp.exp2(jnp.minimum(gap, 0.0))
                    gathered = gathered + dot(sides[side][top:lim], low_ref[:lim, :], NT) * decay
                    part = dot(
                        turned[side * HEAD_DIM : (side + 1) * HEAD_DIM, top:lim],
                        (scores * decay).astype(BF16),
                    )
                    if strip == 0:
                        dxt[side] = jnp.concatenate(
                            [part, jnp.zeros((HEAD_DIM, BLOCK_LEN - STRIP), F32)], axis=1
                        )
                    else:
                        dxt[side] = dxt[side] + part
                dscores_ref[block, top:lim, :lim] += gathered
            inner_ref[...] = jnp.concatenate(dxt, axis=0).T
            skip = skip_ref[0:1, lanes]
            at = step_at * GROUP + 2 * pair
            heads_of = jnp.where(lane_col == at + lane_row // HEAD_DIM, 1.0, 0.0).astype(BF16)
            ends = jnp.zeros((8, width), F32)

            def folded(values):
                return jnp.sum(values.reshape(PART // 8, 8, width), axis=0)

            for top in range(0, BLOCK_LEN, PART):
                part = slice(lo + top, lo + top + PART)
                here = slice(top, top + PART)
                conv = conv_ref[here, :]
                sig = sigmoid(conv)
                x = conv * sig
                step = per_pair(cols_ref, 0, pair, part)
                inner = inner_ref[here, :]
                outer = outer_ref[here, lanes] * per_pair(cols_ref, 3, pair, part)
                dyf = dy_ref[part, lanes].astype(F32)
                dxs = inner + outer
                vs = x * step * outer
                ends = ends + folded(vs)
                runs = dyf * (y_ref[part, lanes] - skip * x) - low_ref[here, :].astype(F32) * inner - vs
                for sums_ref, values in ((runs_ref, runs), (direct_ref, x * dxs)):
                    high = values.astype(BF16)
                    rest = (values - high.astype(F32)).astype(BF16)
                    sums_ref[part, :] += dot(high, heads_of) + dot(rest, heads_of)
                gw[pair][CONV + 1] = gw[pair][CONV + 1] + folded(dyf * x)
                dconv = (dxs * step + skip * dyf) * (sig * (1.0 + conv * (1.0 - sig)))
                gw[pair][CONV] = gw[pair][CONV] + folded(dconv)
                dpad_ref[8 + lo + top : 8 + lo + top + PART, lanes] = dconv
                for tap in range(CONV):
                    first = EDGE - CONV + 1 + tap + lo + top
                    gw[pair][tap] = gw[pair][tap] + folded(dconv * p_ref[first : first + PART, lanes])
            group_lanes = pl.ds(pl.multiple_of(step_at * GCOLS + pair * width, width), width)
            ends_ref[block : block + 1, group_lanes] = jnp.sum(ends, axis=0, keepdims=True)
        gacc_ref[rows, :STATE] += dot(ended_ref[...], dl_ref[block])
        gacc_ref[rows, STATE:] += dot(dye_ref[rows, :], st_ref[block])

    for pair in range(PAIRS):
        lanes = pl.ds(pair * width, width)
        group_lanes = pl.ds(pl.multiple_of(step_at * GCOLS + pair * width, width), width)
        for index in range(CONV + 1):
            t_sent[0, index : index + 1, group_lanes] = jnp.sum(gw[pair][index], axis=0, keepdims=True)
        ends_ref[blocks : blocks + 1, group_lanes] = jnp.sum(gw[pair][CONV + 1], axis=0, keepdims=True)
        edge = jnp.zeros((8, width), F32)
        for tap in range(CONV):
            edge = edge + dpad_ref[CONV - 1 - tap : CONV - 1 - tap + 8, lanes] * w_ref[tap : tap + 1, lanes]
        edge_ref[step_at, :, lanes] = edge
        for top in range(0, positions, PART):
            back = jnp.zeros((PART, width), F32)
            for tap in range(CONV):
                at = 8 + CONV - 1 - tap + top
                back = back + dpad_ref[at : at + PART, lanes] * w_ref[tap : tap + 1, lanes]
            x_ref[slot, top : top + PART, pl.ds(pl.multiple_of(offset + pair * width, width), width)] = (
                back.astype(BF16)
            )
        tail_ref[step_at, :, lanes] = back[PART - 8 :]

    @pl.when(step_at == GROUPS - 1)
    def _():
        row = lax.broadcasted_iota(jnp.int32, (BLOCK_LEN, BLOCK_LEN), 0)
        col = lax.broadcasted_iota(jnp.int32, (BLOCK_LEN, BLOCK_LEN), 1)
        for block in range(blocks):
            rows = slice(block * BLOCK_LEN, (block + 1) * BLOCK_LEN)
            low = jnp.where(row >= col, dscores_ref[block], 0.0).astype(BF16)
            gacc_ref[rows, :STATE] += dot(low, maps_ref[rows, STATE:], TN)
            gacc_ref[rows, STATE:] += dot(low, maps_ref[rows, :STATE])


def scan_backward(
    decays, p, w, b, cols, rows, maps, skip, y, dy, dye, starts, ends, turned, turned_out, cot, grad_gate,
    inw_gate, inw_conv, bias, decay_log, tokens, gain, own_rows, collective_id, *factors,
):
    branch = len(factors) == 2
    positions = y.shape[0]
    features = inw_gate.shape[0]
    blocks = positions // BLOCK_LEN
    ext = p.shape[0]
    zs, n = lax.axis_size("seq"), lax.axis_size("fsdp")
    gates = INNER // PIECE
    pieces = OUT_PIECES + 2 * gates + 1
    count = exchange_count(zs, n)
    steps = pieces + max(LAG * (stages_of(n) - 1), count - LAG, gates + positions // 256)
    width = CHANNELS + 128
    dma = pltpu.SemaphoreType.DMA

    def late(s):
        return jnp.clip(s - max(zs - 1, LAG + 1), 0, GROUPS - 1)

    def turn(s, most):
        return jnp.clip((s - OUT_PIECES) // 2, 0, most)

    def gate_turn(s):
        again = jnp.maximum(s - pieces + 1, 0)
        return turn(s - 1, gates - 1) * (1 - jnp.minimum(again, 1)) + jnp.clip(again - 1, 0, gates - 1)

    once = pl.Buffered(1)
    own = pl.BlockSpec((positions, GCOLS), lambda s: (0, late(s)))
    eight = pl.BlockSpec((8, GCOLS), lambda s: (0, late(s)))
    states = pl.BlockSpec((blocks, GCOLS, STATE), lambda s: (0, late(s), 0))

    def whole(x):
        return pl.BlockSpec(x.shape, lambda s: (0,) * len(x.shape), pipeline_mode=once)

    more_in, more_out, more_shapes = [], [], []
    if branch:
        steps = max(steps, GROUPS + LAG + 1 + features // MIXED_COLS)

        def mixing(s):
            return 0, jnp.clip(s - (GROUPS + LAG + 1), 0, features // MIXED_COLS - 1)

        more_in = [whole(factors[0]), pl.BlockSpec((INNER, MIXED_COLS), mixing)]
        more_out = [pl.BlockSpec((positions, MIXED_COLS), mixing)]
        more_shapes = [jax.ShapeDtypeStruct((positions, features), BF16)]

    return pl.pallas_call(
        functools.partial(scan_backward_kernel, branch),
        grid=(steps,),
        in_specs=[
            pl.BlockSpec(memory_space=pltpu.SMEM),
            pl.BlockSpec((ext, GCOLS), lambda s: (0, late(s))),
            eight,
            pl.BlockSpec((1, GCOLS), lambda s: (0, late(s))),
            pl.BlockSpec((None, positions, 4 * GROUP), lambda s: (late(s), 0, 0)),
            pl.BlockSpec((None, GROUP, positions), lambda s: (late(s), 0, 0)),
            whole(maps),
            pl.BlockSpec((1, GCOLS), lambda s: (0, late(s))),
            own,
            own,
            own,
            states,
            whole(ends),
            whole(turned),
            whole(turned_out),
            whole(cot),
            pl.BlockSpec((positions, PIECE), lambda s: (0, gate_turn(s))),
            pl.BlockSpec((features, PIECE), lambda s: (0, jnp.clip(s - pieces, 0, gates - 1))),
            pl.BlockSpec((features, PIECE), lambda s: (0, turn(s, gates))),
            pl.BlockSpec((ext, PIECE), lambda s: (0, gates), pipeline_mode=once),
            pl.BlockSpec((8, PIECE), lambda s: (0, gates), pipeline_mode=once),
            pl.BlockSpec((1, PIECE), lambda s: (0, gates), pipeline_mode=once),
            whole(bias),
            whole(decay_log),
            whole(decays),
            whole(tokens),
            whole(gain),
        ]
        + more_in,
        out_specs=[
            pl.BlockSpec((own_rows, pieces * PIECE), lambda s: (0, 0), pipeline_mode=once),
            pl.BlockSpec((positions, features), lambda s: (0, 0), pipeline_mode=once),
            pl.BlockSpec((8, width), lambda s: (0, 0), pipeline_mode=once),
        ]
        + more_out,
        out_shape=[
            jax.ShapeDtypeStruct((own_rows, pieces * PIECE), F32),
            jax.ShapeDtypeStruct((positions, features), F32),
            jax.ShapeDtypeStruct((8, width), F32),
        ]
        + more_shapes,
        scratch_shapes=[
            pltpu.VMEM((blocks, BLOCK_LEN, BLOCK_LEN), F32),
            pltpu.VMEM((blocks, BLOCK_LEN, BLOCK_LEN), F32),
            pltpu.VMEM((positions + 16, GCOLS), F32),
            pltpu.VMEM((positions, 2 * STATE), F32),
            pltpu.VMEM((blocks, GCOLS, STATE), BF16),
            pltpu.VMEM((XRING, positions, PIECE), BF16),
            pltpu.VMEM((GROUPS + 1, 8, GCOLS), F32),
            pltpu.VMEM((positions, 128), F32),
            pltpu.VMEM((positions, 128), F32),
            pltpu.VMEM((8, INNER), F32),
            pltpu.VMEM((GROUPS, blocks * GROUP, STATE), F32),
            pltpu.VMEM((BLOCK_LEN, 2 * HEAD_DIM), F32),
            pltpu.VMEM((BLOCK_LEN, 2 * HEAD_DIM), F32),
            pltpu.VMEM((BLOCK_LEN, GCOLS), F32),
            pltpu.VMEM((BLOCK_LEN, 2 * HEAD_DIM), BF16),
            pltpu.VMEM((BLOCK_LEN, GCOLS), BF16),
        ]
        + chain_scratch()
        + [
            pltpu.VMEM((GROUPS + 1, 8, GCOLS), F32),
            pltpu.VMEM((GROUPS + 1, 8, GCOLS), F32),
            dma((GROUPS + 1,)),
            dma((GROUPS + 1,)),
            pltpu.VMEM((2, 8, width), F32),
            pltpu.VMEM((count, 8, width), F32),
            dma((count,)),
            dma((count,)),
        ]
        + Streamed.scratch(own_rows),
        compiler_params=pltpu.CompilerParams(
            collective_id=collective_id, has_side_effects=True, vmem_limit_bytes=63 * 2**20
        ),
        cost_estimate=pl.CostEstimate(
            flops=24 * positions * INNER * BLOCK_LEN, bytes_accessed=30 * positions * INNER,
            transcendentals=HEADS * positions * BLOCK_LEN,
        ),
        name="scan_backward",
    )(
        decays, p, w, b, cols, rows, maps, skip, y, dy, dye, starts, ends, turned, turned_out, cot, grad_gate,
        inw_gate, inw_conv, p, w, b, bias, decay_log, decays, tokens, gain, *factors,
    )


PIECE = 512
LAG = 2
HALF = PIECE // 2
MESH = pl.DeviceIdType.MESH


class Site:
    def __init__(self):
        self.zs, self.n = lax.axis_size("seq"), lax.axis_size("fsdp")
        self.z, self.f = lax.axis_index("seq"), lax.axis_index("fsdp")
        self.chips = self.n // 2
        self.bits = self.chips.bit_length() - 1

    def bit(self, j):
        return (self.f // 2**j) % 2

    def flip(self, js):
        f = self.f
        for j in js:
            f = f + (1 - 2 * self.bit(j)) * 2**j
        return f

    def over(self, dz):
        return (self.z + dz) % self.zs

    def greet(self):
        barrier = pltpu.get_barrier_semaphore()
        for dz in range(1, self.zs):
            pl.semaphore_signal(barrier, inc=1, device_id=(self.over(dz), self.f), device_id_type=MESH)
        for j in range(self.bits + 1):
            pl.semaphore_signal(barrier, inc=1, device_id=(self.z, self.flip([j])), device_id_type=MESH)
        pl.semaphore_wait(barrier, self.zs + self.bits)


def subsets(js):
    found = [()]
    for j in js:
        found = found + [s + (j,) for s in found]
    return found


class Gather:
    def __init__(self, site, own, whole, local_sem, send_sem, recv_sem):
        self.site, self.own, self.whole = site, own, whole
        self.local_sem, self.send_sem, self.recv_sem = local_sem, send_sem, recv_sem
        self.along = len(own.shape) == 2
        self.skipped = 0 if self.along else 1
        self.stages = site.bits + 3 - self.skipped

    @staticmethod
    def slots(zs, n):
        return zs + 4 * (n // 2 - 1)

    def moves(self, piece):
        s = self.site
        start = piece * PIECE
        whole = pl.ds(pl.multiple_of(start, 128), PIECE)
        halves = (
            pl.ds(pl.multiple_of(start, 128), HALF),
            pl.ds(pl.multiple_of(start + HALF, 128), HALF),
        )
        slot = 0
        plan = [[] for _ in range(s.bits + 3)]
        for dz in range(1, s.zs):
            if not self.along:
                slot += 1
                continue
            plan[0].append(
                (slot, self.own.at[:, whole], self.whole.at[s.z, s.f, :, whole],
                 (s.over(dz), s.f), self.whole.at[s.over(s.zs - dz), s.f, :, whole])
            )
            slot += 1
        sibling = s.flip([0])

        def known(js, cols):
            if not js and not self.along:
                return self.own.at[:, :, cols]
            return self.whole.at[:, s.flip(js), :, cols]

        def shared(js, cols):
            return (slot, known(js, cols), self.whole.at[:, s.flip(js), :, cols],
                    (s.z, sibling), self.whole.at[:, s.flip(list(js) + [0]), :, cols])

        plan[1].append(shared([], whole))
        slot += 1
        up = list(range(1, s.bits + 1))
        for half, order in enumerate((up, up[::-1])):
            cols = halves[half]
            for at, j in enumerate(order):
                for js in subsets(order[:at]):
                    js = list(js)
                    plan[at + 1].append(
                        (slot, known(js, cols), self.whole.at[:, s.flip(js), :, cols],
                         (s.z, s.flip([j])), self.whole.at[:, s.flip(js + [j]), :, cols])
                    )
                    slot += 1
                    plan[at + 2].append(shared(js + [j], cols))
                    slot += 1
        return plan[self.skipped :]

    def leaving(self, piece, moves):
        return [
            pltpu.make_async_remote_copy(
                src_ref=src, dst_ref=dst, send_sem=self.send_sem.at[piece, slot],
                recv_sem=self.recv_sem.at[piece, slot], device_id=device, device_id_type=MESH,
            )
            for slot, src, dst, device, _ in moves
        ]

    def arriving(self, piece, moves):
        return [
            pltpu.make_async_remote_copy(
                src_ref=src, dst_ref=incoming, send_sem=self.send_sem.at[piece, slot],
                recv_sem=self.recv_sem.at[piece, slot], device_id=device, device_id_type=MESH,
            )
            for slot, src, _, device, incoming in moves
        ]

    def run(self, stage, piece):
        s = self.site
        plan = self.moves(piece)
        cols = pl.ds(pl.multiple_of(piece * PIECE, 128), PIECE)

        def local():
            if self.along:
                src, dst = self.own.at[:, cols], self.whole.at[s.z, s.f, :, cols]
            else:
                src, dst = self.own.at[:, :, cols], self.whole.at[:, s.f, :, cols]
            return pltpu.make_async_copy(src, dst, self.local_sem.at[piece])

        to_core = [[m for m in moves if self.is_core(stage_at, m)] for stage_at, moves in enumerate(plan)]
        others = [[m for m in moves if not self.is_core(stage_at, m)] for stage_at, moves in enumerate(plan)]
        if stage == 0:
            local().start()
        if stage == 1:
            local().wait()
        if 0 < stage:
            for copy in self.arriving(piece, others[stage - 1]):
                copy.wait_recv()
        if stage < self.stages - 1:
            for copy in self.leaving(piece, others[stage] + to_core[stage]):
                copy.start()
        else:
            for moves in to_core:
                for copy in self.arriving(piece, moves):
                    copy.wait_recv()
            for moves in plan:
                for copy in self.leaving(piece, moves):
                    copy.wait_send()

    def is_core(self, stage, move):
        slot = move[0]
        zs = self.site.zs
        if slot < zs - 1:
            return False
        return (slot - (zs - 1)) % 2 == 0


def at_stages(stages, pieces, lag, step, run):
    for stage in reversed(range(stages)):
        piece = step - lag * stage

        @pl.when(jnp.logical_and(piece >= 0, piece < pieces))
        def _(stage=stage, piece=piece):
            run(stage, piece)


def stages_of(n):
    return (n // 2).bit_length() + 2


def along_line(step, start, site, own, line, local_sem, send_sem, recv_sem):
    local = functools.partial(pltpu.make_async_copy, own, line.at[site.z], local_sem)

    def passing(hop, way):
        z = site.z - way * hop
        return pltpu.make_async_remote_copy(
            src_ref=own if hop == 0 else line.at[z], dst_ref=line.at[z],
            send_sem=send_sem.at[hop, (1 - way) // 2], recv_sem=recv_sem.at[hop, (1 - way) // 2],
            device_id=(site.z + way, site.f), device_id_type=MESH,
        )

    def arriving(hop, way):
        z = site.z - way * (hop + 1)
        return pltpu.make_async_remote_copy(
            src_ref=own, dst_ref=line.at[z],
            send_sem=send_sem.at[hop, (1 - way) // 2], recv_sem=recv_sem.at[hop, (1 - way) // 2],
            device_id=(site.z - way, site.f), device_id_type=MESH,
        )

    def inside(z):
        return jnp.logical_and(z >= 0, z < site.zs)

    for hop in range(site.zs):

        @pl.when(step == start + LAG * hop)
        def _(hop=hop):
            if hop == 0:
                local().start()
            else:
                for way in (1, -1):

                    @pl.when(inside(site.z - way * hop))
                    def _(way=way):
                        arriving(hop - 1, way).wait_recv()

            if hop < site.zs - 1:
                for way in (1, -1):

                    @pl.when(jnp.logical_and(inside(site.z - way * hop), inside(site.z + way)))
                    def _(way=way):
                        passing(hop, way).start()

            else:
                local().wait()
                for early in range(site.zs - 1):
                    for way in (1, -1):

                        @pl.when(jnp.logical_and(inside(site.z - way * early), inside(site.z + way)))
                        def _(way=way, early=early):
                            passing(early, way).wait_send()


def gather_kernel(pieces, start, own, late, last, whole, line, before, *refs):
    step = pl.program_id(0)
    site = Site()

    @pl.when(step == 0)
    def _():
        site.greet()

    edge_send, edge_recv = refs[3:5]

    def edge():
        return pltpu.make_async_remote_copy(
            src_ref=last, dst_ref=before, send_sem=edge_send, recv_sem=edge_recv,
            device_id=(site.over(1), site.f), device_id_type=MESH,
        )

    @pl.when(step == 0)
    def _():
        edge().start()

    gather = Gather(site, own, whole, *refs[:3])
    at_stages(gather.stages, pieces, LAG, step, gather.run)
    along_line(step, start, site, late, line, *refs[5:])

    @pl.when(step == pl.num_programs(0) - 1)
    def _():
        edge().wait()


def gather_scratch(pieces):
    slots = Gather.slots(lax.axis_size("seq"), lax.axis_size("fsdp"))
    return [
        pltpu.SemaphoreType.DMA((pieces,)),
        pltpu.SemaphoreType.DMA((pieces, slots)),
        pltpu.SemaphoreType.DMA((pieces, slots)),
    ]


def gathered(own, late, last, collective_id):
    rows, columns = own.shape
    zs, n = lax.axis_size("seq"), lax.axis_size("fsdp")
    pieces = columns // PIECE
    steps = max(pieces + LAG * (stages_of(n) - 1), LAG * zs)
    start = min(pieces // 2, steps - LAG * (zs - 1) - 1)
    anywhere = pl.BlockSpec(memory_space=pl.ANY)
    dma = pltpu.SemaphoreType.DMA
    return pl.pallas_call(
        functools.partial(gather_kernel, pieces, start),
        grid=(steps,),
        in_specs=[anywhere] * 3,
        out_specs=[anywhere] * 3,
        out_shape=[
            jax.ShapeDtypeStruct((zs, n, rows, columns), own.dtype),
            jax.ShapeDtypeStruct((zs,) + late.shape, late.dtype),
            jax.ShapeDtypeStruct(last.shape, last.dtype),
        ],
        scratch_shapes=gather_scratch(pieces) + [dma, dma, dma, dma((zs - 1, 2)), dma((zs - 1, 2))],
        compiler_params=pltpu.CompilerParams(collective_id=collective_id, has_side_effects=True),
        cost_estimate=pl.CostEstimate(
            flops=0, bytes_accessed=2 * zs * n * rows * columns, transcendentals=0
        ),
        name="gather_rows",
    )(own, late, last)


class Scatter:
    def take(self, refs):
        bits = self.site.bits
        self.kept = refs[:bits]
        self.sent = refs[bits : 2 * bits]
        self.got = refs[2 * bits : 3 * bits]
        self.z_kept, self.z_sent, self.z_got, self.send_sem, self.recv_sem = refs[3 * bits :]
        self.stages = bits + 3

    @staticmethod
    def common(pieces, rows):
        zs, n = lax.axis_size("seq"), lax.axis_size("fsdp")
        chips = n // 2
        bits = chips.bit_length() - 1
        slots = 1 + 2 * bits + zs - 1
        steps = [(pieces, 2, zs, chips >> (k + 1), rows, HALF) for k in range(bits)]
        return (
            [pltpu.VMEM(s, F32) for s in steps]
            + [pltpu.VMEM(s, BF16) for s in steps]
            + [pltpu.VMEM(s, BF16) for s in steps]
            + [
                pltpu.VMEM((pieces, rows, PIECE), F32),
                pltpu.VMEM((pieces, zs, rows, PIECE), BF16),
                pltpu.VMEM((pieces, zs - 1, rows, PIECE), BF16),
                pltpu.SemaphoreType.DMA((pieces, slots)),
                pltpu.SemaphoreType.DMA((pieces, slots)),
            ]
        )

    def remote(self, piece, slot, src, dst, device):
        at = self.at(piece)
        return pltpu.make_async_remote_copy(
            src_ref=src, dst_ref=dst, send_sem=self.send_sem.at[at, slot],
            recv_sem=self.recv_sem.at[at, slot], device_id=device, device_id_type=MESH,
        )

    def order(self, half):
        up = list(range(1, self.site.bits + 1))
        return up[::-1] if half == 0 else up

    def across(self, piece, k, half):
        s, at = self.site, self.at(piece)
        return self.remote(
            piece, 1 + 2 * k + half, self.sent[k].at[at, half], self.got[k].at[at, half],
            (s.z, s.flip([self.order(half)[k]])),
        )

    def along(self, piece, dz):
        s, at = self.site, self.at(piece)
        return self.remote(
            piece, 2 * s.bits + dz, self.z_sent.at[at, s.over(dz)], self.z_got.at[at, dz - 1],
            (s.over(dz), s.f),
        )

    def run(self, stage, piece):
        s, at = self.site, self.at(piece)
        bits = s.bits
        if stage == 0:
            self.begin(piece)
            self.to_core(piece).start()
            return
        if stage == 1:
            self.join(piece)
            self.to_core(piece).wait()
        elif stage <= bits + 1:
            for half in range(2):
                self.across(piece, stage - 2, half).wait()
        if stage <= bits:
            k = stage - 1
            for half in range(2):
                order = self.order(half)
                left = sorted(order[k:])
                j = order[k]
                place = left.index(j)
                mine = s.bit(j)

                def one(zi, carry, half=half, k=k, place=place, mine=mine):
                    for i in range(s.chips >> (k + 1)):
                        low = i % 2**place
                        base = (i - low) * 2 + low
                        self.sent[k][at, half, zi, i] = self.current(
                            k, piece, half, zi, base + (1 - mine) * 2**place
                        ).astype(BF16)
                        self.kept[k][at, half, zi, i] = self.current(
                            k, piece, half, zi, base + mine * 2**place
                        )
                    return carry

                lax.fori_loop(0, s.zs, one, 0)
                self.across(piece, k, half).start()
        elif stage == bits + 1:
            for half in range(2):
                lanes = slice(half * HALF, (half + 1) * HALF)

                def one(zi, carry, half=half, lanes=lanes):
                    self.z_sent[at, zi, :, lanes] = self.current(bits, piece, half, zi, 0).astype(BF16)
                    return carry

                lax.fori_loop(0, s.zs, one, 0)
                self.z_kept[at, :, lanes] = self.current(bits, piece, half, s.z, 0)
            for dz in range(1, s.zs):
                self.along(piece, dz).start()
        else:
            total = self.z_kept[at]
            for dz in range(1, s.zs):
                self.along(piece, dz).wait()
                total = total + self.z_got[at, dz - 1].astype(F32)
            self.out[:, pl.ds(pl.multiple_of(self.column(piece) * PIECE, 128), PIECE)] = total

    def current(self, k, piece, half, zi, index):
        at = self.at(piece)
        lanes = slice(half * HALF, (half + 1) * HALF)
        if k == 0:
            return self.first(piece, zi, index, lanes) + self.came[at, zi, index, :, lanes].astype(F32)
        return self.kept[k - 1][at, half, zi, index] + self.got[k - 1][at, half, zi, index].astype(F32)


RING = 4
XRING = 6
OUT_PIECES = 6
OUT_SPLIT = 2


class Streamed(Scatter):
    def __init__(self, site, turned, turned_out, is_later, x, out, column, refs):
        self.site, self.x, self.out = site, x, out
        self.turned, self.turned_out, self.is_later, self.column = turned, turned_out, is_later, column
        self.ring, self.x_ring = refs[0].shape[0], x.shape[0]
        self.away, self.own, self.came = refs[:3]
        self.take(refs[3:])

    @staticmethod
    def scratch(rows, ring=RING):
        zs, n = lax.axis_size("seq"), lax.axis_size("fsdp")
        full = (zs, n // 2, rows, PIECE)
        return [
            pltpu.VMEM((ring,) + full, BF16),
            pltpu.VMEM(full, BF16),
            pltpu.VMEM((ring,) + full, BF16),
        ] + Scatter.common(ring, rows)

    def at(self, piece):
        return piece % self.ring

    def to_core(self, piece):
        s, at = self.site, self.at(piece)
        return self.remote(piece, 0, self.away.at[at], self.came.at[at], (s.z, s.flip([0])))

    def product(self, core, piece, store):
        s = self.site
        rows = self.away.shape[3]
        together = 2 - s.zs % 2
        count = together * s.chips * rows
        share = OUT_PIECES // OUT_SPLIT

        for later in range(2):

            @pl.when(self.is_later(piece) == later)
            def _(later=later):
                def one(i, carry):
                    span = pl.ds(pl.multiple_of(i * count, 16), count)
                    if later:
                        lhs = self.turned[core, span, :]
                    else:
                        lhs = self.turned_out[jnp.minimum(piece, OUT_PIECES - 1) // share, core, span, :]
                    value = dot(lhs, self.x[piece % self.x_ring]).reshape(together, s.chips, rows, PIECE)
                    store(pl.ds(i * together, together), value)
                    return carry

                lax.fori_loop(0, s.zs // together, one, 0)

    def begin(self, piece):
        at = self.at(piece)

        def store(zi, value):
            self.away[at, zi] = value.astype(BF16)

        self.product(1 - self.site.bit(0), piece, store)

    def join(self, piece):
        def store(zi, value):
            self.own[zi] = value.astype(BF16)

        self.product(self.site.bit(0), piece, store)

    def first(self, piece, zi, index, lanes):
        return self.own[zi, index, :, lanes].astype(F32)


def exchange_count(zs, n):
    return (n.bit_length() - 1) + (zs.bit_length() - 1)


class Totals:
    def __init__(self, site, sent, got, send_sem, recv_sem):
        self.site, self.sent, self.got = site, sent, got
        self.send_sem, self.recv_sem = send_sem, recv_sem
        self.count = exchange_count(site.zs, site.n)

    def move(self, t):
        s = self.site
        if t <= s.bits:
            device = (s.z, s.flip([t]))
        else:
            j = t - s.bits - 1
            device = (s.z + (1 - 2 * ((s.z // 2**j) % 2)) * 2**j, s.f)
        return pltpu.make_async_remote_copy(
            src_ref=self.sent.at[t % 2], dst_ref=self.got.at[t], send_sem=self.send_sem.at[t],
            recv_sem=self.recv_sem.at[t], device_id=device, device_id_type=MESH,
        )

    def start(self, t):
        if t < self.count:
            self.move(t).start()

    def next(self, t):
        if t < self.count:
            self.move(t).wait()
            self.sent[(t + 1) % 2] = self.sent[t % 2] + self.got[t]
            self.start(t + 1)


CONV_COLS = 3584


def local(
    tokens, pre_gain, in_weight, conv_weight, conv_bias, step_bias, decay_log, skip_gain,
    norm_gain, out_weight, cotangent,
):
    both = ("seq", "fsdp")
    _, positions, features = tokens.shape
    blocks = positions // BLOCK_LEN
    devices = lax.axis_size("seq") * lax.axis_size("fsdp")

    rows = in_weight.shape[0]
    padded_rows = -(-rows // 16) * 16
    vectors = jnp.concatenate([pre_gain, conv_weight.reshape(-1), conv_bias, norm_gain])
    extra = -(-vectors.size // rows)
    sizes = (pre_gain.size, conv_weight.size, conv_bias.size, norm_gain.size)
    cuts = [sum(sizes[:i]) for i in range(5)]
    used = PROJ - INNER
    more_rows = ((0, padded_rows - rows), (0, 0))
    own = jnp.concatenate(
        [
            in_weight[:, INNER:],
            jnp.pad(vectors, (0, extra * rows - vectors.size)).reshape(rows, extra),
            jnp.zeros((rows, CONV_COLS - used - extra), BF16),
        ],
        axis=1,
    )
    inw_conv, gate_line, before = gathered(
        jnp.pad(own, more_rows),
        jnp.pad(in_weight[:, :INNER], more_rows),
        tokens[0, positions - EDGE :],
        1,
    )
    later, before = lax.optimization_barrier((out_weight, before))
    outw_full = lax.all_gather(later, both, axis=0, tiled=True)
    inw_conv = inw_conv[:, :, :rows].reshape(features, CONV_COLS)
    small_full = inw_conv[:, used : used + extra].reshape(devices, rows * extra)
    gain_full = small_full[:, : cuts[1]].reshape(1, features).astype(F32)
    convw_full = (
        small_full[:, cuts[1] : cuts[2]]
        .reshape(devices, CONV, -1)
        .transpose(1, 0, 2)
        .reshape(CONV, CHANNELS)
        .astype(F32)
    )
    convb_full = small_full[:, cuts[2] : cuts[3]].reshape(1, CHANNELS).astype(F32)
    normg_full = small_full[:, cuts[3] : cuts[4]].reshape(1, INNER).astype(F32)

    before = jnp.where(lax.axis_index("seq") == 0, jnp.zeros_like(before), before)
    ext = jnp.concatenate([before, tokens[0]], axis=0).astype(F32)
    r0_ext = lax.rsqrt(jnp.mean(ext * ext, axis=-1, keepdims=True) + 1e-05)
    normed_ext = (ext * r0_ext * gain_full).astype(BF16)
    inputs, r0, normed = ext[EDGE:], r0_ext[EDGE:], normed_ext[EDGE:]

    p = dot(normed_ext, inw_conv)
    unused = ((0, 0), (0, CONV_COLS - CHANNELS))
    w = jnp.pad(convw_full, ((0, 8 - CONV), (0, CONV_COLS - CHANNELS)))
    b = jnp.pad(convb_full, unused)
    wide_heads = ((0, 0), (0, 128 - HEADS))
    bias, decay_row = jnp.pad(step_bias[None], wide_heads), jnp.pad(decay_log[None], wide_heads)
    cols, run_rows, maps, run_exp, decays = steps_of(
        p, w, b, bias, decay_row, positions
    )
    skip = jnp.repeat(skip_gain, HEAD_DIM)[None]
    by_rows = jnp.pad(normed.reshape(positions, devices, rows), ((0, 0), (0, 0), more_rows[0]))
    y, starts, gate, turned_in, inw_gate = scan_forward(
        decays, p, w, b, cols, run_rows, maps, skip, by_rows.reshape(positions, -1), gate_line, positions, 2
    )
    inw_gate = inw_gate[:, :, :rows].reshape(features, INNER)
    cot = cotangent[0]
    grad_normed_out = dot(cot, outw_full, NT).astype(BF16)
    normed_out, dy, dye, grad_gate, ends, *turned_out = gated(
        y, gate, grad_normed_out, normg_full, run_exp, maps, rows if rows == padded_rows else None
    )

    if turned_out:
        turned_out = turned_out[0]
    else:
        turned_out = normed_out.T.reshape(-1, 2, OUT_SPLIT, rows, positions)
        turned_out = jnp.pad(turned_out, ((0, 0),) * 3 + more_rows).transpose(2, 1, 0, 3, 4)
    turned_out = turned_out.reshape(OUT_SPLIT, 2, -1, positions)
    in_kernel = rows == padded_rows
    own_main, grad_tokens, totals, *mixed = scan_backward(
        decays, p, w, b, cols, run_rows, maps, skip, y, dy, dye, starts, ends, turned_in, turned_out, cot, grad_gate,
        inw_gate, inw_conv, bias, decay_row, tokens[0], gain_full, padded_rows, 3,
        *((normed_out, outw_full) if in_kernel else ()),
    )
    if in_kernel:
        mixed = mixed[0]
    else:
        mixed = (inputs + dot(normed_out, outw_full)).astype(BF16)
    own_main = own_main[:rows]
    out_cols = OUT_PIECES * PIECE
    share = out_cols // OUT_SPLIT
    own_out = jnp.concatenate([own_main[:, i * share : (i + 1) * share] for i in range(OUT_SPLIT)])
    own_in = own_main[:, out_cols : out_cols + PROJ]
    per_tap = conv_weight.shape[1]
    me = lax.axis_index("seq") * lax.axis_size("fsdp") + lax.axis_index("fsdp")
    own_taps = lax.dynamic_slice_in_dim(totals, me * per_tap, per_tap, axis=1)
    heads = totals[:3, CHANNELS : CHANNELS + HEADS]

    return (
        mixed[None],
        grad_tokens[None],
        jnp.sum(own_in * in_weight.astype(F32), axis=1) / pre_gain.astype(F32),
        own_in,
        own_taps[:CONV],
        own_taps[CONV],
        heads[0],
        heads[1],
        heads[2],
        jnp.sum(own_out * out_weight.astype(F32), axis=1) / norm_gain.astype(F32),
        own_out,
    )


def solution(mesh):
    split = P(("seq", "fsdp"), None)
    flat = P(("seq", "fsdp"))
    taps = P(None, ("seq", "fsdp"))
    data = P("fsdp", "seq", None)
    return jax.shard_map(
        local,
        mesh=mesh,
        in_specs=(data, flat, split, taps, flat, P(), P(), P(), flat, split, data),
        out_specs=(data, data, flat, split, taps, flat, P(), P(), P(), flat, split),
        check_vma=False,
    )
```

```python
import functools
import math
import jax
import jax.numpy as jnp
from jax import lax
from jax.experimental import pallas as pl
from jax.experimental.pallas import tpu as pltpu
from jax.sharding import PartitionSpec as P

INNER = 3072
HEADS = 48
HEAD_DIM = 64
STATE = 128
CONV = 4
BLOCK_LEN = 256
CHANNELS = 3328
PROJ = 6448
EDGE = 16
GROUP = 4
GROUPS = HEADS // GROUP
GCOLS = GROUP * HEAD_DIM
PAIRS = GROUP // 2
STRIP = 128
PART = 64
MIXED_COLS = 256
EARLY = 3
LOG2E = 1.4426950408889634
F32 = jnp.float32
BF16 = jnp.bfloat16

NT = (((1,), (1,)), ((), ()))
TN = (((0,), (0,)), ((), ()))
NN = (((1,), (0,)), ((), ()))


def dot(a, b, dims=NN):
    return lax.dot_general(a, b, dims, preferred_element_type=F32)


def first_half(shape):
    return lax.broadcasted_iota(jnp.int32, shape, len(shape) - 1) < HEAD_DIM


def per_pair(cols, kind, pair, rows):
    at = kind * GROUP + 2 * pair
    left, right = cols[rows, at : at + 1], cols[rows, at + 1 : at + 2]
    shape = (left.shape[0], 2 * HEAD_DIM)
    return jnp.where(
        first_half(shape), jnp.broadcast_to(left, shape), jnp.broadcast_to(right, shape)
    )


def convolved(p_ref, w_ref, b_ref, lo, count, lanes):
    out = b_ref[0:1, lanes] + jnp.zeros((count, lanes.size), F32)
    for tap in range(CONV):
        at = EDGE - CONV + 1 + tap + lo
        out = out + p_ref[at : at + count, lanes] * w_ref[tap : tap + 1, lanes]
    return out


def sigmoid(v):
    return 0.5 + 0.5 * jnp.tanh(0.5 * v)


def softplus(v):
    return jnp.maximum(v, 0.0) + jnp.log1p(jnp.exp(-jnp.abs(v)))


def lower_triangle():
    row = lax.broadcasted_iota(jnp.int32, (BLOCK_LEN, BLOCK_LEN), 0)
    col = lax.broadcasted_iota(jnp.int32, (BLOCK_LEN, BLOCK_LEN), 1)
    return jnp.where(row >= col, 1.0, 0.0)


def exact_dot(a, b, dims=NN):
    return lax.dot_general(
        a, b, dims, precision=lax.Precision.HIGHEST, preferred_element_type=F32
    )


def steps_kernel(
    p_ref, w_ref, b_ref, bias_ref, decay_ref, cols_ref, rows_ref, maps_ref, er_ref, decays_ref
):
    positions = maps_ref.shape[0]
    blocks = positions // BLOCK_LEN
    lower = lower_triangle()
    used = lax.broadcasted_iota(jnp.int32, (1, 128), 1) < HEADS
    rate = -jnp.exp(decay_ref[...])
    total = jnp.zeros((1, 128), F32)
    for block in range(blocks):
        lo = block * BLOCK_LEN
        rows = slice(lo, lo + BLOCK_LEN)
        conv = convolved(p_ref, w_ref, b_ref, lo, BLOCK_LEN, pl.ds(0, 2 * STATE))
        maps_ref[rows, :] = (conv * sigmoid(conv)).astype(BF16)
        step = softplus(p_ref[EDGE + lo : EDGE + lo + BLOCK_LEN, 2 * STATE : 2 * STATE + 128] + bias_ref[...])
        step = jnp.where(used, step, 0.0)
        run = exact_dot(lower, rate * step)
        end = run[BLOCK_LEN - 1 :]
        total = total + end
        run2 = run * LOG2E
        grown = jnp.exp(run)
        er_ref[rows, :] = grown
        decays_ref[block : block + 1, :] = jnp.exp(end)
        turned = run2.T
        kinds = (step, run2, grown, jnp.exp(end - run))
        for group in range(GROUPS):
            heads = slice(group * GROUP, (group + 1) * GROUP)
            rows_ref[group, :, rows] = turned[heads]
            cols_ref[group, rows, :] = jnp.concatenate([kind[:, heads] for kind in kinds], axis=1)
    decays_ref[blocks : blocks + 1, :] = jnp.exp(total)
    decays_ref[blocks + 1 :, :] = jnp.zeros((8 - blocks - 1, 128), F32)


def steps_of(p, w, b, bias, decay_log, positions):
    ext = p.shape[0]
    at = INNER // PIECE
    return pl.pallas_call(
        steps_kernel,
        grid=(1,),
        in_specs=[
            pl.BlockSpec((ext, PIECE), lambda i: (0, at)),
            pl.BlockSpec((8, PIECE), lambda i: (0, at)),
            pl.BlockSpec((1, PIECE), lambda i: (0, at)),
            pl.BlockSpec((1, 128), lambda i: (0, 0)),
            pl.BlockSpec((1, 128), lambda i: (0, 0)),
        ],
        out_specs=[pl.BlockSpec(memory_space=pltpu.VMEM)] * 5,
        out_shape=[
            jax.ShapeDtypeStruct((GROUPS, positions, 4 * GROUP), F32),
            jax.ShapeDtypeStruct((GROUPS, GROUP, positions), F32),
            jax.ShapeDtypeStruct((positions, 2 * STATE), BF16),
            jax.ShapeDtypeStruct((positions, 128), F32),
            jax.ShapeDtypeStruct((8, 128), F32),
        ],
        compiler_params=pltpu.CompilerParams(vmem_limit_bytes=48 * 2**20),
        cost_estimate=pl.CostEstimate(
            flops=4 * positions * BLOCK_LEN * 128, bytes_accessed=16 * positions * 512,
            transcendentals=positions * 1024,
        ),
        name="steps",
    )(p, w, b, bias, decay_log)


def masked_scores(maps_ref, scores_ref, blocks):
    row = lax.broadcasted_iota(jnp.int32, (BLOCK_LEN, BLOCK_LEN), 0)
    col = lax.broadcasted_iota(jnp.int32, (BLOCK_LEN, BLOCK_LEN), 1)
    for block in range(blocks):
        rows = slice(block * BLOCK_LEN, (block + 1) * BLOCK_LEN)
        scores = dot(maps_ref[rows, STATE:], maps_ref[rows, :STATE], NT)
        scores_ref[block] = jnp.where(row >= col, scores, 0.0)


def chain_copy(site, group, by, sent, got, send_sem, recv_sem):
    return pltpu.make_async_remote_copy(
        src_ref=sent.at[group % sent.shape[0]], dst_ref=got.at[group], send_sem=send_sem.at[group],
        recv_sem=recv_sem.at[group], device_id=(site.over(by), site.f), device_id_type=MESH,
    )


def by_head(decays, group, kind, rows=GCOLS):
    return jnp.concatenate(
        [
            jnp.full((HEAD_DIM, STATE), decays[kind, group * GROUP + head], F32)
            for head in range(rows // HEAD_DIM)
        ],
        axis=0,
    )


def scan_forward_kernel(
    pieces, decays, p_ref, w_ref, b_ref, cols_ref, late_ref, rows_ref, maps_ref, skip_ref, normed_ref, own,
    y_ref, starts_ref, gate_ref, turned_ref, whole,
    scores_ref, x_ref, states_ref, weight_ref, weight_sem, sent, got, chain_send, chain_recv, *gather_refs,
):
    positions = y_ref.shape[0]
    blocks = positions // BLOCK_LEN
    step = pl.program_id(0)
    site = Site()
    behind = site.zs - 1

    @pl.when(step == 0)
    def _():
        site.greet()
        masked_scores(maps_ref, scores_ref, blocks)

    @pl.when(step == 1)
    def _():
        put_turned(normed_ref, own.shape[1], lambda at: turned_ref.at[at % 2, span_of(at // 2, own.shape[1])])

    gather = Gather(site, own, whole, *gather_refs)
    arrived = step - LAG * (gather.stages - 1)

    def weight_copy(piece):
        cols = pl.ds(pl.multiple_of(piece * PIECE, 128), PIECE)
        return pltpu.make_async_copy(whole.at[:, :, :, cols], weight_ref, weight_sem)

    @pl.when(jnp.logical_and(arrived >= 1, arrived <= pieces))
    def _():
        weight_copy(arrived - 1).wait()
        gate_ref[...] = dot(normed_ref[...], weight_ref[...].reshape(-1, PIECE))

    at_stages(gather.stages, pieces, LAG, step, gather.run)

    @pl.when(jnp.logical_and(arrived >= 0, arrived < pieces))
    def _():
        weight_copy(arrived).start()

    @pl.when(step < GROUPS)
    def _():
        slot = step % site.zs
        for pair in range(PAIRS):
            lanes = pl.ds(pair * 2 * HEAD_DIM, 2 * HEAD_DIM)
            for block in range(blocks):
                lo = block * BLOCK_LEN
                rows = slice(lo, lo + BLOCK_LEN)
                conv = convolved(p_ref, w_ref, b_ref, lo, BLOCK_LEN, lanes)
                x = conv * sigmoid(conv)
                x_ref[slot, rows, lanes] = x
                xs = x * per_pair(cols_ref, 0, pair, rows)
                ended = (xs * per_pair(cols_ref, 3, pair, rows)).astype(BF16)
                states_ref[slot, block, pair * 2 * HEAD_DIM : (pair + 1) * 2 * HEAD_DIM, :] = dot(
                    ended, maps_ref[rows, :STATE], TN
                )

    linked = step - site.z

    @pl.when(jnp.logical_and(linked >= 0, linked < GROUPS))
    def _():
        slot = linked % site.zs

        @pl.when(site.z == 0)
        def _():
            got[linked] = jnp.zeros((GCOLS, STATE), BF16)

        @pl.when(site.z > 0)
        def _():
            chain_copy(site, linked, 1, sent, got, chain_send, chain_recv).wait_recv()

        @pl.when(site.z < behind)
        def _():
            final = states_ref[slot, 0]
            for block in range(1, blocks):
                final = by_head(decays, linked, block) * final + states_ref[slot, block]
            sent[linked % sent.shape[0]] = (
                by_head(decays, linked, blocks) * got[linked].astype(F32) + final
            ).astype(BF16)
            chain_copy(site, linked, 1, sent, got, chain_send, chain_recv).start()

    group = step - behind

    @pl.when(jnp.logical_and(group >= 0, group < GROUPS))
    def _():
        slot = group % site.zs
        start = got[group].astype(F32)
        for block in range(blocks):
            if block:
                start = by_head(decays, group, block - 1) * start + states_ref[slot, block - 1]
            starts_ref[block] = start.astype(BF16)
        half = first_half((BLOCK_LEN, 2 * HEAD_DIM))
        for pair in range(PAIRS):
            lanes = pl.ds(pair * 2 * HEAD_DIM, 2 * HEAD_DIM)
            span = slice(pair * 2 * HEAD_DIM, (pair + 1) * 2 * HEAD_DIM)
            for block in range(blocks):
                lo = block * BLOCK_LEN
                rows = slice(lo, lo + BLOCK_LEN)
                x = x_ref[slot, rows, lanes]
                low = (x * per_pair(late_ref, 0, pair, rows)).astype(BF16)
                none = jnp.zeros_like(low)
                one, two = jnp.where(half, low, none), jnp.where(half, none, low)
                rest = skip_ref[0:1, lanes] * x + dot(
                    maps_ref[rows, STATE:], starts_ref[block, span, :], NT
                ) * per_pair(late_ref, 2, pair, rows)
                for strip in range(BLOCK_LEN // STRIP):
                    top = strip * STRIP
                    lim = top + STRIP
                    pieces_ = []
                    for side in range(2):
                        head = 2 * pair + side
                        at = GROUP + head
                        gap = (
                            late_ref[lo + top : lo + lim, at : at + 1]
                            - rows_ref[head : head + 1, lo : lo + lim]
                        )
                        decay = jnp.exp2(jnp.minimum(gap, 0.0))
                        pieces_.append((scores_ref[block, top:lim, :lim] * decay).astype(BF16))
                    y = dot(pieces_[0], one[:lim]) + dot(pieces_[1], two[:lim])
                    y_ref[lo + top : lo + lim, lanes] = y + rest[top:lim]

        @pl.when(site.z < behind)
        def _():
            chain_copy(site, group, 1, sent, got, chain_send, chain_recv).wait_send()


def span_of(at, rows):
    return slice(at * rows, (at + 1) * rows)


def put_turned(x_ref, rows, place, lanes=slice(None)):
    together = rows * 128 // math.gcd(rows, 128)
    for at in range(x_ref.shape[1] // together):
        turned = x_ref[:, span_of(at, together)].astype(F32).T
        for index in range(together // rows):
            place(at * (together // rows) + index)[:, lanes] = turned[span_of(index, rows)].astype(BF16)


def chain_scratch():
    ring = max(lax.axis_size("seq"), LAG + 2)
    return [
        pltpu.VMEM((ring, GCOLS, STATE), BF16),
        pltpu.VMEM((GROUPS, GCOLS, STATE), BF16),
        pltpu.SemaphoreType.DMA((GROUPS,)),
        pltpu.SemaphoreType.DMA((GROUPS,)),
    ]


def scan_forward(decays, p, w, b, cols, rows, maps, skip, normed, own, positions, collective_id):
    blocks = positions // BLOCK_LEN
    ext = p.shape[0]
    zs, n = lax.axis_size("seq"), lax.axis_size("fsdp")
    rows_there, columns = own.shape[1:]
    pieces = columns // PIECE
    wait = LAG * (stages_of(n) - 2) + 1
    steps = max(GROUPS + zs - 1, pieces + wait)

    def early(s):
        return jnp.minimum(s, GROUPS - 1)

    def late(s):
        return jnp.clip(s - (zs - 1), 0, GROUPS - 1)

    anywhere = pl.BlockSpec(memory_space=pl.ANY)
    return pl.pallas_call(
        functools.partial(scan_forward_kernel, pieces),
        grid=(steps,),
        in_specs=[
            pl.BlockSpec(memory_space=pltpu.SMEM),
            pl.BlockSpec((ext, GCOLS), lambda s: (0, early(s))),
            pl.BlockSpec((8, GCOLS), lambda s: (0, early(s))),
            pl.BlockSpec((1, GCOLS), lambda s: (0, early(s))),
            pl.BlockSpec((None, positions, 4 * GROUP), lambda s: (early(s), 0, 0)),
            pl.BlockSpec((None, positions, 4 * GROUP), lambda s: (late(s), 0, 0)),
            pl.BlockSpec((None, GROUP, positions), lambda s: (late(s), 0, 0)),
            pl.BlockSpec((positions, 2 * STATE), lambda s: (0, 0)),
            pl.BlockSpec((1, GCOLS), lambda s: (0, late(s))),
            pl.BlockSpec(normed.shape, lambda s: (0, 0), pipeline_mode=pl.Buffered(1)),
            anywhere,
        ],
        out_specs=[
            pl.BlockSpec((positions, GCOLS), lambda s: (0, late(s))),
            pl.BlockSpec((blocks, GCOLS, STATE), lambda s: (0, late(s), 0)),
            pl.BlockSpec((positions, PIECE), lambda s: (0, jnp.clip(s - wait, 0, pieces - 1))),
            pl.BlockSpec(
                (2, zs * n // 2 * rows_there, positions), lambda s: (0, 0, 0), pipeline_mode=pl.Buffered(1)
            ),
            anywhere,
        ],
        out_shape=[
            jax.ShapeDtypeStruct((positions, INNER), F32),
            jax.ShapeDtypeStruct((blocks, INNER, STATE), BF16),
            jax.ShapeDtypeStruct((positions, columns), F32),
            jax.ShapeDtypeStruct((2, zs * n // 2 * rows_there, positions), BF16),
            jax.ShapeDtypeStruct((zs, n, rows_there, columns), BF16),
        ],
        scratch_shapes=[
            pltpu.VMEM((blocks, BLOCK_LEN, BLOCK_LEN), F32),
            pltpu.VMEM((zs, positions, GCOLS), F32),
            pltpu.VMEM((zs, blocks, GCOLS, STATE), F32),
            pltpu.VMEM((zs, n, rows_there, PIECE), BF16),
            pltpu.SemaphoreType.DMA,
        ]
        + chain_scratch()
        + gather_scratch(pieces),
        compiler_params=pltpu.CompilerParams(
            collective_id=collective_id, has_side_effects=True, vmem_limit_bytes=48 * 2**20
        ),
        cost_estimate=pl.CostEstimate(
            flops=12 * positions * INNER * BLOCK_LEN, bytes_accessed=24 * positions * INNER,
            transcendentals=HEADS * positions * BLOCK_LEN,
        ),
        name="scan_forward",
    )(decays, p, w, b, cols, cols, rows, maps, skip, normed, own)


def gate_kernel(
    y_ref, gate_ref, gno_ref, gain_ref, er_ref, maps_ref,
    out_ref, dy_ref, dye_ref, ggate_ref, ends_ref, *more_refs,
):
    gated_ref = more_refs[-1]
    rows = y_ref.shape[0]
    width = 2 * HEAD_DIM
    shape = (rows, width)
    square = jnp.zeros(shape, F32)
    cross = jnp.zeros(shape, F32)

    def decayed(pair):
        return jnp.where(
            first_half(shape),
            jnp.broadcast_to(er_ref[:, 2 * pair : 2 * pair + 1], shape),
            jnp.broadcast_to(er_ref[:, 2 * pair + 1 : 2 * pair + 2], shape),
        )

    for pair in range(HEADS // 2):
        lanes = slice(pair * width, (pair + 1) * width)
        gate = gate_ref[:, lanes]
        gated = y_ref[:, lanes] * gate * sigmoid(gate)
        gated_ref[:, lanes] = gated
        square = square + gated * gated
        cross = cross + gated * (gain_ref[:, lanes] * gno_ref[:, lanes])
    r1 = lax.rsqrt(jnp.sum(square, axis=-1, keepdims=True) * (1.0 / INNER) + 1e-05)
    back = r1 * r1 * r1 * (jnp.sum(cross, axis=-1, keepdims=True) * (1.0 / INNER))

    @pl.when(pl.program_id(0) % (BLOCK_LEN // rows) == 0)
    def _():
        ends_ref[...] = jnp.zeros_like(ends_ref)

    for pair in range(HEADS // 2):
        lanes = slice(pair * width, (pair + 1) * width)
        gate = gate_ref[:, lanes]
        sig = sigmoid(gate)
        gated = gated_ref[:, lanes]
        gain = gain_ref[:, lanes]
        out_ref[:, lanes] = (gated * r1 * gain).astype(BF16)
        ggated = gno_ref[:, lanes] * r1 * gain - gated * back
        low = (ggated * (gate * sig)).astype(BF16)
        dy_ref[:, lanes] = low
        ggate_ref[:, lanes] = (
            ggated * y_ref[:, lanes] * (sig * (1.0 + gate * (1.0 - sig)))
        ).astype(BF16)
        scaled = (low.astype(F32) * decayed(pair)).astype(BF16)
        dye_ref[:, lanes] = scaled
        ends_ref[lanes, :] += dot(scaled, maps_ref[:, STATE:], TN)

    if len(more_refs) == 2:
        turned_ref = more_refs[0]
        own_rows = INNER // (turned_ref.shape[0] * turned_ref.shape[1] * turned_ref.shape[2])

        def place(at):
            rest, split = at // OUT_SPLIT, at % OUT_SPLIT
            return turned_ref.at[split, rest % 2, rest // 2]

        put_turned(out_ref, own_rows, place)


def gated(y, gate, gno, gain, er, maps, own_rows):
    positions = y.shape[0]
    tile = 128
    per_block = BLOCK_LEN // tile
    wide = pl.BlockSpec((tile, INNER), lambda i: (i, 0))
    states = pl.BlockSpec((None, INNER, STATE), lambda i: (i // per_block, 0, 0))
    low = jax.ShapeDtypeStruct((positions, INNER), BF16)
    extra = []
    if own_rows:
        extra.append((OUT_SPLIT, 2, INNER // (2 * OUT_SPLIT * own_rows), own_rows, positions))
    return pl.pallas_call(
        gate_kernel,
        grid=(positions // tile,),
        in_specs=[
            wide,
            wide,
            wide,
            pl.BlockSpec((1, INNER), lambda i: (0, 0)),
            pl.BlockSpec((tile, 128), lambda i: (i, 0)),
            pl.BlockSpec((tile, 2 * STATE), lambda i: (i, 0)),
        ],
        out_specs=[wide] * 4
        + [states]
        + [pl.BlockSpec(turned[:-1] + (tile,), lambda i: (0, 0, 0, 0, i)) for turned in extra],
        out_shape=[
            low,
            low,
            low,
            low,
            jax.ShapeDtypeStruct((positions // BLOCK_LEN, INNER, STATE), F32),
        ]
        + [jax.ShapeDtypeStruct(turned, BF16) for turned in extra],
        scratch_shapes=[pltpu.VMEM((tile, INNER), F32)],
        compiler_params=pltpu.CompilerParams(vmem_limit_bytes=48 * 2**20),
        cost_estimate=pl.CostEstimate(
            flops=4 * positions * INNER * STATE, bytes_accessed=24 * positions * INNER,
            transcendentals=2 * positions * INNER,
        ),
        name="gate",
    )(y, gate, gno, gain, er, maps)


def spread_turn(step, first):
    return jnp.clip(step - first, 0, 2) + jnp.maximum(step - (GROUPS + LAG + 1), 0)


def spread_now(step, first, turns):
    early = jnp.logical_and(step >= first, step < first + 2)
    after = step - (GROUPS + LAG + 1)
    return jnp.logical_or(early, jnp.logical_and(after >= 0, after < turns - 2))


def scan_backward_kernel(
    branch, decays, p_ref, w_ref, b_ref, cols_ref, rows_ref, maps_ref, skip_ref, y_ref, dy_ref,
    dye_ref, st_ref, grads_ref, turned_ref, turned_out_ref, cot_ref, ggate_ref, wgate_ref, wconv_ref,
    plast_ref, wlast_ref, blast_ref, bias_ref, decay_ref, grown_ref, tokens_ref, gain_ref, *more_refs,
):
    if branch:
        nout_ref, wout_ref, *more_refs = more_refs
        mixed_ref = more_refs.pop(3)
        step = pl.program_id(0)
        at = spread_turn(step, 1)

        @pl.when(spread_now(step, 1, tokens_ref.shape[1] // MIXED_COLS))
        def _():
            lanes = pl.ds(pl.multiple_of(at * MIXED_COLS, 128), MIXED_COLS)
            mixed_ref[...] = (
                tokens_ref[:, lanes].astype(F32) + dot(nout_ref[...], wout_ref[...])
            ).astype(BF16)

    scan_backward_steps(
        decays, p_ref, w_ref, b_ref, cols_ref, rows_ref, maps_ref, skip_ref, y_ref, dy_ref,
        dye_ref, st_ref, grads_ref, turned_ref, turned_out_ref, cot_ref, ggate_ref, wgate_ref, wconv_ref,
        plast_ref, wlast_ref, blast_ref, bias_ref, decay_ref, grown_ref, tokens_ref, gain_ref, *more_refs,
    )


def scan_backward_steps(
    decays, p_ref, w_ref, b_ref, cols_ref, rows_ref, maps_ref, skip_ref, y_ref, dy_ref,
    dye_ref, st_ref, grads_ref, turned_ref, turned_out_ref, cot_ref, ggate_ref, wgate_ref, wconv_ref,
    plast_ref, wlast_ref, blast_ref, bias_ref, decay_ref, grown_ref, tokens_ref, gain_ref,
    own_ref, gtokens_ref, total_ref,
    scores_ref, dscores_ref, dpad_ref, gacc_ref, dl_ref, x_ref, tail_ref, runs_ref, direct_ref, ends_ref,
    cross_ref, conv_ref, inner_ref, outer_ref, low_ref, ended_ref, sent, got, chain_send, chain_recv,
    edge_sent, edge_got, edge_send, edge_recv, t_sent, t_got, t_send, t_recv, *scatter_refs,
):
    step_at = pl.program_id(0)
    site = Site()
    behind = site.zs - 1
    positions = y_ref.shape[0]
    gates = INNER // PIECE
    ahead = PIECE // GCOLS
    later = step_at - OUT_PIECES

    @pl.when(step_at == 0)
    def _():
        site.greet()
        gtokens_ref[...] = jnp.zeros_like(gtokens_ref)
        runs_ref[...] = jnp.zeros_like(runs_ref)
        direct_ref[...] = jnp.zeros_like(direct_ref)
        t_sent[0, CONV + 1 :, 0:INNER] = jnp.zeros((8 - CONV - 1, INNER), F32)

    def edge_copy(group):
        return pltpu.make_async_remote_copy(
            src_ref=edge_sent.at[group], dst_ref=edge_got.at[group], send_sem=edge_send.at[group],
            recv_sem=edge_recv.at[group], device_id=(site.over(behind), site.f), device_id_type=MESH,
        )

    def add_normed(weight_ref, grads_of):
        def one(i, carry):
            span = pl.ds(pl.multiple_of(i * PIECE, 128), PIECE)
            gtokens_ref[:, span] += dot(grads_of(), weight_ref[span, :], NT)
            return carry

        lax.fori_loop(0, gtokens_ref.shape[1] // PIECE, one, 0)

    @pl.when(step_at < OUT_PIECES)
    def _():
        cots = cot_ref.shape[1] // PIECE
        span = pl.ds(pl.multiple_of((step_at % cots) * PIECE, 128), PIECE)
        x_ref[step_at % XRING] = cot_ref[:, span]

    inside = jnp.logical_and(later >= 0, later < 2 * gates)

    @pl.when(jnp.logical_and(inside, later % 2 == 1))
    def _():
        x_ref[step_at % XRING] = ggate_ref[...]

    @pl.when(jnp.logical_and(inside, later % 2 == 0))
    def _():
        for side in range(ahead):
            group = (later // 2) * ahead + side
            lanes = slice(side * GCOLS, (side + 1) * GCOLS)

            @pl.when(site.z < behind)
            def _(group=group, lanes=lanes):
                edge_copy(group).wait_recv()
                x_ref[step_at % XRING, positions - 8 :, lanes] = (
                    tail_ref[group] + edge_got[group]
                ).astype(BF16)

            @pl.when(site.z > 0)
            def _(group=group):
                edge_copy(group).wait_send()

        add_normed(wconv_ref, lambda: x_ref[step_at % XRING])

    last = OUT_PIECES + 2 * gates
    start = last - LAG - 1
    slot = last % XRING
    wide = 2 * STATE
    totals = Totals(site, t_sent, t_got, t_send, t_recv)

    def last_edge():
        return pltpu.make_async_remote_copy(
            src_ref=edge_sent.at[GROUPS], dst_ref=edge_got.at[GROUPS], send_sem=edge_send.at[GROUPS],
            recv_sem=edge_recv.at[GROUPS], device_id=(site.over(behind), site.f), device_id_type=MESH,
        )

    @pl.when(step_at == start)
    def _():
        tail, edge = maps_backward(plast_ref, wlast_ref, blast_ref, gacc_ref, dpad_ref, x_ref, slot, t_sent)
        tail_ref[GROUPS] = tail
        edge_sent[GROUPS] = edge

        @pl.when(site.z > 0)
        def _():
            last_edge().start()

        steps_backward(
            plast_ref, bias_ref, decay_ref, grown_ref, runs_ref, direct_ref, ends_ref, cross_ref, x_ref, slot,
            t_sent,
        )
        totals.start(0)

    for t in range(totals.count):

        @pl.when(step_at == start + 1 + t)
        def _(t=t):
            totals.next(t)

    @pl.when(step_at == start + 1 + totals.count)
    def _():
        total_ref[...] = t_sent[totals.count % 2]

    @pl.when(step_at == last)
    def _():
        @pl.when(site.z < behind)
        def _():
            last_edge().wait_recv()
            x_ref[slot, positions - 8 :, 0:wide] = (tail_ref[GROUPS] + edge_got[GROUPS]).astype(BF16)

        @pl.when(site.z > 0)
        def _():
            last_edge().wait_send()

        add_normed(wconv_ref, lambda: x_ref[step_at % XRING])

    after = step_at - last - 1

    @pl.when(jnp.logical_or(step_at < EARLY, jnp.logical_and(after >= 0, after < gates - EARLY)))
    def _():
        add_normed(wgate_ref, lambda: ggate_ref[...])

    tile = 128

    backward = after - (gates - EARLY)

    @pl.when(jnp.logical_and(backward >= 0, backward < positions // (2 * tile)))
    def _():
        def one(i, carry):
            rows = pl.ds(pl.multiple_of(backward * 2 * tile + i * tile, tile), tile)
            features = gtokens_ref.shape[1]
            inputs = tokens_ref[rows, :].astype(F32)
            r0 = lax.rsqrt(jnp.sum(inputs * inputs, axis=-1, keepdims=True) * (1.0 / features) + 1e-05)
            f = gain_ref[...] * gtokens_ref[rows, :]
            share = r0 * r0 * r0 * (jnp.sum(f * inputs, axis=-1, keepdims=True) * (1.0 / features))
            gtokens_ref[rows, :] = cot_ref[rows, :].astype(F32) + r0 * f - inputs * share
            return carry

        lax.fori_loop(0, 2, one, 0)

    def is_later(piece):
        return jnp.minimum(piece, OUT_PIECES) // OUT_PIECES

    def column(piece):
        after = jnp.maximum(piece - OUT_PIECES, 0)
        return jnp.minimum(piece, OUT_PIECES) + is_later(piece) * (1 - after % 2) * gates + after // 2

    scatter = Streamed(site, turned_ref, turned_out_ref, is_later, x_ref, own_ref, column, scatter_refs)
    at_stages(scatter.stages, last + 1, LAG, step_at, scatter.run)

    linked = step_at - (behind - site.z)
    blocks = positions // BLOCK_LEN

    @pl.when(jnp.logical_and(linked >= 0, linked < GROUPS))
    def _():
        @pl.when(site.z == behind)
        def _():
            got[linked] = jnp.zeros((GCOLS, STATE), BF16)

        @pl.when(site.z < behind)
        def _():
            chain_copy(site, linked, behind, sent, got, chain_send, chain_recv).wait_recv()

        @pl.when(site.z > 0)
        def _():
            span = pl.ds(pl.multiple_of(linked * GCOLS, GCOLS), GCOLS)
            grad = got[linked].astype(F32)
            for block in reversed(range(blocks)):
                grad = by_head(decays, linked, block) * grad + grads_ref[block, span, :]
            sent[linked % sent.shape[0]] = grad.astype(BF16)
            chain_copy(site, linked, behind, sent, got, chain_send, chain_recv).start()

    group = step_at - max(behind, LAG + 1)

    @pl.when(jnp.logical_and(group >= 0, group < GROUPS))
    def _():
        scan_backward_group(
            group, decays, p_ref, w_ref, b_ref, cols_ref, rows_ref, maps_ref, skip_ref, y_ref,
            dy_ref, dye_ref, st_ref, grads_ref, x_ref, tail_ref, edge_sent, t_sent, runs_ref, direct_ref,
            ends_ref, cross_ref, scores_ref, dscores_ref, dpad_ref, gacc_ref, dl_ref, got, conv_ref, inner_ref,
            outer_ref, low_ref, ended_ref,
        )

        @pl.when(site.z > 0)
        def _():
            edge_copy(group).start()
            chain_copy(site, group, behind, sent, got, chain_send, chain_recv).wait_send()


def maps_backward(p_ref, w_ref, b_ref, grad_ref, dpad_ref, x_ref, slot, t_sent):
    positions, wide = grad_ref.shape
    blocks = positions // BLOCK_LEN
    lanes = pl.ds(0, wide)
    taps = [jnp.zeros((1, wide), F32) for _ in range(CONV + 1)]
    for block in range(blocks):
        lo = block * BLOCK_LEN
        conv = convolved(p_ref, w_ref, b_ref, lo, BLOCK_LEN, lanes)
        sig = sigmoid(conv)
        dconv = grad_ref[lo : lo + BLOCK_LEN, :] * (sig * (1.0 + conv * (1.0 - sig)))
        dpad_ref[8 + lo : 8 + lo + BLOCK_LEN, :] = dconv
        for tap in range(CONV):
            at = EDGE - CONV + 1 + tap + lo
            taps[tap] = taps[tap] + jnp.sum(
                dconv * p_ref[at : at + BLOCK_LEN, 0:wide], axis=0, keepdims=True
            )
        taps[CONV] = taps[CONV] + jnp.sum(dconv, axis=0, keepdims=True)
    for index in range(CONV + 1):
        t_sent[0, index : index + 1, INNER : INNER + wide] = taps[index]
    t_sent[0, CONV + 1 :, INNER : INNER + wide] = jnp.zeros((8 - CONV - 1, wide), F32)

    def back_rows(at, count):
        back = jnp.zeros((count, wide), F32)
        for tap in range(CONV):
            start = at + CONV - 1 - tap
            back = back + dpad_ref[start : start + count, :] * w_ref[tap : tap + 1, 0:wide]
        return back

    for block in range(blocks):
        lo = block * BLOCK_LEN
        x_ref[slot, lo : lo + BLOCK_LEN, 0:wide] = back_rows(8 + lo, BLOCK_LEN).astype(BF16)
    return back_rows(positions, 8), back_rows(0, 8)


def steps_backward(
    p_ref, bias_ref, decay_ref, decays_ref, runs_ref, direct_ref, ends_ref, cross_ref, x_ref, slot, t_sent
):
    positions = runs_ref.shape[0]
    blocks = positions // BLOCK_LEN
    wide = 2 * STATE
    used = lax.broadcasted_iota(jnp.int32, (1, 128), 1) < HEADS
    rate = -jnp.exp(decay_ref[...])
    by_heads = jnp.zeros((8, 128), F32)
    for at in range(0, INNER, PIECE):
        spread = jnp.where(
            (at + lax.broadcasted_iota(jnp.int32, (PIECE, 128), 0)) // HEAD_DIM
            == lax.broadcasted_iota(jnp.int32, (PIECE, 128), 1),
            1.0,
            0.0,
        )
        by_heads = by_heads + exact_dot(ends_ref[:, at : at + PIECE], spread)
    per_group = blocks * GROUP
    crossed = jnp.sum(cross_ref[...].reshape(GROUPS * per_group, STATE), axis=1, keepdims=True)
    row = lax.broadcasted_iota(jnp.int32, (GROUPS * per_group, 128), 0)
    lane = lax.broadcasted_iota(jnp.int32, (GROUPS * per_group, 128), 1)
    same = (row // per_group) * GROUP + row % GROUP == lane
    tri_row = lax.broadcasted_iota(jnp.int32, (BLOCK_LEN, BLOCK_LEN), 0)
    tri_col = lax.broadcasted_iota(jnp.int32, (BLOCK_LEN, BLOCK_LEN), 1)
    upper = jnp.where(tri_row <= tri_col, 1.0, 0.0)
    grad_bias = jnp.zeros((1, 128), F32)
    grad_decay = jnp.zeros((1, 128), F32)
    for block in range(blocks):
        lo = block * BLOCK_LEN
        rows = slice(lo, lo + BLOCK_LEN)
        here = jnp.logical_and(same, (row % per_group) // GROUP == block)
        end = by_heads[block : block + 1] + decays_ref[block : block + 1, :] * jnp.sum(
            jnp.where(here, crossed, 0.0), axis=0, keepdims=True
        )
        arg = p_ref[EDGE + lo : EDGE + lo + BLOCK_LEN, wide : wide + 128] + bias_ref[...]
        step = softplus(arg)
        grad_log = exact_dot(upper, runs_ref[rows, :]) + end
        grad_step = jnp.where(used, (direct_ref[rows, :] + rate * grad_log) * sigmoid(arg), 0.0)
        grad_bias = grad_bias + jnp.sum(grad_step, axis=0, keepdims=True)
        grad_decay = grad_decay + jnp.sum(
            jnp.where(used, grad_log * (rate * step), 0.0), axis=0, keepdims=True
        )
        x_ref[slot, rows, wide : wide + 128] = grad_step.astype(BF16)
        x_ref[slot, rows, wide + 128 :] = jnp.zeros((BLOCK_LEN, PIECE - wide - 128), BF16)
    t_sent[0, :, INNER + wide :] = jnp.concatenate(
        [grad_bias, grad_decay, by_heads[blocks : blocks + 1], jnp.zeros((5, 128), F32)], axis=0
    )


def scan_backward_group(
    step_at, decays, p_ref, w_ref, b_ref, cols_ref, rows_ref, maps_ref, skip_ref, y_ref, dy_ref,
    dye_ref, st_ref, grads_ref, x_ref, tail_ref, edge_ref, t_sent, runs_ref, direct_ref, ends_ref,
    cross_ref, scores_ref, dscores_ref, dpad_ref, gacc_ref, dl_ref, got, conv_ref, inner_ref, outer_ref,
    low_ref, ended_ref,
):
    positions = y_ref.shape[0]
    blocks = positions // BLOCK_LEN
    width = 2 * HEAD_DIM

    @pl.when(step_at == 0)
    def _():
        masked_scores(maps_ref, scores_ref, blocks)
        ends_ref[...] = jnp.zeros_like(ends_ref)
        dscores_ref[...] = jnp.zeros_like(dscores_ref)
        gacc_ref[...] = jnp.zeros_like(gacc_ref)
        dpad_ref[0:8, :] = jnp.zeros((8, GCOLS), F32)
        dpad_ref[positions + 8 : positions + 16, :] = jnp.zeros((8, GCOLS), F32)

    ahead = PIECE // GCOLS
    slot = (OUT_PIECES + 2 * (step_at // ahead)) % XRING
    offset = (step_at % ahead) * GCOLS
    group_span = pl.ds(pl.multiple_of(step_at * GCOLS, GCOLS), GCOLS)
    grad = got[step_at].astype(F32)
    for block in reversed(range(blocks)):
        if block < blocks - 1:
            grad = by_head(decays, step_at, block + 1) * grad + grads_ref[block + 1, group_span, :]
        dl_ref[block] = grad.astype(BF16)
        product = grad * st_ref[block].astype(F32)
        for head in range(GROUP):
            at = block * GROUP + head
            cross_ref[step_at, at : at + 1, :] = jnp.sum(
                product[head * HEAD_DIM : (head + 1) * HEAD_DIM], axis=0, keepdims=True
            )

    half = first_half((BLOCK_LEN, width))
    lane_row = lax.broadcasted_iota(jnp.int32, (width, 128), 0)
    lane_col = lax.broadcasted_iota(jnp.int32, (width, 128), 1)
    gw = [[jnp.zeros((8, width), F32) for _ in range(CONV + 2)] for _ in range(PAIRS)]
    for block in range(blocks):
        lo = block * BLOCK_LEN
        rows = slice(lo, lo + BLOCK_LEN)
        outer_ref[...] = dot(maps_ref[rows, :STATE], dl_ref[block], NT)
        for pair in range(PAIRS):
            lanes = pl.ds(pair * width, width)
            for top in range(0, BLOCK_LEN, PART):
                part = slice(lo + top, lo + top + PART)
                here = slice(top, top + PART)
                conv = convolved(p_ref, w_ref, b_ref, lo + top, PART, lanes)
                conv_ref[here, :] = conv
                xs = conv * sigmoid(conv) * per_pair(cols_ref, 0, pair, part)
                low_ref[here, :] = xs.astype(BF16)
                ended_ref[here, lanes] = (xs * per_pair(cols_ref, 3, pair, part)).astype(BF16)
            dyl = dy_ref[rows, lanes]
            none = jnp.zeros_like(dyl)
            sides = (jnp.where(half, dyl, none), jnp.where(half, none, dyl))
            turned = dyl.astype(F32).T.astype(BF16)
            dxt = [None, None]
            for strip in range(BLOCK_LEN // STRIP):
                top = strip * STRIP
                lim = top + STRIP
                scores = scores_ref[block, top:lim, :lim]
                gathered = jnp.zeros((STRIP, lim), F32)
                for side in range(2):
                    head = 2 * pair + side
                    at = GROUP + head
                    gap = (
                        cols_ref[lo + top : lo + lim, at : at + 1]
                        - rows_ref[head : head + 1, lo : lo + lim]
                    )
                    decay = jnp.exp2(jnp.minimum(gap, 0.0))
                    gathered = gathered + dot(sides[side][top:lim], low_ref[:lim, :], NT) * decay
                    part = dot(
                        turned[side * HEAD_DIM : (side + 1) * HEAD_DIM, top:lim],
                        (scores * decay).astype(BF16),
                    )
                    if strip == 0:
                        dxt[side] = jnp.concatenate(
                            [part, jnp.zeros((HEAD_DIM, BLOCK_LEN - STRIP), F32)], axis=1
                        )
                    else:
                        dxt[side] = dxt[side] + part
                dscores_ref[block, top:lim, :lim] += gathered
            inner_ref[...] = jnp.concatenate(dxt, axis=0).T
            skip = skip_ref[0:1, lanes]
            at = step_at * GROUP + 2 * pair
            heads_of = jnp.where(lane_col == at + lane_row // HEAD_DIM, 1.0, 0.0).astype(BF16)
            ends = jnp.zeros((8, width), F32)

            def folded(values):
                return jnp.sum(values.reshape(PART // 8, 8, width), axis=0)

            for top in range(0, BLOCK_LEN, PART):
                part = slice(lo + top, lo + top + PART)
                here = slice(top, top + PART)
                conv = conv_ref[here, :]
                sig = sigmoid(conv)
                x = conv * sig
                step = per_pair(cols_ref, 0, pair, part)
                inner = inner_ref[here, :]
                outer = outer_ref[here, lanes] * per_pair(cols_ref, 3, pair, part)
                dyf = dy_ref[part, lanes].astype(F32)
                dxs = inner + outer
                vs = x * step * outer
                ends = ends + folded(vs)
                runs = dyf * (y_ref[part, lanes] - skip * x) - low_ref[here, :].astype(F32) * inner - vs
                for sums_ref, values in ((runs_ref, runs), (direct_ref, x * dxs)):
                    high = values.astype(BF16)
                    rest = (values - high.astype(F32)).astype(BF16)
                    sums_ref[part, :] += dot(high, heads_of) + dot(rest, heads_of)
                gw[pair][CONV + 1] = gw[pair][CONV + 1] + folded(dyf * x)
                dconv = (dxs * step + skip * dyf) * (sig * (1.0 + conv * (1.0 - sig)))
                gw[pair][CONV] = gw[pair][CONV] + folded(dconv)
                dpad_ref[8 + lo + top : 8 + lo + top + PART, lanes] = dconv
                for tap in range(CONV):
                    first = EDGE - CONV + 1 + tap + lo + top
                    gw[pair][tap] = gw[pair][tap] + folded(dconv * p_ref[first : first + PART, lanes])
            group_lanes = pl.ds(pl.multiple_of(step_at * GCOLS + pair * width, width), width)
            ends_ref[block : block + 1, group_lanes] = jnp.sum(ends, axis=0, keepdims=True)
        gacc_ref[rows, :STATE] += dot(ended_ref[...], dl_ref[block])
        gacc_ref[rows, STATE:] += dot(dye_ref[rows, :], st_ref[block])

    for pair in range(PAIRS):
        lanes = pl.ds(pair * width, width)
        group_lanes = pl.ds(pl.multiple_of(step_at * GCOLS + pair * width, width), width)
        for index in range(CONV + 1):
            t_sent[0, index : index + 1, group_lanes] = jnp.sum(gw[pair][index], axis=0, keepdims=True)
        ends_ref[blocks : blocks + 1, group_lanes] = jnp.sum(gw[pair][CONV + 1], axis=0, keepdims=True)
        edge = jnp.zeros((8, width), F32)
        for tap in range(CONV):
            edge = edge + dpad_ref[CONV - 1 - tap : CONV - 1 - tap + 8, lanes] * w_ref[tap : tap + 1, lanes]
        edge_ref[step_at, :, lanes] = edge
        for top in range(0, positions, PART):
            back = jnp.zeros((PART, width), F32)
            for tap in range(CONV):
                at = 8 + CONV - 1 - tap + top
                back = back + dpad_ref[at : at + PART, lanes] * w_ref[tap : tap + 1, lanes]
            x_ref[slot, top : top + PART, pl.ds(pl.multiple_of(offset + pair * width, width), width)] = (
                back.astype(BF16)
            )
        tail_ref[step_at, :, lanes] = back[PART - 8 :]

    @pl.when(step_at == GROUPS - 1)
    def _():
        row = lax.broadcasted_iota(jnp.int32, (BLOCK_LEN, BLOCK_LEN), 0)
        col = lax.broadcasted_iota(jnp.int32, (BLOCK_LEN, BLOCK_LEN), 1)
        for block in range(blocks):
            rows = slice(block * BLOCK_LEN, (block + 1) * BLOCK_LEN)
            low = jnp.where(row >= col, dscores_ref[block], 0.0).astype(BF16)
            gacc_ref[rows, :STATE] += dot(low, maps_ref[rows, STATE:], TN)
            gacc_ref[rows, STATE:] += dot(low, maps_ref[rows, :STATE])


def scan_backward(
    decays, p, w, b, cols, rows, maps, skip, y, dy, dye, starts, ends, turned, turned_out, cot, grad_gate,
    inw_gate, inw_conv, bias, decay_log, tokens, gain, own_rows, collective_id, *factors,
):
    branch = len(factors) == 2
    positions = y.shape[0]
    features = inw_gate.shape[0]
    blocks = positions // BLOCK_LEN
    ext = p.shape[0]
    zs, n = lax.axis_size("seq"), lax.axis_size("fsdp")
    gates = INNER // PIECE
    pieces = OUT_PIECES + 2 * gates + 1
    count = exchange_count(zs, n)
    steps = pieces + max(LAG * (stages_of(n) - 1), count - LAG, gates - EARLY + positions // 256)
    width = CHANNELS + 128
    dma = pltpu.SemaphoreType.DMA

    def late(s):
        return jnp.clip(s - max(zs - 1, LAG + 1), 0, GROUPS - 1)

    def turn(s, most):
        return jnp.clip((s - OUT_PIECES) // 2, 0, most)

    def weight_turn(s):
        return jnp.minimum(s, EARLY - 1) + jnp.clip(s - pieces + 1, 0, gates - EARLY)

    def gate_turn(s):
        within = jnp.minimum(jnp.maximum(s - EARLY + 1, 0), 1) * (1 - jnp.minimum(jnp.maximum(s - pieces + 1, 0), 1))
        return within * turn(s - 1, gates - 1) + (1 - within) * weight_turn(s)

    once = pl.Buffered(1)
    own = pl.BlockSpec((positions, GCOLS), lambda s: (0, late(s)))
    eight = pl.BlockSpec((8, GCOLS), lambda s: (0, late(s)))
    states = pl.BlockSpec((blocks, GCOLS, STATE), lambda s: (0, late(s), 0))

    def whole(x):
        return pl.BlockSpec(x.shape, lambda s: (0,) * len(x.shape), pipeline_mode=once)

    more_in, more_out, more_shapes = [], [], []
    if branch:
        steps = max(steps, GROUPS + LAG + features // MIXED_COLS)

        def mixing(s):
            return 0, jnp.minimum(spread_turn(s, 1), features // MIXED_COLS - 1)

        more_in = [whole(factors[0]), pl.BlockSpec((INNER, MIXED_COLS), mixing)]
        more_out = [pl.BlockSpec((positions, MIXED_COLS), mixing)]
        more_shapes = [jax.ShapeDtypeStruct((positions, features), BF16)]

    return pl.pallas_call(
        functools.partial(scan_backward_kernel, branch),
        grid=(steps,),
        in_specs=[
            pl.BlockSpec(memory_space=pltpu.SMEM),
            pl.BlockSpec((ext, GCOLS), lambda s: (0, late(s))),
            eight,
            pl.BlockSpec((1, GCOLS), lambda s: (0, late(s))),
            pl.BlockSpec((None, positions, 4 * GROUP), lambda s: (late(s), 0, 0)),
            pl.BlockSpec((None, GROUP, positions), lambda s: (late(s), 0, 0)),
            whole(maps),
            pl.BlockSpec((1, GCOLS), lambda s: (0, late(s))),
            own,
            own,
            own,
            states,
            whole(ends),
            whole(turned),
            whole(turned_out),
            whole(cot),
            pl.BlockSpec((positions, PIECE), lambda s: (0, gate_turn(s))),
            pl.BlockSpec((features, PIECE), lambda s: (0, weight_turn(s))),
            pl.BlockSpec((features, PIECE), lambda s: (0, turn(s, gates))),
            pl.BlockSpec((ext, PIECE), lambda s: (0, gates), pipeline_mode=once),
            pl.BlockSpec((8, PIECE), lambda s: (0, gates), pipeline_mode=once),
            pl.BlockSpec((1, PIECE), lambda s: (0, gates), pipeline_mode=once),
            whole(bias),
            whole(decay_log),
            whole(decays),
            whole(tokens),
            whole(gain),
        ]
        + more_in,
        out_specs=[
            pl.BlockSpec((own_rows, pieces * PIECE), lambda s: (0, 0), pipeline_mode=once),
            pl.BlockSpec((positions, features), lambda s: (0, 0), pipeline_mode=once),
            pl.BlockSpec((8, width), lambda s: (0, 0), pipeline_mode=once),
        ]
        + more_out,
        out_shape=[
            jax.ShapeDtypeStruct((own_rows, pieces * PIECE), F32),
            jax.ShapeDtypeStruct((positions, features), F32),
            jax.ShapeDtypeStruct((8, width), F32),
        ]
        + more_shapes,
        scratch_shapes=[
            pltpu.VMEM((blocks, BLOCK_LEN, BLOCK_LEN), F32),
            pltpu.VMEM((blocks, BLOCK_LEN, BLOCK_LEN), F32),
            pltpu.VMEM((positions + 16, GCOLS), F32),
            pltpu.VMEM((positions, 2 * STATE), F32),
            pltpu.VMEM((blocks, GCOLS, STATE), BF16),
            pltpu.VMEM((XRING, positions, PIECE), BF16),
            pltpu.VMEM((GROUPS + 1, 8, GCOLS), F32),
            pltpu.VMEM((positions, 128), F32),
            pltpu.VMEM((positions, 128), F32),
            pltpu.VMEM((8, INNER), F32),
            pltpu.VMEM((GROUPS, blocks * GROUP, STATE), F32),
            pltpu.VMEM((BLOCK_LEN, 2 * HEAD_DIM), F32),
            pltpu.VMEM((BLOCK_LEN, 2 * HEAD_DIM), F32),
            pltpu.VMEM((BLOCK_LEN, GCOLS), F32),
            pltpu.VMEM((BLOCK_LEN, 2 * HEAD_DIM), BF16),
            pltpu.VMEM((BLOCK_LEN, GCOLS), BF16),
        ]
        + chain_scratch()
        + [
            pltpu.VMEM((GROUPS + 1, 8, GCOLS), F32),
            pltpu.VMEM((GROUPS + 1, 8, GCOLS), F32),
            dma((GROUPS + 1,)),
            dma((GROUPS + 1,)),
            pltpu.VMEM((2, 8, width), F32),
            pltpu.VMEM((count, 8, width), F32),
            dma((count,)),
            dma((count,)),
        ]
        + Streamed.scratch(own_rows),
        compiler_params=pltpu.CompilerParams(
            collective_id=collective_id, has_side_effects=True, vmem_limit_bytes=63 * 2**20
        ),
        cost_estimate=pl.CostEstimate(
            flops=24 * positions * INNER * BLOCK_LEN, bytes_accessed=30 * positions * INNER,
            transcendentals=HEADS * positions * BLOCK_LEN,
        ),
        name="scan_backward",
    )(
        decays, p, w, b, cols, rows, maps, skip, y, dy, dye, starts, ends, turned, turned_out, cot, grad_gate,
        inw_gate, inw_conv, p, w, b, bias, decay_log, decays, tokens, gain, *factors,
    )


PIECE = 512
LAG = 2
HALF = PIECE // 2
MESH = pl.DeviceIdType.MESH


class Site:
    def __init__(self):
        self.zs, self.n = lax.axis_size("seq"), lax.axis_size("fsdp")
        self.z, self.f = lax.axis_index("seq"), lax.axis_index("fsdp")
        self.chips = self.n // 2
        self.bits = self.chips.bit_length() - 1

    def bit(self, j):
        return (self.f // 2**j) % 2

    def flip(self, js):
        f = self.f
        for j in js:
            f = f + (1 - 2 * self.bit(j)) * 2**j
        return f

    def over(self, dz):
        return (self.z + dz) % self.zs

    def greet(self):
        barrier = pltpu.get_barrier_semaphore()
        for dz in range(1, self.zs):
            pl.semaphore_signal(barrier, inc=1, device_id=(self.over(dz), self.f), device_id_type=MESH)
        for j in range(self.bits + 1):
            pl.semaphore_signal(barrier, inc=1, device_id=(self.z, self.flip([j])), device_id_type=MESH)
        pl.semaphore_wait(barrier, self.zs + self.bits)


def subsets(js):
    found = [()]
    for j in js:
        found = found + [s + (j,) for s in found]
    return found


class Gather:
    def __init__(self, site, own, whole, local_sem, send_sem, recv_sem):
        self.site, self.own, self.whole = site, own, whole
        self.local_sem, self.send_sem, self.recv_sem = local_sem, send_sem, recv_sem
        self.along = len(own.shape) == 2
        self.skipped = 0 if self.along else 1
        self.stages = site.bits + 3 - self.skipped

    @staticmethod
    def slots(zs, n):
        return zs + 4 * (n // 2 - 1)

    def moves(self, piece):
        s = self.site
        start = piece * PIECE
        whole = pl.ds(pl.multiple_of(start, 128), PIECE)
        halves = (
            pl.ds(pl.multiple_of(start, 128), HALF),
            pl.ds(pl.multiple_of(start + HALF, 128), HALF),
        )
        slot = 0
        plan = [[] for _ in range(s.bits + 3)]
        for dz in range(1, s.zs):
            if not self.along:
                slot += 1
                continue
            plan[0].append(
                (slot, self.own.at[:, whole], self.whole.at[s.z, s.f, :, whole],
                 (s.over(dz), s.f), self.whole.at[s.over(s.zs - dz), s.f, :, whole])
            )
            slot += 1
        sibling = s.flip([0])

        def known(js, cols):
            if not js and not self.along:
                return self.own.at[:, :, cols]
            return self.whole.at[:, s.flip(js), :, cols]

        def shared(js, cols):
            return (slot, known(js, cols), self.whole.at[:, s.flip(js), :, cols],
                    (s.z, sibling), self.whole.at[:, s.flip(list(js) + [0]), :, cols])

        plan[1].append(shared([], whole))
        slot += 1
        up = list(range(1, s.bits + 1))
        for half, order in enumerate((up, up[::-1])):
            cols = halves[half]
            for at, j in enumerate(order):
                for js in subsets(order[:at]):
                    js = list(js)
                    plan[at + 1].append(
                        (slot, known(js, cols), self.whole.at[:, s.flip(js), :, cols],
                         (s.z, s.flip([j])), self.whole.at[:, s.flip(js + [j]), :, cols])
                    )
                    slot += 1
                    plan[at + 2].append(shared(js + [j], cols))
                    slot += 1
        return plan[self.skipped :]

    def leaving(self, piece, moves):
        return [
            pltpu.make_async_remote_copy(
                src_ref=src, dst_ref=dst, send_sem=self.send_sem.at[piece, slot],
                recv_sem=self.recv_sem.at[piece, slot], device_id=device, device_id_type=MESH,
            )
            for slot, src, dst, device, _ in moves
        ]

    def arriving(self, piece, moves):
        return [
            pltpu.make_async_remote_copy(
                src_ref=src, dst_ref=incoming, send_sem=self.send_sem.at[piece, slot],
                recv_sem=self.recv_sem.at[piece, slot], device_id=device, device_id_type=MESH,
            )
            for slot, src, _, device, incoming in moves
        ]

    def run(self, stage, piece):
        s = self.site
        plan = self.moves(piece)
        cols = pl.ds(pl.multiple_of(piece * PIECE, 128), PIECE)

        def local():
            if self.along:
                src, dst = self.own.at[:, cols], self.whole.at[s.z, s.f, :, cols]
            else:
                src, dst = self.own.at[:, :, cols], self.whole.at[:, s.f, :, cols]
            return pltpu.make_async_copy(src, dst, self.local_sem.at[piece])

        to_core = [[m for m in moves if self.is_core(stage_at, m)] for stage_at, moves in enumerate(plan)]
        others = [[m for m in moves if not self.is_core(stage_at, m)] for stage_at, moves in enumerate(plan)]
        if stage == 0:
            local().start()
        if stage == 1:
            local().wait()
        if 0 < stage:
            for copy in self.arriving(piece, others[stage - 1]):
                copy.wait_recv()
        if stage < self.stages - 1:
            for copy in self.leaving(piece, others[stage] + to_core[stage]):
                copy.start()
        else:
            for moves in to_core:
                for copy in self.arriving(piece, moves):
                    copy.wait_recv()
            for moves in plan:
                for copy in self.leaving(piece, moves):
                    copy.wait_send()

    def is_core(self, stage, move):
        slot = move[0]
        zs = self.site.zs
        if slot < zs - 1:
            return False
        return (slot - (zs - 1)) % 2 == 0


def at_stages(stages, pieces, lag, step, run):
    for stage in reversed(range(stages)):
        piece = step - lag * stage

        @pl.when(jnp.logical_and(piece >= 0, piece < pieces))
        def _(stage=stage, piece=piece):
            run(stage, piece)


def stages_of(n):
    return (n // 2).bit_length() + 2


def along_line(step, start, site, own, line, local_sem, send_sem, recv_sem):
    local = functools.partial(pltpu.make_async_copy, own, line.at[site.z], local_sem)

    def passing(hop, way):
        z = site.z - way * hop
        return pltpu.make_async_remote_copy(
            src_ref=own if hop == 0 else line.at[z], dst_ref=line.at[z],
            send_sem=send_sem.at[hop, (1 - way) // 2], recv_sem=recv_sem.at[hop, (1 - way) // 2],
            device_id=(site.z + way, site.f), device_id_type=MESH,
        )

    def arriving(hop, way):
        z = site.z - way * (hop + 1)
        return pltpu.make_async_remote_copy(
            src_ref=own, dst_ref=line.at[z],
            send_sem=send_sem.at[hop, (1 - way) // 2], recv_sem=recv_sem.at[hop, (1 - way) // 2],
            device_id=(site.z - way, site.f), device_id_type=MESH,
        )

    def inside(z):
        return jnp.logical_and(z >= 0, z < site.zs)

    for hop in range(site.zs):

        @pl.when(step == start + LAG * hop)
        def _(hop=hop):
            if hop == 0:
                local().start()
            else:
                for way in (1, -1):

                    @pl.when(inside(site.z - way * hop))
                    def _(way=way):
                        arriving(hop - 1, way).wait_recv()

            if hop < site.zs - 1:
                for way in (1, -1):

                    @pl.when(jnp.logical_and(inside(site.z - way * hop), inside(site.z + way)))
                    def _(way=way):
                        passing(hop, way).start()

            else:
                local().wait()
                for early in range(site.zs - 1):
                    for way in (1, -1):

                        @pl.when(jnp.logical_and(inside(site.z - way * early), inside(site.z + way)))
                        def _(way=way, early=early):
                            passing(early, way).wait_send()


def gather_kernel(pieces, start, own, late, last, whole, line, before, *refs):
    step = pl.program_id(0)
    site = Site()

    @pl.when(step == 0)
    def _():
        site.greet()

    edge_send, edge_recv = refs[3:5]

    def edge():
        return pltpu.make_async_remote_copy(
            src_ref=last, dst_ref=before, send_sem=edge_send, recv_sem=edge_recv,
            device_id=(site.over(1), site.f), device_id_type=MESH,
        )

    @pl.when(step == 0)
    def _():
        edge().start()

    gather = Gather(site, own, whole, *refs[:3])
    at_stages(gather.stages, pieces, LAG, step, gather.run)
    along_line(step, start, site, late, line, *refs[5:])

    @pl.when(step == pl.num_programs(0) - 1)
    def _():
        edge().wait()


def gather_scratch(pieces):
    slots = Gather.slots(lax.axis_size("seq"), lax.axis_size("fsdp"))
    return [
        pltpu.SemaphoreType.DMA((pieces,)),
        pltpu.SemaphoreType.DMA((pieces, slots)),
        pltpu.SemaphoreType.DMA((pieces, slots)),
    ]


def gathered(own, late, last, collective_id):
    rows, columns = own.shape
    zs, n = lax.axis_size("seq"), lax.axis_size("fsdp")
    pieces = columns // PIECE
    steps = max(pieces + LAG * (stages_of(n) - 1), LAG * zs)
    start = min(pieces // 2, steps - LAG * (zs - 1) - 1)
    anywhere = pl.BlockSpec(memory_space=pl.ANY)
    dma = pltpu.SemaphoreType.DMA
    return pl.pallas_call(
        functools.partial(gather_kernel, pieces, start),
        grid=(steps,),
        in_specs=[anywhere] * 3,
        out_specs=[anywhere] * 3,
        out_shape=[
            jax.ShapeDtypeStruct((zs, n, rows, columns), own.dtype),
            jax.ShapeDtypeStruct((zs,) + late.shape, late.dtype),
            jax.ShapeDtypeStruct(last.shape, last.dtype),
        ],
        scratch_shapes=gather_scratch(pieces) + [dma, dma, dma, dma((zs - 1, 2)), dma((zs - 1, 2))],
        compiler_params=pltpu.CompilerParams(collective_id=collective_id, has_side_effects=True),
        cost_estimate=pl.CostEstimate(
            flops=0, bytes_accessed=2 * zs * n * rows * columns, transcendentals=0
        ),
        name="gather_rows",
    )(own, late, last)


class Scatter:
    def take(self, refs):
        bits = self.site.bits
        self.kept = refs[:bits]
        self.sent = refs[bits : 2 * bits]
        self.got = refs[2 * bits : 3 * bits]
        self.z_kept, self.z_sent, self.z_got, self.send_sem, self.recv_sem = refs[3 * bits :]
        self.stages = bits + 3

    @staticmethod
    def common(pieces, rows):
        zs, n = lax.axis_size("seq"), lax.axis_size("fsdp")
        chips = n // 2
        bits = chips.bit_length() - 1
        slots = 1 + 2 * bits + zs - 1
        steps = [(pieces, 2, zs, chips >> (k + 1), rows, HALF) for k in range(bits)]
        return (
            [pltpu.VMEM(s, F32) for s in steps]
            + [pltpu.VMEM(s, BF16) for s in steps]
            + [pltpu.VMEM(s, BF16) for s in steps]
            + [
                pltpu.VMEM((pieces, rows, PIECE), F32),
                pltpu.VMEM((pieces, zs, rows, PIECE), BF16),
                pltpu.VMEM((pieces, zs - 1, rows, PIECE), BF16),
                pltpu.SemaphoreType.DMA((pieces, slots)),
                pltpu.SemaphoreType.DMA((pieces, slots)),
            ]
        )

    def remote(self, piece, slot, src, dst, device):
        at = self.at(piece)
        return pltpu.make_async_remote_copy(
            src_ref=src, dst_ref=dst, send_sem=self.send_sem.at[at, slot],
            recv_sem=self.recv_sem.at[at, slot], device_id=device, device_id_type=MESH,
        )

    def order(self, half):
        up = list(range(1, self.site.bits + 1))
        return up[::-1] if half == 0 else up

    def across(self, piece, k, half):
        s, at = self.site, self.at(piece)
        return self.remote(
            piece, 1 + 2 * k + half, self.sent[k].at[at, half], self.got[k].at[at, half],
            (s.z, s.flip([self.order(half)[k]])),
        )

    def along(self, piece, dz):
        s, at = self.site, self.at(piece)
        return self.remote(
            piece, 2 * s.bits + dz, self.z_sent.at[at, s.over(dz)], self.z_got.at[at, dz - 1],
            (s.over(dz), s.f),
        )

    def run(self, stage, piece):
        s, at = self.site, self.at(piece)
        bits = s.bits
        if stage == 0:
            self.begin(piece)
            self.to_core(piece).start()
            return
        if stage == 1:
            self.join(piece)
            self.to_core(piece).wait()
        elif stage <= bits + 1:
            for half in range(2):
                self.across(piece, stage - 2, half).wait()
        if stage <= bits:
            k = stage - 1
            for half in range(2):
                order = self.order(half)
                left = sorted(order[k:])
                j = order[k]
                place = left.index(j)
                mine = s.bit(j)

                def one(zi, carry, half=half, k=k, place=place, mine=mine):
                    for i in range(s.chips >> (k + 1)):
                        low = i % 2**place
                        base = (i - low) * 2 + low
                        self.sent[k][at, half, zi, i] = self.current(
                            k, piece, half, zi, base + (1 - mine) * 2**place
                        ).astype(BF16)
                        self.kept[k][at, half, zi, i] = self.current(
                            k, piece, half, zi, base + mine * 2**place
                        )
                    return carry

                lax.fori_loop(0, s.zs, one, 0)
                self.across(piece, k, half).start()
        elif stage == bits + 1:
            for half in range(2):
                lanes = slice(half * HALF, (half + 1) * HALF)

                def one(zi, carry, half=half, lanes=lanes):
                    self.z_sent[at, zi, :, lanes] = self.current(bits, piece, half, zi, 0).astype(BF16)
                    return carry

                lax.fori_loop(0, s.zs, one, 0)
                self.z_kept[at, :, lanes] = self.current(bits, piece, half, s.z, 0)
            for dz in range(1, s.zs):
                self.along(piece, dz).start()
        else:
            total = self.z_kept[at]
            for dz in range(1, s.zs):
                self.along(piece, dz).wait()
                total = total + self.z_got[at, dz - 1].astype(F32)
            self.out[:, pl.ds(pl.multiple_of(self.column(piece) * PIECE, 128), PIECE)] = total

    def current(self, k, piece, half, zi, index):
        at = self.at(piece)
        lanes = slice(half * HALF, (half + 1) * HALF)
        if k == 0:
            return self.first(piece, zi, index, lanes) + self.came[at, zi, index, :, lanes].astype(F32)
        return self.kept[k - 1][at, half, zi, index] + self.got[k - 1][at, half, zi, index].astype(F32)


RING = 4
XRING = 6
OUT_PIECES = 6
OUT_SPLIT = 2


class Streamed(Scatter):
    def __init__(self, site, turned, turned_out, is_later, x, out, column, refs):
        self.site, self.x, self.out = site, x, out
        self.turned, self.turned_out, self.is_later, self.column = turned, turned_out, is_later, column
        self.ring, self.x_ring = refs[0].shape[0], x.shape[0]
        self.away, self.own, self.came = refs[:3]
        self.take(refs[3:])

    @staticmethod
    def scratch(rows, ring=RING):
        zs, n = lax.axis_size("seq"), lax.axis_size("fsdp")
        full = (zs, n // 2, rows, PIECE)
        return [
            pltpu.VMEM((ring,) + full, BF16),
            pltpu.VMEM(full, BF16),
            pltpu.VMEM((ring,) + full, BF16),
        ] + Scatter.common(ring, rows)

    def at(self, piece):
        return piece % self.ring

    def to_core(self, piece):
        s, at = self.site, self.at(piece)
        return self.remote(piece, 0, self.away.at[at], self.came.at[at], (s.z, s.flip([0])))

    def product(self, core, piece, store):
        s = self.site
        rows = self.away.shape[3]
        share = OUT_PIECES // OUT_SPLIT
        for later in range(2):

            @pl.when(self.is_later(piece) == later)
            def _(later=later):
                if later:
                    lhs = self.turned[core]
                else:
                    lhs = self.turned_out[jnp.minimum(piece, OUT_PIECES - 1) // share, core]
                value = dot(lhs, self.x[piece % self.x_ring])
                store(value.astype(BF16).reshape(s.zs, s.chips, rows, PIECE))

    def begin(self, piece):
        at = self.at(piece)

        def store(value):
            self.away[at] = value

        self.product(1 - self.site.bit(0), piece, store)

    def join(self, piece):
        def store(value):
            self.own[...] = value

        self.product(self.site.bit(0), piece, store)

    def first(self, piece, zi, index, lanes):
        return self.own[zi, index, :, lanes].astype(F32)


def exchange_count(zs, n):
    return (n.bit_length() - 1) + (zs.bit_length() - 1)


class Totals:
    def __init__(self, site, sent, got, send_sem, recv_sem):
        self.site, self.sent, self.got = site, sent, got
        self.send_sem, self.recv_sem = send_sem, recv_sem
        self.count = exchange_count(site.zs, site.n)

    def move(self, t):
        s = self.site
        if t <= s.bits:
            device = (s.z, s.flip([t]))
        else:
            j = t - s.bits - 1
            device = (s.z + (1 - 2 * ((s.z // 2**j) % 2)) * 2**j, s.f)
        return pltpu.make_async_remote_copy(
            src_ref=self.sent.at[t % 2], dst_ref=self.got.at[t], send_sem=self.send_sem.at[t],
            recv_sem=self.recv_sem.at[t], device_id=device, device_id_type=MESH,
        )

    def start(self, t):
        if t < self.count:
            self.move(t).start()

    def next(self, t):
        if t < self.count:
            self.move(t).wait()
            self.sent[(t + 1) % 2] = self.sent[t % 2] + self.got[t]
            self.start(t + 1)


CONV_COLS = 3584


def local(
    tokens, pre_gain, in_weight, conv_weight, conv_bias, step_bias, decay_log, skip_gain,
    norm_gain, out_weight, cotangent,
):
    both = ("seq", "fsdp")
    _, positions, features = tokens.shape
    blocks = positions // BLOCK_LEN
    devices = lax.axis_size("seq") * lax.axis_size("fsdp")

    rows = in_weight.shape[0]
    padded_rows = -(-rows // 16) * 16
    vectors = jnp.concatenate([pre_gain, conv_weight.reshape(-1), conv_bias, norm_gain])
    extra = -(-vectors.size // rows)
    sizes = (pre_gain.size, conv_weight.size, conv_bias.size, norm_gain.size)
    cuts = [sum(sizes[:i]) for i in range(5)]
    used = PROJ - INNER
    more_rows = ((0, padded_rows - rows), (0, 0))
    own = jnp.concatenate(
        [
            in_weight[:, INNER:],
            jnp.pad(vectors, (0, extra * rows - vectors.size)).reshape(rows, extra),
            jnp.zeros((rows, CONV_COLS - used - extra), BF16),
        ],
        axis=1,
    )
    inw_conv, gate_line, before = gathered(
        jnp.pad(own, more_rows),
        jnp.pad(in_weight[:, :INNER], more_rows),
        tokens[0, positions - EDGE :],
        1,
    )
    later, before = lax.optimization_barrier((out_weight, before))
    outw_full = lax.all_gather(later, both, axis=0, tiled=True)
    inw_conv = inw_conv[:, :, :rows].reshape(features, CONV_COLS)
    small_full = inw_conv[:, used : used + extra].reshape(devices, rows * extra)
    gain_full = small_full[:, : cuts[1]].reshape(1, features).astype(F32)
    convw_full = (
        small_full[:, cuts[1] : cuts[2]]
        .reshape(devices, CONV, -1)
        .transpose(1, 0, 2)
        .reshape(CONV, CHANNELS)
        .astype(F32)
    )
    convb_full = small_full[:, cuts[2] : cuts[3]].reshape(1, CHANNELS).astype(F32)
    normg_full = small_full[:, cuts[3] : cuts[4]].reshape(1, INNER).astype(F32)

    before = jnp.where(lax.axis_index("seq") == 0, jnp.zeros_like(before), before)
    ext = jnp.concatenate([before, tokens[0]], axis=0).astype(F32)
    r0_ext = lax.rsqrt(jnp.mean(ext * ext, axis=-1, keepdims=True) + 1e-05)
    normed_ext = (ext * r0_ext * gain_full).astype(BF16)
    inputs, r0, normed = ext[EDGE:], r0_ext[EDGE:], normed_ext[EDGE:]

    p = dot(normed_ext, inw_conv)
    unused = ((0, 0), (0, CONV_COLS - CHANNELS))
    w = jnp.pad(convw_full, ((0, 8 - CONV), (0, CONV_COLS - CHANNELS)))
    b = jnp.pad(convb_full, unused)
    wide_heads = ((0, 0), (0, 128 - HEADS))
    bias, decay_row = jnp.pad(step_bias[None], wide_heads), jnp.pad(decay_log[None], wide_heads)
    cols, run_rows, maps, run_exp, decays = steps_of(
        p, w, b, bias, decay_row, positions
    )
    skip = jnp.repeat(skip_gain, HEAD_DIM)[None]
    by_rows = jnp.pad(normed.reshape(positions, devices, rows), ((0, 0), (0, 0), more_rows[0]))
    y, starts, gate, turned_in, inw_gate = scan_forward(
        decays, p, w, b, cols, run_rows, maps, skip, by_rows.reshape(positions, -1), gate_line, positions, 2
    )
    inw_gate = inw_gate[:, :, :rows].reshape(features, INNER)
    cot = cotangent[0]
    grad_normed_out = dot(cot, outw_full, NT)
    normed_out, dy, dye, grad_gate, ends, *turned_out = gated(
        y, gate, grad_normed_out, normg_full, run_exp, maps, rows if rows == padded_rows else None
    )

    if turned_out:
        turned_out = turned_out[0]
    else:
        turned_out = normed_out.T.reshape(-1, 2, OUT_SPLIT, rows, positions)
        turned_out = jnp.pad(turned_out, ((0, 0),) * 3 + more_rows).transpose(2, 1, 0, 3, 4)
    turned_out = turned_out.reshape(OUT_SPLIT, 2, -1, positions)
    in_kernel = rows == padded_rows
    own_main, grad_tokens, totals, *mixed = scan_backward(
        decays, p, w, b, cols, run_rows, maps, skip, y, dy, dye, starts, ends, turned_in, turned_out, cot, grad_gate,
        inw_gate, inw_conv, bias, decay_row, tokens[0], gain_full, padded_rows, 3,
        *((normed_out, outw_full) if in_kernel else ()),
    )
    if in_kernel:
        mixed = mixed[0]
    else:
        mixed = (inputs + dot(normed_out, outw_full)).astype(BF16)
    own_main = own_main[:rows]
    out_cols = OUT_PIECES * PIECE
    share = out_cols // OUT_SPLIT
    own_out = jnp.concatenate([own_main[:, i * share : (i + 1) * share] for i in range(OUT_SPLIT)])
    own_in = own_main[:, out_cols : out_cols + PROJ]
    per_tap = conv_weight.shape[1]
    me = lax.axis_index("seq") * lax.axis_size("fsdp") + lax.axis_index("fsdp")
    own_taps = lax.dynamic_slice_in_dim(totals, me * per_tap, per_tap, axis=1)
    heads = totals[:3, CHANNELS : CHANNELS + HEADS]

    return (
        mixed[None],
        grad_tokens[None],
        jnp.sum(own_in * in_weight.astype(F32), axis=1) / pre_gain.astype(F32),
        own_in,
        own_taps[:CONV],
        own_taps[CONV],
        heads[0],
        heads[1],
        heads[2],
        jnp.sum(own_out * out_weight.astype(F32), axis=1) / norm_gain.astype(F32),
        own_out,
    )


def solution(mesh):
    split = P(("seq", "fsdp"), None)
    flat = P(("seq", "fsdp"))
    taps = P(None, ("seq", "fsdp"))
    data = P("fsdp", "seq", None)
    return jax.shard_map(
        local,
        mesh=mesh,
        in_specs=(data, flat, split, taps, flat, P(), P(), P(), flat, split, data),
        out_specs=(data, data, flat, split, taps, flat, P(), P(), P(), flat, split),
        check_vma=False,
    )
```
